32 devices in a mesh: dp: 16 (over z, x, core), mp: 2 (over y).
Axes of the slice: x: 2, y: 2, z: 4, core: 2. Of those that a mesh axis runs over, the one named last changes fastest.
Arguments:
- queries: bfloat16 [16384, 256], P('dp'), may hold values from -1400 to 1400, as said below
- item_table: bfloat16 [8192, 512], P('dp'), may hold values from -6 to 6
- cand_row: int32 [4096], P('dp'), may hold values from 0 to 511
- cand_owner: int32 [4096, 1], P('dp'), may hold values from 0 to 15; in each aligned block of 256 rows (0 to 255, 256 to 511, ...) at most 32 rows name the same one
- cand_count: int32 [4096], P('dp'), may hold values from 1 to 100
- positive: int32 [16384], P('dp'), may hold values from 0 to 4095
- w_in: bfloat16 [512, 1024], P(None, 'mp'), may hold values from -0.25 to 0.25
- b_in: float32 [1024], P('mp'), may hold values from -3 to 3
- w_out: bfloat16 [1024, 256], P('mp'), may hold values from -0.1875 to 0.1875
Outputs:
- loss: float32 [16384], P('dp')
- query_grad: float32 [16384, 256], P(('dp', 'mp'))
- grad_w_in: float32 [512, 1024], P(None, 'mp')
- grad_b_in: float32 [1024], P('mp')
- grad_w_out: float32 [1024, 256], P('mp')
- grad_table: float32 [8192, 512], P('dp')
The draws below stay inside these ranges and needn't reach their ends.
Inputs may be any that keep to these rules, and one draw needn't show every extreme that they name: `cand_owner`: no owner is named by more than 32 of the candidates of one index of dp; in some index of dp one owner is named by exactly 32. `queries`: query vectors are finite.
All inputs are finite; a program needn't handle non-finite values.
Results may differ from the reference program's by a relative error of at most 0.01.
Values may be sent and summed in bfloat16 or wider, within the bound.
No kernel may reach another device: no remote copies, remote signals or barrier semaphores. Data moves between devices by JAX's collectives and lax.ppermute only.
A program may use at most 64 MiB of HBM per device.

```python
import math
import jax
import jax.numpy as jnp
import numpy as np
from jax import lax

EMB = 512
HID = 1024
OUT = 256
ROWS_DEV = 512
NCAND = 4096
QUERIES = 16384
ROWS = 8192
CAND_DP = 256
CAP = 32
N_DP = 16


def draw_queries(key, part):
    first = jax.random.fold_in(key, 0)
    return jax.random.normal(first, (QUERIES, OUT), jnp.float32).astype(jnp.bfloat16)


def plant(result, key, low, top_value):
    shape = result.shape
    spot = [jax.random.randint(jax.random.fold_in(key, axis), (), 0, shape[axis]) for axis in range(len(shape))]
    result = result.at[tuple(spot)].set(low)
    longest = shape.index(max(shape))
    spot[longest] = (spot[longest] + 1) % shape[longest]
    return result.at[tuple(spot)].set(top_value)


def steps_of(own_key, shape, cuts, least, top_value):
    gain = 1.0
    for dim, parts in cuts:
        heights = jax.random.uniform(jax.random.fold_in(jax.random.fold_in(own_key, 6), dim), (parts,), jnp.float32, least / len(cuts), top_value / len(cuts))
        gain = gain * jnp.repeat(jnp.exp(heights), shape[dim] // parts).reshape((-1,) + (1,) * (len(shape) - 1 - dim))
    return gain


def shared_out(key, own, number, rows, number_of, top, limit, slope):
    sequence = jax.random.permutation(key, number_of)
    heavy_load, common = load_shares(number_of, rows * top, limit, slope, True), load_shares(number_of, rows * top, limit, slope, False)
    places = jnp.arange(number_of)

    def named(lengths, turn):
        used = int((lengths > 0).sum())
        fixed = max(1, used // 4)
        passed = fixed + (places - fixed + turn * (used - fixed)) % max(1, number_of - fixed)
        return jnp.zeros((number_of,), jnp.int32).at[sequence[jnp.where(places < fixed, places, passed)]].set(jnp.asarray(lengths, jnp.int32))

    lengths = jnp.where(number % 4 == 0, named(heavy_load, number // 4), named(common, number - number // 4 - 1))
    mixed = jax.random.permutation(jax.random.fold_in(own, 3), number_of)
    donor, sink = mixed[0:number_of // 2 * 2:2], mixed[1:number_of // 2 * 2:2]
    margin = jnp.minimum(lengths[donor] - 1, limit - lengths[sink]) // 2
    margin = jnp.where((donor == sequence[0]) | (sink == sequence[0]) | (lengths[sink] == 0), 0, jnp.maximum(margin, 0))
    passed = jax.random.randint(jax.random.fold_in(own, 4), (number_of // 2,), 0, 1 << 20) % (margin + 1)
    lengths = lengths.at[donor].add(-passed).at[sink].add(passed)
    labels = jnp.searchsorted(jnp.cumsum(lengths), jnp.arange(rows * top), side="right").astype(jnp.int32)
    listing = labels.reshape(top, rows).T
    listing = listing[jax.random.permutation(jax.random.fold_in(own, 1), rows)]
    turn = jax.random.randint(jax.random.fold_in(own, 2), (rows, 1), 0, top)
    return jnp.take_along_axis(listing, (jnp.arange(top)[None, :] + turn) % top, axis=1)


def load_shares(count, total, limit, lean, full):
    portions = [(1 << 20) // math.isqrt(standing ** lean) + 1 for standing in range(1, count + 1)]
    largest = limit if full else min(limit, max(-(-total // count), total * portions[0] // sum(portions)))
    least = 1 if total - largest >= count - 1 else 0
    counts, rest = [largest] + [least] * (count - 1), total - largest - least * (count - 1)
    while rest > 0:
        free = [i for i in range(1, count) if counts[i] < largest] or [i for i in range(1, count) if counts[i] < limit]
        pool, left = sum([portions[i] for i in free]), rest
        for i in free:
            more = min(limit - counts[i], max(1, left * portions[i] // pool), rest)
            counts[i] = counts[i] + more
            rest = rest - more
    return np.array(counts)


def centred(key, dims, spread, most, cuts=(), held_as=jnp.bfloat16):
    drawn = spread * jax.random.normal(key, dims, jnp.float32)
    if cuts:
        drawn = drawn * steps_of(key, dims, cuts, -0.22, 0.18)
    return jnp.clip(drawn, -most, most).astype(held_as)


def setup_inputs(seed: int = 0) -> dict:
    streams_of = jax.random.split(jax.random.key(seed), 10)
    queries = draw_queries(jax.random.fold_in(streams_of[9], 71), 0)
    item_table = centred(streams_of[1], (ROWS, EMB), 1.0, 6.0, ((0, 16),))
    cand_row = plant(jax.random.randint(streams_of[2], (NCAND,), 0, ROWS_DEV), jax.random.fold_in(streams_of[2], 1), 0, ROWS_DEV - 1).astype(jnp.int32)
    cand_owner_keys = jax.random.split(jax.random.fold_in(streams_of[3], 1), NCAND // CAND_DP)
    cand_owner_turns = jax.random.permutation(jax.random.fold_in(streams_of[3], 3), NCAND // CAND_DP)
    cand_owner = jax.vmap(lambda own, number: shared_out(jax.random.fold_in(streams_of[3], 2), own, number, CAND_DP, N_DP, 1, CAP, 1))(cand_owner_keys, cand_owner_turns).reshape((NCAND, 1))
    cand_count = plant(jax.random.randint(streams_of[4], (NCAND,), 1, 101), jax.random.fold_in(streams_of[4], 1), 1, 100).astype(jnp.int32)
    positive = plant(jax.random.randint(streams_of[5], (QUERIES,), 0, NCAND), jax.random.fold_in(streams_of[5], 1), 0, NCAND - 1).astype(jnp.int32)
    w_in = centred(streams_of[6], (EMB, HID), EMB ** -0.5, 0.25, ((1, 2),))
    b_in = centred(streams_of[7], (HID,), 0.5, 3.0, ((0, 2),), jnp.float32)
    w_out = centred(streams_of[8], (HID, OUT), HID ** -0.5, 0.1875, ((0, 2),))
    return {"queries": queries, "item_table": item_table, "cand_row": cand_row, "cand_owner": cand_owner, "cand_count": cand_count, "positive": positive, "w_in": w_in, "b_in": b_in, "w_out": w_out}


def reference(queries, item_table, cand_row, cand_owner, cand_count, positive, w_in, b_in, w_out):
    ids = (cand_owner[:, 0] * ROWS_DEV + cand_row).astype(jnp.int32)
    emb = jnp.take(item_table, ids, axis=0)
    pre = jnp.dot(emb, w_in, preferred_element_type=jnp.float32) + b_in
    hidden = jnp.maximum(pre, 0.0).astype(jnp.bfloat16)
    items = jnp.dot(hidden, w_out, preferred_element_type=jnp.float32).astype(jnp.bfloat16)
    logq = jnp.log(cand_count.astype(jnp.float32))
    scale = 1.0 / math.sqrt(OUT)
    block = math.gcd(QUERIES, 4096)
    nblocks = QUERIES // block
    columns = jnp.arange(NCAND).astype(jnp.int32)

    def step(carry, pieces):
        qblock, pblock = pieces
        scores = jnp.dot(qblock, items.T, preferred_element_type=jnp.float32) * scale - logq[None, :]
        top = lax.optimization_barrier(jnp.max(scores, axis=1, keepdims=True))
        lse = top[:, 0] + jnp.log(lax.optimization_barrier(jnp.sum(jnp.exp(scores - top), axis=1)))
        onehot = pblock[:, None] == columns[None, :]
        pos = lax.optimization_barrier(jnp.sum(jnp.where(onehot, scores, 0.0), axis=1))
        probgrad = (jnp.exp(scores - lse[:, None]) - onehot.astype(jnp.float32)).astype(jnp.bfloat16)
        qgrad = jnp.dot(probgrad, items, preferred_element_type=jnp.float32) * scale
        carry = carry + jnp.dot(probgrad.T, qblock, preferred_element_type=jnp.float32) * scale
        return (carry, (lse - pos, qgrad))
    start = jnp.zeros((NCAND, OUT), jnp.float32)
    total, outs = lax.scan(step, start, (queries.reshape(nblocks, block, OUT), positive.reshape(nblocks, block)))
    loss = outs[0].reshape(QUERIES)
    query_grad = outs[1].reshape(QUERIES, OUT)
    item_grad = total.astype(jnp.bfloat16)
    grad_w_out = jnp.dot(hidden.T, item_grad, preferred_element_type=jnp.float32)
    back = jnp.dot(item_grad, w_out.T, preferred_element_type=jnp.float32)
    pre_grad = jnp.where(pre > 0.0, back, 0.0).astype(jnp.bfloat16)
    grad_w_in = jnp.dot(emb.T, pre_grad, preferred_element_type=jnp.float32)
    grad_b_in = lax.optimization_barrier(jnp.sum(pre_grad.astype(jnp.float32), axis=0))
    emb_grad = jnp.dot(pre_grad, w_in.T, preferred_element_type=jnp.float32).astype(jnp.bfloat16)
    grad_table = jnp.zeros((ROWS, EMB), jnp.float32).at[ids].add(emb_grad.astype(jnp.float32))
    return (loss, query_grad, grad_w_in, grad_b_in, grad_w_out, grad_table)
```

```python
import functools
import math

import jax
import jax.numpy as jnp
from jax import lax
from jax.experimental import pallas as pl
from jax.experimental.pallas import tpu as pltpu
from jax.sharding import PartitionSpec as P

F32 = jnp.float32
BF16 = jnp.bfloat16
ABSENT = -1e30
COUNT_BASE = 128
NT = (((1,), (1,)), ((), ()))
TN = (((0,), (0,)), ((), ()))


def hop(value, bits, axis="dp"):
    size = lax.axis_size(axis)
    return lax.ppermute(value, axis, [(i, i ^ bits) for i in range(size)])


def dot(a, b, dims=None, **kw):
    if dims is None:
        dims = (((1,), (0,)), ((), ()))
    return lax.dot_general(a, b, dims, preferred_element_type=F32, **kw)


def stats_kernel(scale, items_ref, qt_ref, bias_ref, m_in_ref, l_in_ref, m_ref, l_ref):
    @pl.when(pl.program_id(0) == 0)
    def _():
        m_ref[...] = m_in_ref[...]
        l_ref[...] = l_in_ref[...]

    scores = dot(items_ref[...], qt_ref[...]) * scale + bias_ref[...]
    cols, queries = scores.shape
    groups = scores.reshape(cols // 8, 8, queries)
    old = m_ref[...]
    new = jnp.maximum(old, jnp.max(groups, axis=0))
    l_ref[...] = l_ref[...] * jnp.exp(old - new) + jnp.sum(jnp.exp(groups - new[None]), axis=0)
    m_ref[...] = new


def run_stats(items, qt, bias, m, l, scale, block):
    cols, width = items.shape
    nq = qt.shape[1]
    whole = lambda shape: pl.BlockSpec(shape, lambda i: (0, 0))
    return pl.pallas_call(
        functools.partial(stats_kernel, scale),
        grid=(cols // block,),
        in_specs=[
            pl.BlockSpec((block, width), lambda i: (i, 0)),
            whole((width, nq)),
            pl.BlockSpec((block, 1), lambda i: (i, 0)),
            whole((8, nq)),
            whole((8, nq)),
        ],
        out_specs=[whole((8, nq)), whole((8, nq))],
        out_shape=[jax.ShapeDtypeStruct((8, nq), F32)] * 2,
        compiler_params=pltpu.CompilerParams(vmem_limit_bytes=24 << 20),
        cost_estimate=pl.CostEstimate(
            flops=2 * cols * width * nq, bytes_accessed=2 * cols * width, transcendentals=cols * nq
        ),
    )(items, qt, bias, m, l)


def grad_kernel(
    scale, base, items_ref, qt_ref, q_ref, bias_ref, lse_ref, pos_ref, qg_in_ref, sp_in_ref,
    ig_ref, qg_ref, sp_ref,
):
    step = pl.program_id(0)

    @pl.when(step == 0)
    def _():
        qg_ref[...] = qg_in_ref[...]
        sp_ref[...] = sp_in_ref[...]

    items = items_ref[...]
    scores = dot(items, qt_ref[...]) * scale
    cols, queries = scores.shape
    here = lax.broadcasted_iota(jnp.int32, scores.shape, 0) == pos_ref[...] - (base + step * cols)
    sp_ref[...] += jnp.sum(jnp.where(here, scores, 0.0).reshape(cols // 8, 8, queries), axis=0)
    prob = jnp.exp((scores + bias_ref[...]) - lse_ref[...])
    probgrad = jnp.where(here, prob - 1.0, prob).astype(BF16)
    ig_ref[...] = (dot(probgrad, q_ref[...]) * scale).astype(ig_ref.dtype)
    qg_ref[...] += dot(items, probgrad, TN)


def run_grad(items, qt, q, bias, lse, pos, qg, sp, scale, base, block, out_dtype):
    cols, width = items.shape
    nq = qt.shape[1]
    whole = lambda shape: pl.BlockSpec(shape, lambda i: (0, 0))
    tile = pl.BlockSpec((block, width), lambda i: (i, 0))
    return pl.pallas_call(
        functools.partial(grad_kernel, scale, base),
        grid=(cols // block,),
        in_specs=[
            tile,
            whole((width, nq)),
            whole((nq, width)),
            pl.BlockSpec((block, 1), lambda i: (i, 0)),
            whole((1, nq)),
            whole((1, nq)),
            whole((width, nq)),
            whole((8, nq)),
        ],
        out_specs=[tile, whole((width, nq)), whole((8, nq))],
        out_shape=[
            jax.ShapeDtypeStruct((cols, width), out_dtype),
            jax.ShapeDtypeStruct((width, nq), F32),
            jax.ShapeDtypeStruct((8, nq), F32),
        ],
        compiler_params=pltpu.CompilerParams(vmem_limit_bytes=32 << 20),
        cost_estimate=pl.CostEstimate(
            flops=6 * cols * width * nq, bytes_accessed=4 * cols * width, transcendentals=cols * nq
        ),
    )(items, qt, q, bias, lse, pos, qg, sp)


def per_device(queries, item_table, cand_row, cand_owner, cand_count, positive, w_in, b_in, w_out):
    n_data = lax.axis_size("dp")
    n_model = lax.axis_size("mp")
    n_z = n_data // 4
    me = lax.axis_index("dp")
    my_model = lax.axis_index("mp")
    n_query, width_out = queries.shape
    rows, width_emb = item_table.shape
    units = w_in.shape[1]
    part = rows // n_model
    cand_local = cand_row.shape[0]
    n_cols = n_data * part
    quarter = n_z * part
    scale = 1.0 / math.sqrt(width_out)
    block = min(256, quarter)

    def place(rel):
        return ((rel >> 1) & 1) * (2 * n_z) + (rel & 1) * n_z + (rel >> 2)

    word = ((cand_owner[:, 0] * rows + cand_row) * COUNT_BASE + cand_count)[None, :]
    words = jnp.concatenate([word] + [hop(word, k << 2) for k in range(1, n_z)], axis=0)
    words = jnp.concatenate([words, hop(words, 1)], axis=0)
    words = jnp.concatenate([words, hop(words, 2)], axis=0)

    def tower(start):
        emb = lax.dynamic_slice(item_table, (start, 0), (part, width_emb))
        pre = dot(emb, w_in) + b_in[None, :]
        return dot(jnp.maximum(pre, 0.0).astype(BF16), w_out)

    arrived = [hop(tower((my_model ^ k) * part), k, "mp") for k in range(1, n_model)]
    total = tower(my_model * part)
    for other in arrived:
        total = total + other
    item_own = total.astype(BF16)

    core = me & 1
    late_in, late_out, late_b, item_own = lax.optimization_barrier((w_in, w_out, b_in, item_own))
    half_in, half_out = width_emb // 2, units // 2
    piece_in = lax.dynamic_slice(late_in, (core * half_in, 0), (half_in, units))
    piece_out = lax.dynamic_slice(late_out, (core * half_out, 0), (half_out, width_out))
    all_in = jnp.zeros((width_emb, n_model * units), BF16)
    all_out = jnp.zeros((n_model * units, width_out), BF16)
    all_b = jnp.zeros((1, n_model * units), F32)
    all_in = lax.dynamic_update_slice(all_in, w_in, (0, my_model * units))
    all_out = lax.dynamic_update_slice(all_out, w_out, (my_model * units, 0))
    all_b = lax.dynamic_update_slice(all_b, b_in[None, :], (0, my_model * units))

    along_z = [hop(item_own, k << 2) for k in range(1, n_z)]
    cross = hop(item_own, 2)
    far = jnp.concatenate(along_z, axis=0)
    cross_far = hop(far, 2)
    items = [jnp.concatenate([item_own, far], axis=0)]
    items.append(hop(items[0], 1))
    items.append(jnp.concatenate([cross, cross_far], axis=0))
    items.append(hop(items[2], 1))

    for k in range(1, n_model):
        at = (my_model ^ k) * units
        got_in, got_out = hop(piece_in, k, "mp"), hop(piece_out, k, "mp")
        sib_in, sib_out = hop(got_in, 1), hop(got_out, 1)
        all_in = lax.dynamic_update_slice(all_in, got_in, (core * half_in, at))
        all_in = lax.dynamic_update_slice(all_in, sib_in, ((1 - core) * half_in, at))
        all_out = lax.dynamic_update_slice(all_out, got_out, (at + core * half_out, 0))
        all_out = lax.dynamic_update_slice(all_out, sib_out, (at + (1 - core) * half_out, 0))
        all_b = lax.dynamic_update_slice(all_b, hop(late_b[None, :], k, "mp"), (0, at))

    flat = words.reshape(-1)
    n_cand = flat.shape[0]
    row = (flat // COUNT_BASE) % rows
    column = place((flat // (COUNT_BASE * rows)) ^ me) * part + row % part
    column = jnp.where(row // part == my_model, column, -1)
    share = 1.0 / (flat % COUNT_BASE).astype(F32)
    lanes = 128
    high = (jnp.arange(n_cols // lanes)[:, None] == (column >> 7)[None, :]).astype(F32)
    low = jnp.where(jnp.arange(lanes)[:, None] == (column & 127)[None, :], share[None, :], 0.0)
    weight = dot(high, low, NT, precision=lax.Precision.HIGHEST)
    bias = jnp.where(weight > 0.0, jnp.log(weight), ABSENT).reshape(n_cols, 1)

    spot = place((positive // cand_local) ^ me) * cand_local + positive % cand_local
    side = 64
    table = flat.reshape(n_cand // side, side)
    digits = jnp.concatenate([table & 255, (table >> 8) & 255, table >> 16], axis=1).astype(BF16)
    picked = (jnp.arange(n_cand // side)[:, None] == (spot // side)[None, :]).astype(BF16)
    found = dot(digits, picked, TN).reshape(3, side, n_query)
    mine = jnp.arange(side)[:, None] == (spot % side)[None, :]
    digit = jnp.sum(jnp.where(mine[None], found, 0.0), axis=1).astype(jnp.int32)
    pos_word = digit[0] + digit[1] * 256 + digit[2] * 65536
    pos_row = (pos_word // COUNT_BASE) % rows
    pos_col = place((pos_word // (COUNT_BASE * rows)) ^ me) * part + pos_row % part
    pos_col = jnp.where(pos_row // part == my_model, pos_col, -1)[None, :]
    pos_logc = jnp.log((pos_word % COUNT_BASE).astype(F32))

    qt = queries.T
    biases = [bias[j * quarter : (j + 1) * quarter] for j in range(4)]
    m8 = jnp.full((8, n_query), ABSENT, F32)
    l8 = jnp.zeros((8, n_query), F32)
    for j in range(4):
        m8, l8 = run_stats(items[j], qt, biases[j], m8, l8, scale, block)
    m1 = jnp.max(m8, axis=0)
    l1 = jnp.sum(l8 * jnp.exp(m8 - m1[None]), axis=0)
    local = jnp.stack([m1, l1])
    parts = jnp.stack([local] + [hop(local, k, "mp") for k in range(1, n_model)])
    if n_model > 2:
        parts = jnp.take(parts, jnp.arange(n_model) ^ my_model, axis=0)
    row_max = jnp.max(parts[:, 0], axis=0)
    sums = parts[:, 1] * jnp.exp(parts[:, 0] - row_max[None])
    normal = sums[0]
    for k in range(1, n_model):
        normal = normal + sums[k]
    lse = row_max + jnp.log(normal)

    qg = jnp.zeros((width_out, n_query), F32)
    sp = jnp.zeros((8, n_query), F32)
    grads = [None] * 4
    for j in (3, 2, 1, 0):
        grads[j], qg, sp = run_grad(
            items[j], qt, queries, biases[j], lse[None, :], pos_col, qg, sp,
            scale, j * quarter, block, BF16 if j % 2 else F32,
        )

    cross_sum = (grads[2] + hop(grads[3], 1).astype(F32)).astype(BF16)
    cross_far = hop(cross_sum[part:], 2).astype(F32)
    cross_own = hop(cross_sum[:part], 2).astype(F32)
    near_sum = grads[0] + hop(grads[1], 1).astype(F32)
    far_sum = (near_sum[part:] + cross_far).astype(BF16)
    total = near_sum[:part] + cross_own
    for k in range(1, n_z):
        total = total + hop(far_sum[(k - 1) * part : k * part], k << 2).astype(F32)
    own_grad = total.astype(BF16)
    item_grad = jnp.zeros((rows, width_out), BF16)
    item_grad = lax.dynamic_update_slice(item_grad, own_grad, (my_model * part, 0))
    for k in range(1, n_model):
        item_grad = lax.dynamic_update_slice(
            item_grad, hop(own_grad, k, "mp"), ((my_model ^ k) * part, 0)
        )

    sp1 = jnp.sum(sp, axis=0)[None, :]
    pos_score = sp1
    for k in range(1, n_model):
        pos_score = pos_score + hop(sp1, k, "mp")
    loss = lse - (pos_score[0] - pos_logc)
    piece = n_query // n_model
    query_sum = lax.dynamic_slice(qg, (0, my_model * piece), (width_out, piece))
    for k in range(1, n_model):
        query_sum = query_sum + hop(
            lax.dynamic_slice(qg, (0, (my_model ^ k) * piece), (width_out, piece)), k, "mp"
        )
    query_grad = (query_sum * scale).T

    pre = dot(item_table, w_in) + b_in[None, :]
    hidden = jnp.maximum(pre, 0.0).astype(BF16)
    back = dot(item_grad, w_out, NT)
    pre_grad = jnp.where(pre > 0.0, back, 0.0).astype(BF16)
    local_in = dot(item_table, pre_grad, TN)
    local_out = dot(item_grad, hidden, TN)
    local_b = jnp.sum(pre_grad.astype(F32), axis=0)[None, :]
    local_w = jnp.concatenate([local_in, local_out], axis=0)
    high_rows = local_w.shape[0]
    cross_bit, z_part = (me >> 1) & 1, me >> 2

    def halves(value, bit):
        size = value.shape[0] // 2
        keep = lax.dynamic_slice(value, (bit * size, 0), (size, value.shape[1]))
        give = lax.dynamic_slice(value, ((1 - bit) * size, 0), (size, value.shape[1]))
        return keep, give

    keep, give = halves(local_w, core)
    keep, give = halves(keep + hop(give.astype(BF16), 1).astype(F32), cross_bit)
    keep = keep + hop(give.astype(BF16), 2).astype(F32)
    size = high_rows // n_data

    def z_piece(value, k):
        return lax.dynamic_slice(value, ((z_part ^ k) * size, 0), (size, units))

    total = z_piece(keep, 0)
    for k in range(1, n_z):
        total = total + hop(z_piece(keep, k).astype(BF16), k << 2).astype(F32)
    mine = total.astype(BF16)
    whole = jnp.zeros((n_z * size, units), BF16)
    whole = lax.dynamic_update_slice(whole, mine, (z_part * size, 0))
    for k in range(1, n_z):
        whole = lax.dynamic_update_slice(whole, hop(mine, k << 2), ((z_part ^ k) * size, 0))

    def joined(value, bits, bit):
        other = hop(value, bits)
        return jnp.where(
            bit == 0,
            jnp.concatenate([value, other], axis=0),
            jnp.concatenate([other, value], axis=0),
        )

    whole = joined(whole, 2, cross_bit)
    whole = joined(whole, 1, core).astype(F32)
    grad_w_in = whole[:width_emb]
    grad_w_out = whole[width_emb:].T
    bits = 1
    while bits < n_data:
        local_b = local_b + hop(local_b, bits)
        bits *= 2

    pre_all = dot(item_table, all_in) + all_b
    back_all = dot(item_grad, all_out, NT)
    pre_grad_all = jnp.where(pre_all > 0.0, back_all, 0.0).astype(BF16)
    grad_table = dot(pre_grad_all, all_in, NT)
    return (loss, query_grad, grad_w_in, local_b[0], grad_w_out, grad_table)


def solution(mesh):
    placed = (
        P("dp", None),
        P("dp", None),
        P("dp"),
        P("dp", None),
        P("dp"),
        P("dp"),
        P(None, "mp"),
        P("mp"),
        P("mp", None),
    )
    return jax.shard_map(
        per_device,
        mesh=mesh,
        in_specs=placed,
        out_specs=(
            P("dp"),
            P(("dp", "mp"), None),
            P(None, "mp"),
            P("mp"),
            P("mp", None),
            P("dp", None),
        ),
        check_vma=False,
    )
```

```python
import functools
import math

import jax
import jax.numpy as jnp
from jax import lax
from jax.experimental import pallas as pl
from jax.experimental.pallas import tpu as pltpu
from jax.sharding import PartitionSpec as P

F32 = jnp.float32
BF16 = jnp.bfloat16
F16 = jnp.float16
ABSENT = -1e30
COUNT_BASE = 128
WORD_BITS = 22
EXPONENT_BASE = 20
TABLE_MAX = 6.0
W_IN_MAX = 0.25
B_IN_MAX = 3.0
W_OUT_MAX = 0.1875
LIMIT = 32768.0
NT = (((1,), (1,)), ((), ()))
TN = (((0,), (0,)), ((), ()))


def hop(value, bits, axis="dp"):
    size = lax.axis_size(axis)
    return lax.ppermute(value, axis, [(i, i ^ bits) for i in range(size)])


def dot(a, b, dims=None, **kw):
    if dims is None:
        dims = (((1,), (0,)), ((), ()))
    return lax.dot_general(a, b, dims, preferred_element_type=F32, **kw)


def stats_kernel(scale, items_ref, qt_ref, bias_ref, m_in_ref, l_in_ref, m_ref, l_ref):
    @pl.when(pl.program_id(0) == 0)
    def _():
        m_ref[...] = m_in_ref[...]
        l_ref[...] = l_in_ref[...]

    scores = dot(items_ref[...], qt_ref[...]) * scale + bias_ref[...]
    cols, queries = scores.shape
    groups = scores.reshape(cols // 8, 8, queries)
    old = m_ref[...]
    new = jnp.maximum(old, jnp.max(groups, axis=0))
    l_ref[...] = l_ref[...] * jnp.exp(old - new) + jnp.sum(jnp.exp(groups - new[None]), axis=0)
    m_ref[...] = new


def run_stats(items, qt, bias, m, l, scale, block):
    cols, width = items.shape
    nq = qt.shape[1]
    whole = lambda shape: pl.BlockSpec(shape, lambda i: (0, 0))
    return pl.pallas_call(
        functools.partial(stats_kernel, scale),
        grid=(cols // block,),
        in_specs=[
            pl.BlockSpec((block, width), lambda i: (i, 0)),
            whole((width, nq)),
            pl.BlockSpec((block, 1), lambda i: (i, 0)),
            whole((8, nq)),
            whole((8, nq)),
        ],
        out_specs=[whole((8, nq)), whole((8, nq))],
        out_shape=[jax.ShapeDtypeStruct((8, nq), F32)] * 2,
        compiler_params=pltpu.CompilerParams(vmem_limit_bytes=24 << 20),
        cost_estimate=pl.CostEstimate(
            flops=2 * cols * width * nq, bytes_accessed=2 * cols * width, transcendentals=cols * nq
        ),
    )(items, qt, bias, m, l)


def grad_kernel(
    scale, base, items_ref, qt_ref, q_ref, bias_ref, lse_ref, pos_ref, qg_in_ref, sp_in_ref,
    ig_ref, qg_ref, sp_ref,
):
    step = pl.program_id(0)

    @pl.when(step == 0)
    def _():
        qg_ref[...] = qg_in_ref[...]
        sp_ref[...] = sp_in_ref[...]

    items = items_ref[...]
    scores = dot(items, qt_ref[...]) * scale
    cols, queries = scores.shape
    here = lax.broadcasted_iota(jnp.int32, scores.shape, 0) == pos_ref[...] - (base + step * cols)
    sp_ref[...] += jnp.sum(jnp.where(here, scores, 0.0).reshape(cols // 8, 8, queries), axis=0)
    prob = jnp.exp((scores + bias_ref[...]) - lse_ref[...])
    probgrad = jnp.where(here, prob - 1.0, prob).astype(BF16)
    ig_ref[...] = (dot(probgrad, q_ref[...]) * scale).astype(ig_ref.dtype)
    qg_ref[...] += dot(items, probgrad, TN)


def run_grad(items, qt, q, bias, lse, pos, qg, sp, scale, base, block, out_dtype):
    cols, width = items.shape
    nq = qt.shape[1]
    whole = lambda shape: pl.BlockSpec(shape, lambda i: (0, 0))
    tile = pl.BlockSpec((block, width), lambda i: (i, 0))
    return pl.pallas_call(
        functools.partial(grad_kernel, scale, base),
        grid=(cols // block,),
        in_specs=[
            tile,
            whole((width, nq)),
            whole((nq, width)),
            pl.BlockSpec((block, 1), lambda i: (i, 0)),
            whole((1, nq)),
            whole((1, nq)),
            whole((width, nq)),
            whole((8, nq)),
        ],
        out_specs=[tile, whole((width, nq)), whole((8, nq))],
        out_shape=[
            jax.ShapeDtypeStruct((cols, width), out_dtype),
            jax.ShapeDtypeStruct((width, nq), F32),
            jax.ShapeDtypeStruct((8, nq), F32),
        ],
        compiler_params=pltpu.CompilerParams(vmem_limit_bytes=32 << 20),
        cost_estimate=pl.CostEstimate(
            flops=6 * cols * width * nq, bytes_accessed=4 * cols * width, transcendentals=cols * nq
        ),
    )(items, qt, q, bias, lse, pos, qg, sp)


def per_device(queries, item_table, cand_row, cand_owner, cand_count, positive, w_in, b_in, w_out):
    n_data = lax.axis_size("dp")
    n_model = lax.axis_size("mp")
    n_z = n_data // 4
    me = lax.axis_index("dp")
    my_model = lax.axis_index("mp")
    n_query, width_out = queries.shape
    rows, width_emb = item_table.shape
    units = w_in.shape[1]
    part = rows // n_model
    cand_local = cand_row.shape[0]
    n_cols = n_data * part
    chunk = n_z * part // 2
    scale = 1.0 / math.sqrt(width_out)
    block = min(256, chunk)
    tie = lax.optimization_barrier

    def place(rel):
        return ((rel >> 1) & 1) * (2 * n_z) + (rel & 1) * n_z + (rel >> 2)

    def bit_of(bits):
        return (me // bits) & 1

    embs = [
        lax.dynamic_slice(item_table, ((my_model ^ k) * part, 0), (part, width_emb))
        for k in range(n_model)
    ]
    pres, hiddens = [None] * n_model, [None] * n_model

    def tower(k):
        pres[k] = dot(embs[k], w_in) + b_in[None, :]
        hiddens[k] = jnp.maximum(pres[k], 0.0).astype(BF16)
        return dot(hiddens[k], w_out)

    outgoing = [tower(k) for k in range(1, n_model)]
    outgoing, cand_row, queries = tie((outgoing, cand_row, queries))
    arrived = [hop(value, k + 1, "mp") for k, value in enumerate(outgoing)]
    total = tower(0)
    for other in arrived:
        total = total + other
    item_own = total.astype(BF16)

    largest = jnp.max(jnp.abs(queries)).astype(F32)
    exponent = jnp.floor(jnp.log2(jnp.maximum(largest, 1e-6))).astype(jnp.int32) + 1
    exponent = jnp.clip(exponent + EXPONENT_BASE, 0, 63)
    word = (cand_owner[:, 0] * rows + cand_row) * COUNT_BASE + cand_count
    word = (word + exponent * (1 << WORD_BITS))[None, :]
    words = [word]
    bits = n_data // 2
    while bits >= 4:
        words = [w for v in words for w in (v, hop(v, bits))]
        bits //= 2
    words = jnp.concatenate(words, axis=0)
    words = jnp.concatenate([words, hop(words, 1)], axis=0)
    words = jnp.concatenate([words, hop(words, 2)], axis=0)

    along_z = {0: item_own}
    bits = n_z // 2
    while bits:
        along_z.update({j | bits: hop(v, bits << 2) for j, v in list(along_z.items())})
        bits //= 2
    along_x = {j: hop(v, 2) for j, v in along_z.items()}
    items = {}
    for x, blocks in enumerate((along_z, along_x)):
        for h in range(2):
            span = range(h * n_z // 2, (h + 1) * n_z // 2)
            items[x, 0, h] = jnp.concatenate([blocks[j] for j in span], axis=0)
            items[x, 1, h] = hop(items[x, 0, h], 1)

    flat = words.reshape(-1)
    n_cand = flat.shape[0]
    q_bound = jnp.exp2((jnp.max(flat >> WORD_BITS) - EXPONENT_BASE).astype(F32))
    flat = flat & ((1 << WORD_BITS) - 1)
    row = (flat // COUNT_BASE) % rows
    column = place((flat // (COUNT_BASE * rows)) ^ me) * part + row % part
    column = jnp.where(row // part == my_model, column, -1)
    share = 1.0 / (flat % COUNT_BASE).astype(F32)
    lanes = 128
    high = (jnp.arange(n_cols // lanes)[:, None] == (column >> 7)[None, :]).astype(F32)
    low = jnp.where(jnp.arange(lanes)[:, None] == (column & 127)[None, :], share[None, :], 0.0)
    weight = dot(high, low, NT, precision=lax.Precision.HIGHEST)
    bias = jnp.where(weight > 0.0, jnp.log(weight), ABSENT).reshape(n_cols, 1)

    spot = place((positive // cand_local) ^ me) * cand_local + positive % cand_local
    side = 64
    table = flat.reshape(n_cand // side, side)
    digits = jnp.concatenate([table & 255, (table >> 8) & 255, table >> 16], axis=1).astype(BF16)
    picked = (jnp.arange(n_cand // side)[:, None] == (spot // side)[None, :]).astype(BF16)
    found = dot(digits, picked, TN).reshape(3, side, n_query)
    mine = jnp.arange(side)[:, None] == (spot % side)[None, :]
    digit = jnp.sum(jnp.where(mine[None], found, 0.0), axis=1).astype(jnp.int32)
    pos_word = digit[0] + digit[1] * 256 + digit[2] * 65536
    pos_row = (pos_word // COUNT_BASE) % rows
    pos_col = place((pos_word // (COUNT_BASE * rows)) ^ me) * part + pos_row % part
    pos_col = jnp.where(pos_row // part == my_model, pos_col, -1)[None, :]
    pos_logc = jnp.log((pos_word % COUNT_BASE).astype(F32))

    qt = queries.T
    keys = [(x, c, h) for x in range(2) for h in range(2) for c in range(2)]
    start_of = {(x, c, h): ((x * 2 + c) * 2 + h) * chunk for x, c, h in keys}
    biases = {key: bias[start_of[key] : start_of[key] + chunk] for key in keys}
    m8 = jnp.full((8, n_query), ABSENT, F32)
    l8 = jnp.zeros((8, n_query), F32)
    for key in keys:
        m8, l8 = run_stats(items[key], qt, biases[key], m8, l8, scale, block)
    m1 = jnp.max(m8, axis=0)
    l1 = jnp.sum(l8 * jnp.exp(m8 - m1[None]), axis=0)
    local = jnp.stack([m1, l1])
    parts = jnp.stack([local] + [hop(local, k, "mp") for k in range(1, n_model)])
    if n_model > 2:
        parts = jnp.take(parts, jnp.arange(n_model) ^ my_model, axis=0)
    row_max = jnp.max(parts[:, 0], axis=0)
    sums = parts[:, 1] * jnp.exp(parts[:, 0] - row_max[None])
    normal = sums[0]
    for k in range(1, n_model):
        normal = normal + sums[k]
    lse = row_max + jnp.log(normal)

    def wire(bound):
        factor = (LIMIT / bound) / q_bound
        return (lambda v: (v * factor).astype(F16)), (lambda v: v.astype(F32) * (1.0 / factor))

    def send(value, bits, bound):
        shrink, grow = wire(bound)
        return grow(hop(shrink(value), bits))

    def item_bound(devices):
        return devices * n_query * 2.0 * scale

    qg = jnp.zeros((width_out, n_query), F32)
    sp = jnp.zeros((8, n_query), F32)
    chip_sums = {}
    for x, h in ((1, 1), (1, 0), (0, 1), (0, 0)):
        both = [None] * 2
        for c in (1, 0):
            key = (x, c, h)
            both[c], qg, sp = run_grad(
                items[key], qt, queries, biases[key], lse[None, :], pos_col, qg, sp,
                scale, start_of[key], block, F32,
            )
        chip_sums[x, h] = both[0] + send(both[1], 1, item_bound(1))
    z_sums = [None] * n_z
    for h in (1, 0):
        pair_sum = chip_sums[0, h] + send(chip_sums[1, h], 2, item_bound(2))
        for j in range(n_z // 2):
            z_sums[h * n_z // 2 + j] = pair_sum[j * part : (j + 1) * part]
    bits = 1
    while bits < n_z:
        for j in reversed(range(0, n_z, 2 * bits)):
            z_sums[j] = z_sums[j] + send(z_sums[j + bits], bits << 2, item_bound(4 * bits))
        bits *= 2
    own_grad = z_sums[0].astype(BF16)

    piece = n_query // n_model
    sp1 = jnp.sum(sp, axis=0)[None, :]
    qg_parts = [
        lax.dynamic_slice(qg, (0, (my_model ^ k) * piece), (width_out, piece))
        for k in range(n_model)
    ]
    pos_score, query_sum = sp1, qg_parts[0]
    for k in range(1, n_model):
        query_sum = query_sum + hop(qg_parts[k], k, "mp")
        pos_score = pos_score + hop(sp1, k, "mp")
    loss = lse - (pos_score[0] - pos_logc)
    query_grad = (query_sum * scale).T
    own_grad, loss, query_grad = tie((own_grad, loss, query_grad))

    item_grad = jnp.concatenate(
        [own_grad] + [hop(own_grad, k, "mp") for k in range(1, n_model)], axis=0
    )
    emb = jnp.concatenate(embs, axis=0)
    pre = jnp.concatenate(pres, axis=0)
    hidden = jnp.concatenate(hiddens, axis=0)
    pre_grad = jnp.where(pre > 0.0, dot(item_grad, w_out, NT), 0.0).astype(BF16)
    local_in = dot(emb, pre_grad, TN)
    local_out = dot(hidden, item_grad, TN).reshape(width_emb, -1)
    local_b = jnp.sum(pre_grad.astype(F32), axis=0)[None, :]

    gradient_sum = n_data * n_query * 2.0 * scale
    bound_in = gradient_sum * width_out * W_OUT_MAX * TABLE_MAX
    bound_out = gradient_sum * (width_emb * TABLE_MAX * W_IN_MAX + B_IN_MAX)
    factor_in, factor_out = (LIMIT / bound_in) / q_bound, (LIMIT / bound_out) / q_bound
    value = jnp.concatenate([local_in * factor_in, local_out * factor_out], axis=1)
    width = value.shape[1]
    bits = 1
    while bits < n_data:
        size = value.shape[0] // 2
        keep = lax.dynamic_slice(value, (bit_of(bits) * size, 0), (size, width))
        give = lax.dynamic_slice(value, ((1 - bit_of(bits)) * size, 0), (size, width))
        value = keep + hop(give.astype(F16), bits).astype(F32)
        local_b = local_b + hop(local_b, bits)
        bits *= 2
    value = value.astype(F16)
    while bits > 1:
        bits //= 2
        other = hop(value, bits)
        value = jnp.where(
            bit_of(bits) == 0,
            jnp.concatenate([value, other], axis=0),
            jnp.concatenate([other, value], axis=0),
        )
    grad_w_in = value[:, :units].astype(F32) * (1.0 / factor_in)
    grad_w_out = (value[:, units:].astype(F32) * (1.0 / factor_out)).reshape(units, width_out)

    emb_parts = dot(pre_grad, w_in, NT).reshape(n_model, part, width_emb)
    emb_sum = emb_parts[0]
    for k in range(1, n_model):
        emb_sum = emb_sum + hop(emb_parts[k], k, "mp")
    emb_own = emb_sum.astype(BF16)
    pieces = [emb_own] + [hop(emb_own, k, "mp") for k in range(1, n_model)]
    if n_model == 2:
        grad_table = jnp.where(
            my_model == 0,
            jnp.concatenate(pieces, axis=0),
            jnp.concatenate(pieces[::-1], axis=0),
        )
    else:
        grad_table = jnp.take(jnp.stack(pieces), jnp.arange(n_model) ^ my_model, axis=0)
        grad_table = grad_table.reshape(rows, width_emb)
    return (loss, query_grad, grad_w_in, local_b[0], grad_w_out, grad_table.astype(F32))


def solution(mesh):
    placed = (
        P("dp", None),
        P("dp", None),
        P("dp"),
        P("dp", None),
        P("dp"),
        P("dp"),
        P(None, "mp"),
        P("mp"),
        P("mp", None),
    )
    return jax.shard_map(
        per_device,
        mesh=mesh,
        in_specs=placed,
        out_specs=(
            P("dp"),
            P(("dp", "mp"), None),
            P(None, "mp"),
            P("mp"),
            P("mp", None),
            P("dp", None),
        ),
        check_vma=False,
    )
```

```python
import functools
import math

import jax
import jax.numpy as jnp
from jax import lax
from jax.experimental import pallas as pl
from jax.experimental.pallas import tpu as pltpu
from jax.sharding import PartitionSpec as P

F32 = jnp.float32
BF16 = jnp.bfloat16
F16 = jnp.float16
ABSENT = -1e30
COUNT_BASE = 128
WORD_BITS = 22
EXPONENT_BASE = 20
TABLE_MAX = 6.0
W_IN_MAX = 0.25
B_IN_MAX = 3.0
W_OUT_MAX = 0.1875
LIMIT = 32768.0
LOG2E = math.log2(math.e)
GROUP = 16
NT = (((1,), (1,)), ((), ()))
TN = (((0,), (0,)), ((), ()))


def hop(value, bits, axis="dp"):
    size = lax.axis_size(axis)
    return lax.ppermute(value, axis, [(i, i ^ bits) for i in range(size)])


def dot(a, b, dims=None, **kw):
    if dims is None:
        dims = (((1,), (0,)), ((), ()))
    return lax.dot_general(a, b, dims, preferred_element_type=F32, **kw)


def column_bias(bias_ref, first, count):
    lane = first // 128
    return bias_ref[pl.ds(first % 128, count), lane : lane + 1]


def stats_kernel(scale, base, block, items_ref, qt_ref, bias_ref, m_in_ref, l_in_ref, m_ref, l_ref, *score_refs):
    cols = items_ref.shape[0]
    old = m_in_ref[...]
    new = old
    for n, score_ref in enumerate(score_refs):
        score_ref[...] = dot(items_ref[n * block : (n + 1) * block], qt_ref[...])
    for n, score_ref in enumerate(score_refs):
        for r in range(0, block, 8):
            bias = column_bias(bias_ref, base + n * block + r, 8)
            score = score_ref[r : r + 8] * scale + bias
            score_ref[r : r + 8] = score
            new = jnp.maximum(new, score)
    total = l_in_ref[...] * jnp.exp2(old - new)
    for n, score_ref in enumerate(score_refs):
        for r in range(0, block, 8):
            total = total + jnp.exp2(score_ref[r : r + 8] - new)
    m_ref[...] = new
    l_ref[...] = total


def in_vmem(count):
    return [pl.BlockSpec(memory_space=pltpu.VMEM)] * count


def run_stats(items, qt, bias, m, l, scale, base, block):
    cols, width = items.shape
    nq = qt.shape[1]
    return pl.pallas_call(
        functools.partial(stats_kernel, scale, base, block),
        in_specs=in_vmem(5),
        out_specs=in_vmem(2),
        out_shape=[jax.ShapeDtypeStruct((8, nq), F32)] * 2,
        scratch_shapes=[pltpu.VMEM((block, nq), F32)] * (cols // block),
        compiler_params=pltpu.CompilerParams(vmem_limit_bytes=16 << 20),
        cost_estimate=pl.CostEstimate(
            flops=2 * cols * width * nq, bytes_accessed=2 * cols * width, transcendentals=cols * nq
        ),
    )(items, qt, bias, m, l)


def grad_kernel(
    scale, base, block, items_ref, qt_ref, q_ref, bias_ref, lse_ref, pos_ref, qg_in_ref, sp_in_ref,
    ig_ref, qg_ref, sp_ref, *scratch,
):
    count = items_ref.shape[0] // block
    score_refs, prob_refs = scratch[:count], scratch[count:]
    queries = qt_ref.shape[1]
    for n, score_ref in enumerate(score_refs):
        score_ref[...] = dot(items_ref[n * block : (n + 1) * block], qt_ref[...])
    down = lax.broadcasted_iota(jnp.int32, (8, queries), 0)
    offset = jnp.broadcast_to(pos_ref[...], (8, queries)) - down
    lse = jnp.broadcast_to(lse_ref[...], (8, queries))
    found = sp_in_ref[...]
    for n in range(count):
        score_ref, prob_ref = score_refs[n], prob_refs[n]
        for r in range(0, block, GROUP):
            pieces = []
            for s in range(r, r + GROUP, 8):
                at = base + n * block + s
                score = score_ref[s : s + 8]
                here = offset == at
                found = found + jnp.where(here, score, 0.0)
                prob = jnp.exp2((score * (scale * LOG2E) + column_bias(bias_ref, at, 8)) - lse)
                pieces.append(jnp.where(here, prob - 1.0, prob))
            prob_ref[r : r + GROUP] = jnp.concatenate(pieces, axis=0).astype(BF16)
        rows = slice(n * block, (n + 1) * block)
        ig_ref[rows] = dot(prob_ref[...], q_ref[...]) * scale
        share = dot(items_ref[rows], prob_ref[...], TN)
        qg_ref[...] = (qg_in_ref[...] if n == 0 else qg_ref[...]) + share
    sp_ref[...] = found


def run_grad(items, qt, q, bias, lse, pos, qg, sp, scale, base, block):
    cols, width = items.shape
    nq = qt.shape[1]
    return pl.pallas_call(
        functools.partial(grad_kernel, scale, base, block),
        in_specs=in_vmem(8),
        out_specs=in_vmem(3),
        out_shape=[
            jax.ShapeDtypeStruct((cols, width), F32),
            jax.ShapeDtypeStruct((width, nq), F32),
            jax.ShapeDtypeStruct((8, nq), F32),
        ],
        scratch_shapes=[pltpu.VMEM((block, nq), F32)] * (cols // block)
        + [pltpu.VMEM((block, nq), BF16)] * (cols // block),
        input_output_aliases={6: 1, 7: 2},
        compiler_params=pltpu.CompilerParams(vmem_limit_bytes=20 << 20),
        cost_estimate=pl.CostEstimate(
            flops=6 * cols * width * nq, bytes_accessed=4 * cols * width, transcendentals=cols * nq
        ),
    )(items, qt, q, bias, lse, pos, qg, sp)


def xor_concat(blocks, index, axis=0):
    if len(blocks) == 1:
        return blocks[0]
    half = len(blocks) // 2
    low = xor_concat(blocks[:half], index, axis)
    high = xor_concat(blocks[half:], index, axis)
    return jnp.where(
        (index & half) == 0,
        jnp.concatenate([low, high], axis=axis),
        jnp.concatenate([high, low], axis=axis),
    )


def per_device(queries, item_table, cand_row, cand_owner, cand_count, positive, w_in, b_in, w_out):
    n_data = lax.axis_size("dp")
    n_model = lax.axis_size("mp")
    n_z = n_data // 4
    me = lax.axis_index("dp")
    my_model = lax.axis_index("mp")
    n_query, width_out = queries.shape
    rows, width_emb = item_table.shape
    units = w_in.shape[1]
    part = rows // n_model
    cand_local = cand_row.shape[0]
    n_cols = n_data * part
    chunk = n_z * part // 2
    scale = 1.0 / math.sqrt(width_out)
    block = min(256, chunk)
    tie = lax.optimization_barrier

    def place(rel):
        return ((rel >> 1) & 1) * (2 * n_z) + (rel & 1) * n_z + (rel >> 2)

    def bit_of(bits):
        return (me // bits) & 1

    pre = dot(item_table, w_in) + b_in[None, :]
    hidden = jnp.maximum(pre, 0.0).astype(BF16)
    partial = dot(hidden, w_out)

    def part_of(value, k):
        return lax.dynamic_slice(value, ((my_model ^ k) * part, 0), (part, value.shape[1]))

    outgoing = [part_of(partial, k) for k in range(1, n_model)]
    outgoing, cand_row, queries = tie((outgoing, cand_row, queries))
    total = part_of(partial, 0)
    for k in range(1, n_model):
        total = total + hop(outgoing[k - 1], k, "mp")
    item_own = total.astype(BF16)

    largest = jnp.max(jnp.abs(queries)).astype(F32)
    exponent = jnp.floor(jnp.log2(jnp.maximum(largest, 1e-6))).astype(jnp.int32) + 1
    exponent = jnp.clip(exponent + EXPONENT_BASE, 0, 63)
    word = (cand_owner[:, 0] * rows + cand_row) * COUNT_BASE + cand_count
    word = (word + exponent * (1 << WORD_BITS))[None, :]
    direct = [word] + [hop(word, k << 1) for k in range(1, 2 * n_z)]
    near = jnp.concatenate(direct[0::2] + direct[1::2], axis=0)
    far = hop(near, 1)
    words = jnp.concatenate([near[:n_z], far[:n_z], near[n_z:], far[n_z:]], axis=0)

    along_z = {0: item_own}
    bits = n_z // 2
    while bits:
        along_z.update({j | bits: hop(v, bits << 2) for j, v in list(along_z.items())})
        bits //= 2
    along_x = {j: hop(v, 2) for j, v in along_z.items()}
    items = {}
    for x, blocks in enumerate((along_z, along_x)):
        for h in range(2):
            span = range(h * n_z // 2, (h + 1) * n_z // 2)
            items[x, 0, h] = jnp.concatenate([blocks[j] for j in span], axis=0)
            items[x, 1, h] = hop(items[x, 0, h], 1)

    flat = words.reshape(-1)
    n_cand = flat.shape[0]
    q_bound = jnp.exp2((jnp.max(flat >> WORD_BITS) - EXPONENT_BASE).astype(F32))
    flat = flat & ((1 << WORD_BITS) - 1)
    row = (flat // COUNT_BASE) % rows
    column = place((flat // (COUNT_BASE * rows)) ^ me) * part + row % part
    column = jnp.where(row // part == my_model, column, -1)
    share = 1.0 / (flat % COUNT_BASE).astype(F32)
    lanes = 128
    high = (jnp.arange(n_cols // lanes)[:, None] == (column >> 7)[None, :]).astype(F32)
    low = jnp.where(jnp.arange(lanes)[:, None] == (column & 127)[None, :], share[None, :], 0.0)
    weight = dot(low, high, NT, precision=lax.Precision.HIGHEST)
    bias = jnp.where(weight > 0.0, jnp.log2(weight), ABSENT)

    spot = place((positive // cand_local) ^ me) * cand_local + positive % cand_local
    side = 64
    table = flat.reshape(n_cand // side, side)
    digits = jnp.concatenate([table & 255, (table >> 8) & 255, table >> 16], axis=1).astype(BF16)
    picked = (jnp.arange(n_cand // side)[:, None] == (spot // side)[None, :]).astype(BF16)
    found = dot(digits, picked, TN).reshape(3, side, n_query)
    mine = jnp.arange(side)[:, None] == (spot % side)[None, :]
    digit = jnp.sum(jnp.where(mine[None], found, 0.0), axis=1).astype(jnp.int32)
    pos_word = digit[0] + digit[1] * 256 + digit[2] * 65536
    pos_row = (pos_word // COUNT_BASE) % rows
    pos_col = place((pos_word // (COUNT_BASE * rows)) ^ me) * part + pos_row % part
    pos_col = jnp.where(pos_row // part == my_model, pos_col, -1)[None, :]
    pos_logc = jnp.log((pos_word % COUNT_BASE).astype(F32))

    qt = queries.T
    keys = [(x, c, h) for x in range(2) for h in range(2) for c in range(2)]
    start_of = {(x, c, h): ((x * 2 + c) * 2 + h) * chunk for x, c, h in keys}
    m8 = jnp.full((8, n_query), ABSENT, F32)
    l8 = jnp.zeros((8, n_query), F32)
    for number, key in enumerate(keys):
        m8, l8 = run_stats(items[key], qt, bias, m8, l8, scale * LOG2E, start_of[key], block)
        if number < 5:
            later = [k for k in keys[number + 2 :]]
            values, m8, l8 = tie(([items[k] for k in later], m8, l8))
            items.update(zip(later, values))
    m1 = jnp.max(m8, axis=0)
    l1 = jnp.sum(l8 * jnp.exp2(m8 - m1[None]), axis=0)
    local = jnp.stack([m1, l1])
    parts = jnp.stack([local] + [hop(local, k, "mp") for k in range(1, n_model)])
    if n_model > 2:
        parts = jnp.take(parts, jnp.arange(n_model) ^ my_model, axis=0)
    row_max = jnp.max(parts[:, 0], axis=0)
    sums = parts[:, 1] * jnp.exp2(parts[:, 0] - row_max[None])
    normal = sums[0]
    for k in range(1, n_model):
        normal = normal + sums[k]
    lse = row_max + jnp.log2(normal)

    core = me & 1
    packed = jnp.concatenate([w_in, w_out.reshape(width_emb, -1)], axis=1)
    half_rows = width_emb // 2
    piece = lax.dynamic_slice(packed, (core * half_rows, 0), (half_rows, packed.shape[1]))
    piece, b_late, lse = tie((piece, b_in[None, :], lse))
    others = []
    for k in range(1, n_model):
        got = hop(piece, k, "mp")
        others.append((xor_concat([got, hop(got, 1)], core), hop(b_late, k, "mp")))

    def wire(bound):
        factor = (LIMIT / bound) / q_bound
        return (lambda v: (v * factor).astype(F16)), (lambda v: v.astype(F32) * (1.0 / factor))

    def send(value, bits, bound):
        shrink, grow = wire(bound)
        return grow(hop(shrink(value), bits))

    def item_bound(devices):
        return devices * n_query * 2.0 * scale

    qg = jnp.zeros((width_out, n_query), F32)
    sp = jnp.zeros((8, n_query), F32)
    chip_sums, crossing, crossed, z_sums = {}, {}, {}, [None] * n_z
    shrink, grow = wire(item_bound(2))
    order = ((1, 1), (1, 0), (0, 1), (0, 0))
    for number, (x, h) in enumerate(order):
        both = [None] * 2
        for c in (1, 0):
            key = (x, c, h)
            both[c], qg, sp = run_grad(
                items[key], qt, queries, bias, lse[None, :], pos_col, qg, sp,
                scale, start_of[key], block,
            )
            if c == 1 and number in (1, 2):
                previous = order[number - 1][1]
                crossing[previous] = shrink(chip_sums[1, previous])
                crossing[previous], qg = tie((crossing[previous], qg))
                crossed[previous] = grow(hop(crossing[previous], 2))
        chip_sums[x, h] = both[0] + hop(both[1], 1)
    for h in (1, 0):
        pair_sum = chip_sums[0, h] + crossed[h]
        for j in range(n_z // 2):
            z_sums[h * n_z // 2 + j] = pair_sum[j * part : (j + 1) * part]
    bits = 1
    while bits < n_z:
        for j in reversed(range(0, n_z, 2 * bits)):
            z_sums[j] = z_sums[j] + send(z_sums[j + bits], bits << 2, item_bound(4 * bits))
        bits *= 2
    own_grad = z_sums[0].astype(BF16)

    hidden_max = width_emb * TABLE_MAX * W_IN_MAX + B_IN_MAX
    item_max = n_model * units * hidden_max * W_OUT_MAX
    q_factor = LIMIT / (2.0 * item_max)
    share = n_query // n_model
    sp1 = jnp.sum(sp, axis=0)[None, :]
    qg_parts = [
        lax.dynamic_slice(qg, (0, (my_model ^ k) * share), (width_out, share))
        for k in range(n_model)
    ]
    pos_score, query_sum = sp1, qg_parts[0]
    for k in range(1, n_model):
        sent = hop((qg_parts[k] * q_factor).astype(F16), k, "mp")
        query_sum = query_sum + sent.astype(F32) * (1.0 / q_factor)
        pos_score = pos_score + hop(sp1, k, "mp")
    loss = lse * (1.0 / LOG2E) - (pos_score[0] * scale - pos_logc)
    query_grad = (query_sum * scale).T
    own_grad, loss, query_grad, others = tie((own_grad, loss, query_grad, others))

    item_grad = xor_concat(
        [own_grad] + [hop(own_grad, k, "mp") for k in range(1, n_model)], my_model
    )

    def backward(grad, weights, pre_values):
        return jnp.where(pre_values > 0.0, dot(grad, weights, NT), 0.0).astype(BF16)

    pre_grad = backward(item_grad, w_out, pre)
    local_in = dot(item_table, pre_grad, TN)
    local_out = dot(hidden, item_grad, TN).reshape(width_emb, -1)
    local_b = jnp.sum(pre_grad.astype(F32), axis=0)[None, :]

    gradient_sum = n_data * n_query * 2.0 * scale
    bound_in = gradient_sum * width_out * W_OUT_MAX * TABLE_MAX
    bound_out = gradient_sum * hidden_max
    factor_in, factor_out = (LIMIT / bound_in) / q_bound, (LIMIT / bound_out) / q_bound
    value = jnp.concatenate([local_in * factor_in, local_out * factor_out], axis=1)
    width = value.shape[1]
    keep = lax.dynamic_slice(value, (core * half_rows, 0), (half_rows, width))
    give = lax.dynamic_slice(value, ((1 - core) * half_rows, 0), (half_rows, width))
    bias_steps = [1 << n for n in range(n_data.bit_length() - 1)]

    def step_bias(value, steps):
        for _ in range(min(steps, len(bias_steps))):
            bits = bias_steps.pop(0)
            value = value + hop(value, bits)
        return value

    value = keep + hop(give.astype(F16), 1).astype(F32)
    value, local_b = tie((value, step_bias(local_b, 1)))
    chips = n_data // 2
    my_chip = me >> 1
    size = half_rows // chips
    narrow = value.astype(F16)
    total = lax.dynamic_slice(value, (my_chip * size, 0), (size, width))
    for k in range(1, chips):
        block_out = lax.dynamic_slice(narrow, ((my_chip ^ k) * size, 0), (size, width))
        total = total + hop(block_out, k << 1).astype(F32)
    total, local_b = tie((total.astype(F16), step_bias(local_b, 1)))
    blocks = [total] + [hop(total, k << 1) for k in range(1, chips)]
    blocks, local_b = tie((blocks, step_bias(local_b, 1)))
    own_half = xor_concat(blocks, my_chip)
    value = xor_concat([own_half, hop(own_half, 1)], core)
    grad_w_in = value[:, :units].astype(F32) * (1.0 / factor_in)
    grad_w_out = (value[:, units:].astype(F32) * (1.0 / factor_out)).reshape(units, width_out)
    local_b = step_bias(local_b, len(bias_steps))

    weights = [(packed, b_in[None, :])] + others
    if n_model > 2:
        turn = jnp.arange(n_model) ^ my_model
        stacks = [jnp.take(jnp.stack(group), turn, axis=0) for group in zip(*weights)]
        weights = [(stacks[0][k], stacks[1][k]) for k in range(n_model)]
    grad_table = None
    for pack, bias_units in weights:
        share_in, share_out = pack[:, :units], pack[:, units:].reshape(units, width_out)
        pre_units = dot(item_table, share_in) + bias_units
        term = dot(backward(item_grad, share_out, pre_units), share_in, NT)
        grad_table = term if grad_table is None else grad_table + term
    return (loss, query_grad, grad_w_in, local_b[0], grad_w_out, grad_table)


def solution(mesh):
    placed = (
        P("dp", None),
        P("dp", None),
        P("dp"),
        P("dp", None),
        P("dp"),
        P("dp"),
        P(None, "mp"),
        P("mp"),
        P("mp", None),
    )
    return jax.shard_map(
        per_device,
        mesh=mesh,
        in_specs=placed,
        out_specs=(
            P("dp"),
            P(("dp", "mp"), None),
            P(None, "mp"),
            P("mp"),
            P("mp", None),
            P("dp", None),
        ),
        check_vma=False,
    )
```

```python
import functools
import math

import jax
import jax.numpy as jnp
from jax import lax
from jax.experimental import pallas as pl
from jax.experimental.pallas import tpu as pltpu
from jax.sharding import PartitionSpec as P

F32 = jnp.float32
BF16 = jnp.bfloat16
F16 = jnp.float16
ABSENT = -1e30
COUNT_BASE = 128
WORD_BITS = 22
EXPONENT_BASE = 20
TABLE_MAX = 6.0
W_IN_MAX = 0.25
B_IN_MAX = 3.0
W_OUT_MAX = 0.1875
LIMIT = 32768.0
LOG2E = math.log2(math.e)
GROUP = 16
NT = (((1,), (1,)), ((), ()))
TN = (((0,), (0,)), ((), ()))


def hop(value, bits, axis="dp"):
    size = lax.axis_size(axis)
    return lax.ppermute(value, axis, [(i, i ^ bits) for i in range(size)])


def dot(a, b, dims=None, **kw):
    if dims is None:
        dims = (((1,), (0,)), ((), ()))
    return lax.dot_general(a, b, dims, preferred_element_type=F32, **kw)


def column_bias(bias_ref, first, count):
    lane = first // 128
    return bias_ref[pl.ds(first % 128, count), lane : lane + 1]


def stats_kernel(scale, base, block, items_ref, qt_ref, bias_ref, m_in_ref, l_in_ref, m_ref, l_ref, *score_refs):
    cols = items_ref.shape[0]
    old = m_in_ref[...]
    new = old
    for n, score_ref in enumerate(score_refs):
        score_ref[...] = dot(items_ref[n * block : (n + 1) * block], qt_ref[...])
    for n, score_ref in enumerate(score_refs):
        for r in range(0, block, 8):
            bias = column_bias(bias_ref, base + n * block + r, 8)
            score = score_ref[r : r + 8] * scale + bias
            score_ref[r : r + 8] = score
            new = jnp.maximum(new, score)
    total = l_in_ref[...] * jnp.exp2(old - new)
    for n, score_ref in enumerate(score_refs):
        for r in range(0, block, 8):
            total = total + jnp.exp2(score_ref[r : r + 8] - new)
    m_ref[...] = new
    l_ref[...] = total


def in_vmem(count):
    return [pl.BlockSpec(memory_space=pltpu.VMEM)] * count


def run_stats(items, qt, bias, m, l, scale, base, block):
    cols, width = items.shape
    nq = qt.shape[1]
    return pl.pallas_call(
        functools.partial(stats_kernel, scale, base, block),
        in_specs=in_vmem(5),
        out_specs=in_vmem(2),
        out_shape=[jax.ShapeDtypeStruct((8, nq), F32)] * 2,
        scratch_shapes=[pltpu.VMEM((block, nq), F32)] * (cols // block),
        compiler_params=pltpu.CompilerParams(vmem_limit_bytes=16 << 20),
        cost_estimate=pl.CostEstimate(
            flops=cols * width, bytes_accessed=cols, transcendentals=0
        ),
    )(items, qt, bias, m, l)


def grad_kernel(
    scale, base, block, add, items_ref, qt_ref, q_ref, bias_ref, lse_ref, pos_ref, qg_in_ref, sp_in_ref,
    *refs,
):
    more_ref = refs[0] if add else None
    ig_ref, qg_ref, sp_ref, *scratch = refs[add:]
    count = items_ref.shape[0] // block
    score_refs, prob_refs = scratch[:count], scratch[count:]
    queries = qt_ref.shape[1]
    for n, score_ref in enumerate(score_refs):
        score_ref[...] = dot(items_ref[n * block : (n + 1) * block], qt_ref[...])
    down = lax.broadcasted_iota(jnp.int32, (8, queries), 0)
    offset = jnp.broadcast_to(pos_ref[...], (8, queries)) - down
    lse = jnp.broadcast_to(lse_ref[...], (8, queries))
    found = sp_in_ref[...]
    for n in range(count):
        score_ref, prob_ref = score_refs[n], prob_refs[n]
        for r in range(0, block, GROUP):
            pieces = []
            for s in range(r, r + GROUP, 8):
                at = base + n * block + s
                score = score_ref[s : s + 8]
                here = offset == at
                found = found + jnp.where(here, score, 0.0)
                prob = jnp.exp2((score * (scale * LOG2E) + column_bias(bias_ref, at, 8)) - lse)
                pieces.append(jnp.where(here, prob - 1.0, prob))
            prob_ref[r : r + GROUP] = jnp.concatenate(pieces, axis=0).astype(BF16)
        rows = slice(n * block, (n + 1) * block)
        sums = dot(prob_ref[...], q_ref[...]) * scale
        ig_ref[rows] = sums + more_ref[rows] if add else sums
        share = dot(items_ref[rows], prob_ref[...], TN)
        qg_ref[...] = (qg_in_ref[...] if n == 0 else qg_ref[...]) + share
    sp_ref[...] = found


def run_grad(items, qt, q, bias, lse, pos, qg, sp, more, scale, base, block):
    cols, width = items.shape
    nq = qt.shape[1]
    return pl.pallas_call(
        functools.partial(grad_kernel, scale, base, block, len(more)),
        in_specs=in_vmem(8 + len(more)),
        out_specs=in_vmem(3),
        out_shape=[
            jax.ShapeDtypeStruct((cols, width), F32),
            jax.ShapeDtypeStruct((width, nq), F32),
            jax.ShapeDtypeStruct((8, nq), F32),
        ],
        scratch_shapes=[pltpu.VMEM((block, nq), F32)] * (cols // block)
        + [pltpu.VMEM((block, nq), BF16)] * (cols // block),
        input_output_aliases={6: 1, 7: 2},
        compiler_params=pltpu.CompilerParams(vmem_limit_bytes=20 << 20),
        cost_estimate=pl.CostEstimate(
            flops=cols * width, bytes_accessed=cols, transcendentals=0
        ),
    )(items, qt, q, bias, lse, pos, qg, sp, *more)


def xor_concat(blocks, index, axis=0):
    if len(blocks) == 1:
        return blocks[0]
    half = len(blocks) // 2
    low = xor_concat(blocks[:half], index, axis)
    high = xor_concat(blocks[half:], index, axis)
    return jnp.where(
        (index & half) == 0,
        jnp.concatenate([low, high], axis=axis),
        jnp.concatenate([high, low], axis=axis),
    )


def per_device(queries, item_table, cand_row, cand_owner, cand_count, positive, w_in, b_in, w_out):
    n_data = lax.axis_size("dp")
    n_model = lax.axis_size("mp")
    n_z = n_data // 4
    me = lax.axis_index("dp")
    my_model = lax.axis_index("mp")
    n_query, width_out = queries.shape
    rows, width_emb = item_table.shape
    units = w_in.shape[1]
    part = rows // n_model
    cand_local = cand_row.shape[0]
    n_cols = n_data * part
    chunk = n_z * part // 2
    scale = 1.0 / math.sqrt(width_out)
    block = min(256, chunk)
    tie = lax.optimization_barrier

    def place(rel):
        return ((rel >> 1) & 1) * (2 * n_z) + (rel & 1) * n_z + (rel >> 2)

    def bit_of(bits):
        return (me // bits) & 1

    pre = dot(item_table, w_in) + b_in[None, :]
    hidden = jnp.maximum(pre, 0.0).astype(BF16)
    partial = dot(hidden, w_out)

    def part_of(value, k):
        return lax.dynamic_slice(value, ((my_model ^ k) * part, 0), (part, value.shape[1]))

    outgoing = [part_of(partial, k) for k in range(1, n_model)]
    outgoing, cand_row, queries = tie((outgoing, cand_row, queries))
    total = part_of(partial, 0)
    for k in range(1, n_model):
        total = total + hop(outgoing[k - 1], k, "mp")
    item_own = total.astype(BF16)

    largest = jnp.max(jnp.abs(queries)).astype(F32)
    exponent = jnp.floor(jnp.log2(jnp.maximum(largest, 1e-6))).astype(jnp.int32) + 1
    exponent = jnp.clip(exponent + EXPONENT_BASE, 0, 63)
    word = (cand_owner[:, 0] * rows + cand_row) * COUNT_BASE + cand_count
    word = (word + exponent * (1 << WORD_BITS))[None, :]
    words = lax.all_to_all(
        jnp.broadcast_to(word, (n_data, cand_local)), "dp", split_axis=0, concat_axis=0, tiled=True
    )

    words, item_own = tie((words, item_own))

    flat = words.reshape(-1)
    n_cand = flat.shape[0]
    q_bound = jnp.exp2((jnp.max(flat >> WORD_BITS) - EXPONENT_BASE).astype(F32))
    flat = flat & ((1 << WORD_BITS) - 1)
    row = (flat // COUNT_BASE) % rows
    column = place((flat // (COUNT_BASE * rows)) ^ me) * part + row % part
    column = jnp.where(row // part == my_model, column, -1)
    share = 1.0 / (flat % COUNT_BASE).astype(F32)
    lanes = 128
    high = (jnp.arange(n_cols // lanes)[:, None] == (column >> 7)[None, :]).astype(F32)
    low = jnp.where(jnp.arange(lanes)[:, None] == (column & 127)[None, :], share[None, :], 0.0)
    weight = dot(low, high, NT, precision=lax.Precision.HIGHEST)
    bias = jnp.where(weight > 0.0, jnp.log2(weight), ABSENT)

    side = 64
    table = flat.reshape(n_cand // side, side)
    digits = jnp.concatenate([table & 255, (table >> 8) & 255, table >> 16], axis=1).astype(BF16)
    picked = (jnp.arange(n_cand // side)[:, None] == (positive // side)[None, :]).astype(BF16)
    found = dot(digits, picked, TN).reshape(3, side, n_query)
    mine = jnp.arange(side)[:, None] == (positive % side)[None, :]
    digit = jnp.sum(jnp.where(mine[None], found, 0.0), axis=1).astype(jnp.int32)
    pos_word = digit[0] + digit[1] * 256 + digit[2] * 65536
    pos_row = (pos_word // COUNT_BASE) % rows
    pos_col = place((pos_word // (COUNT_BASE * rows)) ^ me) * part + pos_row % part
    pos_col = jnp.where(pos_row // part == my_model, pos_col, -1)[None, :]
    pos_logc = jnp.log((pos_word % COUNT_BASE).astype(F32))

    qt = queries.T
    last = n_z - 1
    halves = [range(h * n_z // 2, (h + 1) * n_z // 2) for h in range(2)]
    start_of = {
        (x, c, h): ((x * 2 + c) * 2 + h) * chunk for x in range(2) for c in range(2) for h in range(2)
    }
    items = {}
    m8 = jnp.full((8, n_query), ABSENT, F32)
    l8 = jnp.zeros((8, n_query), F32)

    def gathered(x, h, blocks):
        items[x, 0, h] = jnp.concatenate([blocks[j] for j in halves[h]], axis=0)
        items[x, 1, h] = hop(items[x, 0, h], 1)

    def statistics(m, l, *chosen):
        for key in chosen:
            m, l = run_stats(items[key], qt, bias, m, l, scale * LOG2E, start_of[key], block)
        return m, l

    along_z, along_x = {0: item_own}, {}
    bits = n_z // 2
    while bits:
        along_z.update({j | bits: hop(v, bits << 2) for j, v in list(along_z.items())})
        bits //= 2
    for j in range(last):
        along_x[j] = hop(along_z[j], 2)
    gathered(0, 0, along_z)
    m8, l8 = statistics(m8, l8, (0, 0, 0), (0, 1, 0))
    along_z[last], m8, l8 = tie((along_z[last], m8, l8))
    along_x[last] = hop(along_z[last], 2)
    gathered(0, 1, along_z)
    m8, l8 = statistics(m8, l8, (0, 0, 1), (0, 1, 1))
    gathered(1, 0, along_x)
    m8, l8 = statistics(m8, l8, (1, 0, 0))
    along_x[last], m8, l8 = tie((along_x[last], m8, l8))
    gathered(1, 1, along_x)
    m8, l8 = statistics(m8, l8, (1, 1, 0), (1, 0, 1), (1, 1, 1))
    m1 = jnp.max(m8, axis=0)
    l1 = jnp.sum(l8 * jnp.exp2(m8 - m1[None]), axis=0)
    local = jnp.stack([m1, l1])
    parts = jnp.stack([local] + [hop(local, k, "mp") for k in range(1, n_model)])
    if n_model > 2:
        parts = jnp.take(parts, jnp.arange(n_model) ^ my_model, axis=0)
    row_max = jnp.max(parts[:, 0], axis=0)
    sums = parts[:, 1] * jnp.exp2(parts[:, 0] - row_max[None])
    normal = sums[0]
    for k in range(1, n_model):
        normal = normal + sums[k]
    lse = row_max + jnp.log2(normal)

    core = me & 1
    packed = jnp.concatenate([w_in, w_out.reshape(width_emb, -1)], axis=1)
    half_rows = width_emb // 2
    piece = lax.dynamic_slice(packed, (core * half_rows, 0), (half_rows, packed.shape[1]))
    piece, b_late, lse = tie((piece, b_in[None, :], lse))
    others = [(hop(piece, k, "mp"), hop(b_late, k, "mp")) for k in range(1, n_model)]

    def wire(bound):
        factor = (LIMIT / bound) / q_bound
        return (lambda v: (v * factor).astype(F16)), (lambda v: v.astype(F32) * (1.0 / factor))

    def send(value, bits, bound):
        shrink, grow = wire(bound)
        return grow(hop(shrink(value), bits))

    def item_bound(devices):
        return devices * n_query * 2.0 * scale

    qg = jnp.zeros((width_out, n_query), F32)
    sp = jnp.zeros((8, n_query), F32)
    chip_sums, crossed, z_sums = {}, {}, [None] * n_z
    shrink, grow = wire(item_bound(2))

    def gradients(key, qg, sp, *more):
        return run_grad(
            items[key], qt, queries, bias, lse[None, :], pos_col, qg, sp, more,
            scale, start_of[key], block,
        )

    for x in (1, 0):
        siblings = {}
        for h in (1, 0):
            sums, qg, sp = gradients((x, 1, h), qg, sp)
            siblings[h] = hop(sums, 1)
        for h in (1, 0):
            chip_sums[x, h], qg, sp = gradients((x, 0, h), qg, sp, siblings[h])
            if x == 1:
                crossing, qg = tie((shrink(chip_sums[x, h]), qg))
                crossed[h] = hop(crossing, 2)
        if x == 1:
            others, qg = tie((others, qg))
    for h in (1, 0):
        pair_sum = chip_sums[0, h] + grow(crossed[h])
        for j in range(n_z // 2):
            z_sums[h * n_z // 2 + j] = pair_sum[j * part : (j + 1) * part]
    bits = 1
    while bits < n_z:
        for j in reversed(range(0, n_z, 2 * bits)):
            z_sums[j] = z_sums[j] + send(z_sums[j + bits], bits << 2, item_bound(4 * bits))
        bits *= 2
    own_grad = z_sums[0].astype(BF16)

    hidden_max = width_emb * TABLE_MAX * W_IN_MAX + B_IN_MAX
    item_max = n_model * units * hidden_max * W_OUT_MAX
    q_factor = LIMIT / (2.0 * item_max)
    share = n_query // n_model
    sp1 = jnp.sum(sp, axis=0)[None, :]
    qg_parts = [
        lax.dynamic_slice(qg, (0, (my_model ^ k) * share), (width_out, share))
        for k in range(n_model)
    ]
    pos_score, query_sum = sp1, qg_parts[0]
    for k in range(1, n_model):
        sent = hop((qg_parts[k] * q_factor).astype(F16), k, "mp")
        query_sum = query_sum + sent.astype(F32) * (1.0 / q_factor)
        pos_score = pos_score + hop(sp1, k, "mp")
    loss = lse * (1.0 / LOG2E) - (pos_score[0] * scale - pos_logc)
    query_grad = (query_sum * scale).T
    others = [(xor_concat([got, hop(got, 1)], core), b) for got, b in others]

    item_grad = xor_concat(
        [own_grad] + [hop(own_grad, k, "mp") for k in range(1, n_model)], my_model
    )

    def backward(grad, weights, pre_values):
        return jnp.where(pre_values > 0.0, dot(grad, weights, NT), 0.0).astype(BF16)

    pre_grad = backward(item_grad, w_out, pre)
    local_in = dot(item_table, pre_grad, TN)
    local_out = dot(hidden, item_grad, TN).reshape(width_emb, -1)
    local_b = jnp.sum(pre_grad.astype(F32), axis=0)[None, :]

    gradient_sum = n_data * n_query * 2.0 * scale
    bound_in = gradient_sum * width_out * W_OUT_MAX * TABLE_MAX
    bound_out = gradient_sum * hidden_max
    factor_in, factor_out = (LIMIT / bound_in) / q_bound, (LIMIT / bound_out) / q_bound
    value = jnp.concatenate([local_in * factor_in, local_out * factor_out], axis=1)
    width = value.shape[1]
    keep = lax.dynamic_slice(value, (core * half_rows, 0), (half_rows, width))
    give = lax.dynamic_slice(value, ((1 - core) * half_rows, 0), (half_rows, width))
    bias_steps = [1 << n for n in range(n_data.bit_length() - 1)]

    def step_bias(value, steps):
        for _ in range(min(steps, len(bias_steps))):
            bits = bias_steps.pop(0)
            value = value + hop(value, bits)
        return value

    value = keep + hop(give.astype(F16), 1).astype(F32)
    value, local_b = tie((value, step_bias(local_b, 1)))
    chips = n_data // 2
    groups = [[2 * chip + c for chip in range(chips)] for c in range(2)]

    def exchange(blocks):
        return lax.all_to_all(
            blocks, "dp", split_axis=0, concat_axis=0, axis_index_groups=groups, tiled=True
        )

    size = half_rows // chips
    pieces = exchange(value.astype(F16).reshape(chips, size, width))
    total = jnp.sum(pieces.astype(F32), axis=0).astype(F16)
    total, local_b = tie((total, step_bias(local_b, 1)))
    own_half = exchange(jnp.broadcast_to(total[None], (chips, size, width)))
    own_half, local_b = tie((own_half.reshape(half_rows, width), step_bias(local_b, 1)))
    value = xor_concat([own_half, hop(own_half, 1)], core)
    grad_w_in = value[:, :units].astype(F32) * (1.0 / factor_in)
    grad_w_out = (value[:, units:].astype(F32) * (1.0 / factor_out)).reshape(units, width_out)
    local_b = step_bias(local_b, len(bias_steps))

    weights = [(packed, b_in[None, :])] + others
    if n_model > 2:
        turn = jnp.arange(n_model) ^ my_model
        stacks = [jnp.take(jnp.stack(group), turn, axis=0) for group in zip(*weights)]
        weights = [(stacks[0][k], stacks[1][k]) for k in range(n_model)]
    grad_table = None
    for pack, bias_units in weights:
        share_in, share_out = pack[:, :units], pack[:, units:].reshape(units, width_out)
        pre_units = dot(item_table, share_in) + bias_units
        term = dot(backward(item_grad, share_out, pre_units), share_in, NT)
        grad_table = term if grad_table is None else grad_table + term
    return (loss, query_grad, grad_w_in, local_b[0], grad_w_out, grad_table)


def solution(mesh):
    placed = (
        P("dp", None),
        P("dp", None),
        P("dp"),
        P("dp", None),
        P("dp"),
        P("dp"),
        P(None, "mp"),
        P("mp"),
        P("mp", None),
    )
    return jax.shard_map(
        per_device,
        mesh=mesh,
        in_specs=placed,
        out_specs=(
            P("dp"),
            P(("dp", "mp"), None),
            P(None, "mp"),
            P("mp"),
            P("mp", None),
            P("dp", None),
        ),
        check_vma=False,
    )
```

```python
import functools
import math

import jax
import jax.numpy as jnp
from jax import lax
from jax.experimental import pallas as pl
from jax.experimental.pallas import tpu as pltpu
from jax.sharding import PartitionSpec as P

F32 = jnp.float32
BF16 = jnp.bfloat16
F16 = jnp.float16
ABSENT = -1e30
COUNT_BASE = 128
WORD_BITS = 22
EXPONENT_BASE = 20
TABLE_MAX = 6.0
W_IN_MAX = 0.25
B_IN_MAX = 3.0
W_OUT_MAX = 0.1875
LIMIT = 32768.0
LOG2E = math.log2(math.e)
GROUP = 16
NT = (((1,), (1,)), ((), ()))
TN = (((0,), (0,)), ((), ()))


def hop(value, bits, axis="dp"):
    size = lax.axis_size(axis)
    return lax.ppermute(value, axis, [(i, i ^ bits) for i in range(size)])


def dot(a, b, dims=None, **kw):
    if dims is None:
        dims = (((1,), (0,)), ((), ()))
    return lax.dot_general(a, b, dims, preferred_element_type=F32, **kw)


def column_bias(bias_ref, first, count):
    lane = first // 128
    return bias_ref[pl.ds(first % 128, count), lane : lane + 1]


def stats_kernel(scale, base, block, items_ref, qt_ref, bias_ref, m_in_ref, l_in_ref, m_ref, l_ref, *score_refs):
    cols = items_ref.shape[0]
    old = m_in_ref[...]
    new = old
    for n, score_ref in enumerate(score_refs):
        score_ref[...] = dot(items_ref[n * block : (n + 1) * block], qt_ref[...])
    for n, score_ref in enumerate(score_refs):
        for r in range(0, block, 8):
            bias = column_bias(bias_ref, base + n * block + r, 8)
            score = score_ref[r : r + 8] * scale + bias
            score_ref[r : r + 8] = score
            new = jnp.maximum(new, score)
    total = l_in_ref[...] * jnp.exp2(old - new)
    for n, score_ref in enumerate(score_refs):
        for r in range(0, block, 8):
            total = total + jnp.exp2(score_ref[r : r + 8] - new)
    m_ref[...] = new
    l_ref[...] = total


def in_vmem(count):
    return [pl.BlockSpec(memory_space=pltpu.VMEM)] * count


def run_stats(items, qt, bias, m, l, scale, base, block):
    cols, width = items.shape
    nq = qt.shape[1]
    return pl.pallas_call(
        functools.partial(stats_kernel, scale, base, block),
        in_specs=in_vmem(5),
        out_specs=in_vmem(2),
        out_shape=[jax.ShapeDtypeStruct((8, nq), F32)] * 2,
        scratch_shapes=[pltpu.VMEM((block, nq), F32)] * (cols // block),
        compiler_params=pltpu.CompilerParams(vmem_limit_bytes=6 << 20),
        cost_estimate=pl.CostEstimate(
            flops=cols * width, bytes_accessed=cols, transcendentals=0
        ),
    )(items, qt, bias, m, l)


def grad_kernel(
    scale, base, block, add, items_ref, qt_ref, q_ref, bias_ref, lse_ref, pos_ref, qg_in_ref, sp_in_ref,
    *refs,
):
    more_ref = refs[0] if add else None
    ig_ref, qg_ref, sp_ref, *scratch = refs[add:]
    count = items_ref.shape[0] // block
    score_refs, prob_refs = scratch[:count], scratch[count:]
    queries = qt_ref.shape[1]
    for n, score_ref in enumerate(score_refs):
        score_ref[...] = dot(items_ref[n * block : (n + 1) * block], qt_ref[...])
    down = lax.broadcasted_iota(jnp.int32, (8, queries), 0)
    offset = jnp.broadcast_to(pos_ref[...], (8, queries)) - down
    lse = jnp.broadcast_to(lse_ref[...], (8, queries))
    found = sp_in_ref[...]
    for n in range(count):
        score_ref, prob_ref = score_refs[n], prob_refs[n]
        for r in range(0, block, GROUP):
            pieces = []
            for s in range(r, r + GROUP, 8):
                at = base + n * block + s
                score = score_ref[s : s + 8]
                here = offset == at
                found = found + jnp.where(here, score, 0.0)
                prob = jnp.exp2((score * (scale * LOG2E) + column_bias(bias_ref, at, 8)) - lse)
                pieces.append(jnp.where(here, prob - 1.0, prob))
            prob_ref[r : r + GROUP] = jnp.concatenate(pieces, axis=0).astype(BF16)
        rows = slice(n * block, (n + 1) * block)
        sums = dot(prob_ref[...], q_ref[...]) * scale
        ig_ref[rows] = sums + more_ref[rows] if add else sums
        share = dot(items_ref[rows], prob_ref[...], TN)
        qg_ref[...] = (qg_in_ref[...] if n == 0 else qg_ref[...]) + share
    sp_ref[...] = found


def run_grad(items, qt, q, bias, lse, pos, qg, sp, more, scale, base, block):
    cols, width = items.shape
    nq = qt.shape[1]
    return pl.pallas_call(
        functools.partial(grad_kernel, scale, base, block, len(more)),
        in_specs=in_vmem(8 + len(more)),
        out_specs=in_vmem(3),
        out_shape=[
            jax.ShapeDtypeStruct((cols, width), F32),
            jax.ShapeDtypeStruct((width, nq), F32),
            jax.ShapeDtypeStruct((8, nq), F32),
        ],
        scratch_shapes=[pltpu.VMEM((block, nq), F32)] * (cols // block)
        + [pltpu.VMEM((block, nq), BF16)] * (cols // block),
        input_output_aliases={6: 1, 7: 2},
        compiler_params=pltpu.CompilerParams(vmem_limit_bytes=8 << 20),
        cost_estimate=pl.CostEstimate(
            flops=cols * width, bytes_accessed=cols, transcendentals=0
        ),
    )(items, qt, q, bias, lse, pos, qg, sp, *more)


def backward_kernel(count, index_ref, factor_ref, *refs):
    grad_refs, (pre_ref, hidden_ref, emb_ref, w_out_ref) = refs[:count], refs[count : count + 4]
    grad_ref, pre_grad_ref, in_ref, out_ref, b_ref = refs[count + 4 :]
    part = grad_refs[0].shape[0]
    for k in range(count):
        start = pl.multiple_of((index_ref[0] ^ k) * part, part)
        grad_ref[pl.ds(start, part)] = grad_refs[k][...]
    back = dot(grad_ref[...], w_out_ref[...], NT)
    pre_grad = jnp.where(pre_ref[...] > 0.0, back, 0.0).astype(BF16)
    pre_grad_ref[...] = pre_grad
    b_ref[...] = jnp.sum(pre_grad.astype(F32), axis=0, keepdims=True)
    in_ref[...] = dot(emb_ref[...], pre_grad, TN) * factor_ref[0]
    out_ref[...] = dot(hidden_ref[...], grad_ref[...], TN) * factor_ref[1]


def run_backward(index, factors, grads, pre, hidden, emb, w_out):
    rows, units = pre.shape
    width_emb, width_out = emb.shape[1], w_out.shape[1]
    return pl.pallas_call(
        functools.partial(backward_kernel, len(grads)),
        in_specs=[pl.BlockSpec(memory_space=pltpu.SMEM)] * 2 + in_vmem(len(grads) + 4),
        out_specs=in_vmem(5),
        out_shape=[
            jax.ShapeDtypeStruct((rows, width_out), BF16),
            jax.ShapeDtypeStruct((rows, units), BF16),
            jax.ShapeDtypeStruct((width_emb, units), F32),
            jax.ShapeDtypeStruct((units, width_out), F32),
            jax.ShapeDtypeStruct((1, units), F32),
        ],
        compiler_params=pltpu.CompilerParams(vmem_limit_bytes=12 << 20),
    )(index, factors, *grads, pre, hidden, emb, w_out)


def xor_concat(blocks, index, axis=0):
    if len(blocks) == 1:
        return blocks[0]
    half = len(blocks) // 2
    low = xor_concat(blocks[:half], index, axis)
    high = xor_concat(blocks[half:], index, axis)
    return jnp.where(
        (index & half) == 0,
        jnp.concatenate([low, high], axis=axis),
        jnp.concatenate([high, low], axis=axis),
    )


def per_device(queries, item_table, cand_row, cand_owner, cand_count, positive, w_in, b_in, w_out):
    n_data = lax.axis_size("dp")
    n_model = lax.axis_size("mp")
    n_z = n_data // 4
    me = lax.axis_index("dp")
    my_model = lax.axis_index("mp")
    n_query, width_out = queries.shape
    rows, width_emb = item_table.shape
    units = w_in.shape[1]
    part = rows // n_model
    cand_local = cand_row.shape[0]
    n_cols = n_data * part
    chunk = n_z * part // 2
    scale = 1.0 / math.sqrt(width_out)
    block = min(256, chunk)
    tie = lax.optimization_barrier

    def place(rel):
        return ((rel >> 1) & 1) * (2 * n_z) + (rel & 1) * n_z + (rel >> 2)

    def bit_of(bits):
        return (me // bits) & 1

    pre = dot(item_table, w_in) + b_in[None, :]
    hidden = jnp.maximum(pre, 0.0).astype(BF16)
    partial = dot(hidden, w_out)

    def part_of(value, k):
        return lax.dynamic_slice(value, ((my_model ^ k) * part, 0), (part, value.shape[1]))

    outgoing = [part_of(partial, k) for k in range(1, n_model)]
    arrived = [hop(outgoing[k - 1], k, "mp") for k in range(1, n_model)]
    qt = queries.T
    core = me & 1
    packed = jnp.concatenate([w_in, w_out.reshape(width_emb, -1)], axis=1)
    half_rows = width_emb // 2
    piece = lax.dynamic_slice(packed, (core * half_rows, 0), (half_rows, packed.shape[1]))
    largest = jnp.max(jnp.abs(queries)).astype(F32)
    total, arrived, qt, piece, largest = tie((part_of(partial, 0), arrived, qt, piece, largest))
    for other in arrived:
        total = total + other
    item_own = total.astype(BF16)
    along_z, along_x = {0: item_own}, {}
    for j in range(1, n_z):
        along_z[j] = hop(item_own, j << 2)
    along_z[1], cand_row = tie((along_z[1], cand_row))

    exponent = jnp.floor(jnp.log2(jnp.maximum(largest, 1e-6))).astype(jnp.int32) + 1
    exponent = jnp.clip(exponent + EXPONENT_BASE, 0, 63)
    word = (cand_owner[:, 0] * rows + cand_row) * COUNT_BASE + cand_count
    word = (word + exponent * (1 << WORD_BITS))[None, :]
    words = lax.all_to_all(
        jnp.broadcast_to(word, (n_data, cand_local)), "dp", split_axis=0, concat_axis=0, tiled=True
    )


    flat = words.reshape(-1)
    n_cand = flat.shape[0]
    q_bound = jnp.exp2((jnp.max(flat >> WORD_BITS) - EXPONENT_BASE).astype(F32))
    flat = flat & ((1 << WORD_BITS) - 1)
    row = (flat // COUNT_BASE) % rows
    column = place((flat // (COUNT_BASE * rows)) ^ me) * part + row % part
    column = jnp.where(row // part == my_model, column, -1)
    share = 1.0 / (flat % COUNT_BASE).astype(F32)
    lanes = 128
    high = (jnp.arange(n_cols // lanes)[:, None] == (column >> 7)[None, :]).astype(F32)
    low = jnp.where(jnp.arange(lanes)[:, None] == (column & 127)[None, :], share[None, :], 0.0)
    weight = dot(low, high, NT, precision=lax.Precision.HIGHEST)
    bias = jnp.where(weight > 0.0, jnp.log2(weight), ABSENT)

    side = 64
    table = flat.reshape(n_cand // side, side)
    digits = jnp.concatenate([table & 255, (table >> 8) & 255, table >> 16], axis=1).astype(BF16)
    picked = (jnp.arange(n_cand // side)[:, None] == (positive // side)[None, :]).astype(BF16)
    found = dot(digits, picked, TN).reshape(3, side, n_query)
    mine = jnp.arange(side)[:, None] == (positive % side)[None, :]
    digit = jnp.sum(jnp.where(mine[None], found, 0.0), axis=1).astype(jnp.int32)
    pos_word = digit[0] + digit[1] * 256 + digit[2] * 65536
    pos_row = (pos_word // COUNT_BASE) % rows
    pos_col = place((pos_word // (COUNT_BASE * rows)) ^ me) * part + pos_row % part
    pos_col = jnp.where(pos_row // part == my_model, pos_col, -1)[None, :]
    pos_logc = jnp.log((pos_word % COUNT_BASE).astype(F32))

    last = n_z - 1
    halves = [range(h * n_z // 2, (h + 1) * n_z // 2) for h in range(2)]
    start_of = {
        (x, c, h): ((x * 2 + c) * 2 + h) * chunk for x in range(2) for c in range(2) for h in range(2)
    }
    items = {}
    m8 = jnp.full((8, n_query), ABSENT, F32)
    l8 = jnp.zeros((8, n_query), F32)

    def gathered(x, h, blocks):
        items[x, 0, h] = jnp.concatenate([blocks[j] for j in halves[h]], axis=0)
        items[x, 1, h] = hop(items[x, 0, h], 1)

    def statistics(m, l, *chosen):
        for key in chosen:
            m, l = run_stats(items[key], qt, bias, m, l, scale * LOG2E, start_of[key], block)
        return m, l

    for j in range(last):
        along_x[j] = hop(along_z[j], 2)
    gathered(0, 0, along_z)
    m8, l8 = statistics(m8, l8, (0, 0, 0), (0, 1, 0))
    along_z[last], m8, l8 = tie((along_z[last], m8, l8))
    along_x[last] = hop(along_z[last], 2)
    gathered(0, 1, along_z)
    m8, l8 = statistics(m8, l8, (0, 0, 1), (0, 1, 1))
    gathered(1, 0, along_x)
    m8, l8 = statistics(m8, l8, (1, 0, 0))
    along_x[last], m8, l8 = tie((along_x[last], m8, l8))
    gathered(1, 1, along_x)
    m8, l8 = statistics(m8, l8, (1, 1, 0), (1, 0, 1), (1, 1, 1))
    m1 = jnp.max(m8, axis=0)
    l1 = jnp.sum(l8 * jnp.exp2(m8 - m1[None]), axis=0)
    local = jnp.stack([m1, l1])
    parts = jnp.stack([local] + [hop(local, k, "mp") for k in range(1, n_model)])
    if n_model > 2:
        parts = jnp.take(parts, jnp.arange(n_model) ^ my_model, axis=0)
    row_max = jnp.max(parts[:, 0], axis=0)
    sums = parts[:, 1] * jnp.exp2(parts[:, 0] - row_max[None])
    normal = sums[0]
    for k in range(1, n_model):
        normal = normal + sums[k]
    lse = row_max + jnp.log2(normal)

    piece, b_late, lse = tie((piece, b_in[None, :], lse))
    others = [(hop(piece, k, "mp"), hop(b_late, k, "mp")) for k in range(1, n_model)]

    def wire(bound):
        factor = (LIMIT / bound) / q_bound
        return (lambda v: (v * factor).astype(F16)), (lambda v: v.astype(F32) * (1.0 / factor))

    def send(value, bits, bound):
        shrink, grow = wire(bound)
        return grow(hop(shrink(value), bits))

    def item_bound(devices):
        return devices * n_query * 2.0 * scale

    qg = jnp.zeros((width_out, n_query), F32)
    sp = jnp.zeros((8, n_query), F32)
    chip_sums, crossed, z_sums = {}, {}, [None] * n_z
    shrink, grow = wire(item_bound(2))

    def gradients(key, qg, sp, *more):
        return run_grad(
            items[key], qt, queries, bias, lse[None, :], pos_col, qg, sp, more,
            scale, start_of[key], block,
        )

    siblings, crossing = {}, {}
    for h in (1, 0):
        sums, qg, sp = gradients((1, 1, h), qg, sp)
        siblings[1, h] = hop(sums, 1)
    for h in (1, 0):
        chip_sums[1, h], qg, sp = gradients((1, 0, h), qg, sp, siblings[1, h])
        crossing[h], qg = tie((shrink(chip_sums[1, h]), qg))
        crossed[h] = hop(crossing[h], 2)
    for h in (1, 0):
        sums, qg, sp = gradients((0, 1, h), qg, sp)
        siblings[0, h] = hop(sums, 1)
    for h in (1, 0):
        crossed[h], qg = tie((crossed[h], qg))
        chip_sums[0, h], qg, sp = gradients((0, 0, h), qg, sp, siblings[0, h])
        pair_sum = chip_sums[0, h] + grow(crossed[h])
        for j in range(n_z // 2):
            z_sums[h * n_z // 2 + j] = pair_sum[j * part : (j + 1) * part]
    own_sum = z_sums[0]
    for j in range(n_z - 1, 0, -1):
        own_sum = own_sum + send(z_sums[j], j << 2, item_bound(4))
    own_grad, others = tie((own_sum.astype(BF16), others))

    hidden_max = width_emb * TABLE_MAX * W_IN_MAX + B_IN_MAX
    item_max = n_model * units * hidden_max * W_OUT_MAX
    q_factor = LIMIT / (2.0 * item_max)
    share = n_query // n_model
    sp1 = jnp.sum(sp, axis=0)[None, :]
    qg_parts = [
        lax.dynamic_slice(qg, (0, (my_model ^ k) * share), (width_out, share))
        for k in range(n_model)
    ]
    pos_score, query_sum = sp1, qg_parts[0]
    for k in range(1, n_model):
        sent = hop((qg_parts[k] * q_factor).astype(F16), k, "mp")
        query_sum = query_sum + sent.astype(F32) * (1.0 / q_factor)
        pos_score = pos_score + hop(sp1, k, "mp")
    loss = lse * (1.0 / LOG2E) - (pos_score[0] * scale - pos_logc)
    query_grad = (query_sum * scale).T
    others = [(xor_concat([got, hop(got, 1)], core), b) for got, b in others]

    gradient_sum = n_data * n_query * 2.0 * scale
    bound_in = gradient_sum * width_out * W_OUT_MAX * TABLE_MAX
    bound_out = gradient_sum * hidden_max
    factor_in, factor_out = (LIMIT / bound_in) / q_bound, (LIMIT / bound_out) / q_bound
    grads = [own_grad] + [hop(own_grad, k, "mp") for k in range(1, n_model)]
    item_grad, pre_grad, local_in, local_out, local_b = run_backward(
        my_model.astype(jnp.int32).reshape(1), jnp.stack([factor_in, factor_out]), grads, pre, hidden, item_table, w_out
    )
    local_out = local_out.reshape(width_emb, -1)

    value = jnp.concatenate([local_in, local_out], axis=1)
    width = value.shape[1]
    keep = lax.dynamic_slice(value, (core * half_rows, 0), (half_rows, width))
    give = lax.dynamic_slice(value, ((1 - core) * half_rows, 0), (half_rows, width))
    bias_steps = [1 << n for n in range(n_data.bit_length() - 1)]

    def step_bias(value, steps):
        for _ in range(min(steps, len(bias_steps))):
            bits = bias_steps.pop(0)
            value = value + hop(value, bits)
        return value

    value = keep + hop(give.astype(F16), 1).astype(F32)
    value, local_b = tie((value, step_bias(local_b, 1)))
    chips = n_data // 2
    groups = [[2 * chip + c for chip in range(chips)] for c in range(2)]

    def exchange(blocks):
        return lax.all_to_all(
            blocks, "dp", split_axis=0, concat_axis=0, axis_index_groups=groups, tiled=True
        )

    size = half_rows // chips
    pieces = exchange(value.astype(F16).reshape(chips, size, width))
    total = jnp.sum(pieces.astype(F32), axis=0).astype(F16)
    total, local_b = tie((total, step_bias(local_b, 2)))
    own_half = exchange(jnp.broadcast_to(total[None], (chips, size, width)))
    own_half, local_b = tie((own_half.reshape(half_rows, width), step_bias(local_b, 9)))
    weights = [(packed, b_in[None, :])] + others
    if n_model > 2:
        turn = jnp.arange(n_model) ^ my_model
        stacks = [jnp.take(jnp.stack(group), turn, axis=0) for group in zip(*weights)]
        weights = [(stacks[0][k], stacks[1][k]) for k in range(n_model)]
    def backward(grad, weight, pre_values):
        return jnp.where(pre_values > 0.0, dot(grad, weight, NT), 0.0).astype(BF16)

    grad_table = None
    for pack, bias_units in weights:
        share_in, share_out = pack[:, :units], pack[:, units:].reshape(units, width_out)
        pre_units = dot(item_table, share_in) + bias_units
        term = dot(backward(item_grad, share_out, pre_units), share_in, NT)
        grad_table = term if grad_table is None else grad_table + term
    own_half, grad_table = tie((own_half, grad_table))
    sides = [own_half, hop(own_half, 1)]
    sides_in = [v[:, :units].astype(F32) * (1.0 / factor_in) for v in sides]
    sides_out = [v[:, units:].astype(F32) * (1.0 / factor_out) for v in sides]
    grad_w_in = xor_concat(sides_in, core)
    grad_w_out = xor_concat(sides_out, core).reshape(units, width_out)
    return (loss, query_grad, grad_w_in, local_b[0], grad_w_out, grad_table)


def solution(mesh):
    placed = (
        P("dp", None),
        P("dp", None),
        P("dp"),
        P("dp", None),
        P("dp"),
        P("dp"),
        P(None, "mp"),
        P("mp"),
        P("mp", None),
    )
    return jax.shard_map(
        per_device,
        mesh=mesh,
        in_specs=placed,
        out_specs=(
            P("dp"),
            P(("dp", "mp"), None),
            P(None, "mp"),
            P("mp"),
            P("mp", None),
            P("dp", None),
        ),
        check_vma=False,
    )
```

```python
import functools
import math

import jax
import jax.numpy as jnp
from jax import lax
from jax.experimental import pallas as pl
from jax.experimental.pallas import tpu as pltpu
from jax.sharding import PartitionSpec as P

F32 = jnp.float32
BF16 = jnp.bfloat16
F16 = jnp.float16
ABSENT = -1e30
COUNT_BASE = 128
WORD_BITS = 22
EXPONENT_BASE = 20
TABLE_MAX = 6.0
W_IN_MAX = 0.25
B_IN_MAX = 3.0
W_OUT_MAX = 0.1875
LIMIT = 32768.0
LOG2E = math.log2(math.e)
GROUP = 16
NT = (((1,), (1,)), ((), ()))
TN = (((0,), (0,)), ((), ()))


def hop(value, bits, axis="dp"):
    size = lax.axis_size(axis)
    return lax.ppermute(value, axis, [(i, i ^ bits) for i in range(size)])


def dot(a, b, dims=None, **kw):
    if dims is None:
        dims = (((1,), (0,)), ((), ()))
    return lax.dot_general(a, b, dims, preferred_element_type=F32, **kw)


def column_bias(bias_ref, first, count):
    lane = first // 128
    return bias_ref[pl.ds(first % 128, count), lane : lane + 1]


def stats_kernel(scale, base, count, *refs):
    items_refs, refs = refs[:count], refs[count:]
    qt_ref, bias_ref, m_in_ref, l_in_ref, m_ref, l_ref, *score_refs = refs
    block = items_refs[0].shape[0]
    old = m_in_ref[...]
    new = old
    for items_ref, score_ref in zip(items_refs, score_refs):
        score_ref[...] = dot(items_ref[...], qt_ref[...])
    for n, score_ref in enumerate(score_refs):
        for r in range(0, block, 8):
            bias = column_bias(bias_ref, base + n * block + r, 8)
            score = score_ref[r : r + 8] * scale + bias
            score_ref[r : r + 8] = score
            new = jnp.maximum(new, score)
    total = l_in_ref[...] * jnp.exp2(old - new)
    for score_ref in score_refs:
        for r in range(0, block, 8):
            total = total + jnp.exp2(score_ref[r : r + 8] - new)
    m_ref[...] = new
    l_ref[...] = total


def in_vmem(count):
    return [pl.BlockSpec(memory_space=pltpu.VMEM)] * count


def run_stats(items, qt, bias, m, l, scale, base):
    count, (block, width), nq = len(items), items[0].shape, qt.shape[1]
    return pl.pallas_call(
        functools.partial(stats_kernel, scale, base, count),
        in_specs=in_vmem(count + 4),
        out_specs=in_vmem(2),
        out_shape=[jax.ShapeDtypeStruct((8, nq), F32)] * 2,
        scratch_shapes=[pltpu.VMEM((block, nq), F32)] * count,
        compiler_params=pltpu.CompilerParams(vmem_limit_bytes=6 << 20),
    )(*items, qt, bias, m, l)


def grad_kernel(scale, base, count, add, *refs):
    items_refs, refs = refs[:count], refs[count:]
    more_refs, refs = refs[:add], refs[add:]
    qt_ref, q_ref, bias_ref, lse_ref, pos_ref, qg_in_ref, sp_in_ref, *refs = refs
    sums_refs, (qg_ref, sp_ref, *scratch) = refs[:count], refs[count:]
    score_refs, prob_refs = scratch[:count], scratch[count:]
    block, queries = items_refs[0].shape[0], qt_ref.shape[1]
    for items_ref, score_ref in zip(items_refs, score_refs):
        score_ref[...] = dot(items_ref[...], qt_ref[...])
    down = lax.broadcasted_iota(jnp.int32, (8, queries), 0)
    offset = jnp.broadcast_to(pos_ref[...], (8, queries)) - down
    lse = jnp.broadcast_to(lse_ref[...], (8, queries))
    found = sp_in_ref[...]
    for n in range(count):
        score_ref, prob_ref = score_refs[n], prob_refs[n]
        for r in range(0, block, GROUP):
            pieces = []
            for s in range(r, r + GROUP, 8):
                at = base + n * block + s
                score = score_ref[s : s + 8]
                here = offset == at
                found = found + jnp.where(here, score, 0.0)
                prob = jnp.exp2((score * (scale * LOG2E) + column_bias(bias_ref, at, 8)) - lse)
                pieces.append(jnp.where(here, prob - 1.0, prob))
            prob_ref[r : r + GROUP] = jnp.concatenate(pieces, axis=0).astype(BF16)
        sums = dot(prob_ref[...], q_ref[...]) * scale
        sums_refs[n][...] = sums + more_refs[n][...] if add else sums
        share = dot(items_refs[n][...], prob_ref[...], TN)
        qg_ref[...] = (qg_in_ref[...] if n == 0 else qg_ref[...]) + share
    sp_ref[...] = found


def run_grad(items, more, qt, q, bias, lse, pos, qg, sp, scale, base):
    count, (block, width), nq = len(items), items[0].shape, qt.shape[1]
    before = count + len(more)
    *sums, qg, sp = pl.pallas_call(
        functools.partial(grad_kernel, scale, base, count, len(more)),
        in_specs=in_vmem(before + 7),
        out_specs=in_vmem(count + 2),
        out_shape=[jax.ShapeDtypeStruct((block, width), F32)] * count
        + [jax.ShapeDtypeStruct((width, nq), F32), jax.ShapeDtypeStruct((8, nq), F32)],
        scratch_shapes=[pltpu.VMEM((block, nq), F32)] * count
        + [pltpu.VMEM((block, nq), BF16)] * count,
        input_output_aliases={before + 5: count, before + 6: count + 1},
        compiler_params=pltpu.CompilerParams(vmem_limit_bytes=8 << 20),
    )(*items, *more, qt, q, bias, lse, pos, qg, sp)
    return sums, qg, sp


def backward_kernel(count, index_ref, factor_ref, *refs):
    grad_refs, (pre_ref, hidden_ref, emb_ref, w_out_ref) = refs[:count], refs[count : count + 4]
    grad_ref, pre_grad_ref, b_ref, *sums_refs = refs[count + 4 :]
    part = grad_refs[0].shape[0]
    for k in range(count):
        start = pl.multiple_of((index_ref[0] ^ k) * part, part)
        grad_ref[pl.ds(start, part)] = grad_refs[k][...]
    back = dot(grad_ref[...], w_out_ref[...], NT)
    pre_grad = jnp.where(pre_ref[...] > 0.0, back, 0.0).astype(BF16)
    pre_grad_ref[...] = pre_grad
    b_ref[...] = jnp.sum(pre_grad.astype(F32), axis=0, keepdims=True)
    sums_in = dot(emb_ref[...], pre_grad, TN) * factor_ref[0]
    sums_out = dot(hidden_ref[...], grad_ref[...], TN) * factor_ref[1]
    if len(sums_refs) == 1:
        units = sums_in.shape[1]
        sums_refs[0][:, :units] = sums_in
        sums_refs[0][:, units:] = sums_out
    else:
        sums_refs[0][...] = sums_in
        sums_refs[1][...] = sums_out


def run_backward(index, factors, grads, pre, hidden, emb, w_out):
    rows, units = pre.shape
    width_emb, width_out = emb.shape[1], w_out.shape[1]
    if units == width_emb:
        sums = [(width_emb, units + width_out)]
    else:
        sums = [(width_emb, units), (units, width_out)]
    grad, pre_grad, local_b, *sums = pl.pallas_call(
        functools.partial(backward_kernel, len(grads)),
        in_specs=[pl.BlockSpec(memory_space=pltpu.SMEM)] * 2 + in_vmem(len(grads) + 4),
        out_specs=in_vmem(3 + len(sums)),
        out_shape=[
            jax.ShapeDtypeStruct((rows, width_out), BF16),
            jax.ShapeDtypeStruct((rows, units), BF16),
            jax.ShapeDtypeStruct((1, units), F32),
        ]
        + [jax.ShapeDtypeStruct(shape, F32) for shape in sums],
        compiler_params=pltpu.CompilerParams(vmem_limit_bytes=12 << 20),
    )(index, factors, *grads, pre, hidden, emb, w_out)
    if len(sums) > 1:
        sums = [jnp.concatenate([sums[0], sums[1].reshape(width_emb, -1)], axis=1)]
    return grad, pre_grad, local_b, sums[0]


def xor_concat(blocks, index, axis=0):
    if len(blocks) == 1:
        return blocks[0]
    half = len(blocks) // 2
    low = xor_concat(blocks[:half], index, axis)
    high = xor_concat(blocks[half:], index, axis)
    return jnp.where(
        (index & half) == 0,
        jnp.concatenate([low, high], axis=axis),
        jnp.concatenate([high, low], axis=axis),
    )


def per_device(queries, item_table, cand_row, cand_owner, cand_count, positive, w_in, b_in, w_out):
    n_data = lax.axis_size("dp")
    n_model = lax.axis_size("mp")
    n_z = n_data // 4
    me = lax.axis_index("dp")
    my_model = lax.axis_index("mp")
    n_query, width_out = queries.shape
    rows, width_emb = item_table.shape
    units = w_in.shape[1]
    part = rows // n_model
    cand_local = cand_row.shape[0]
    n_cols = n_data * part
    chunk = n_z * part // 2
    scale = 1.0 / math.sqrt(width_out)
    tie = lax.optimization_barrier

    def place(rel):
        return ((rel >> 1) & 1) * (2 * n_z) + (rel & 1) * n_z + (rel >> 2)

    def bit_of(bits):
        return (me // bits) & 1

    pre = dot(item_table, w_in) + b_in[None, :]
    hidden = jnp.maximum(pre, 0.0).astype(BF16)
    partial = dot(hidden, w_out)

    def part_of(value, k):
        return lax.dynamic_slice(value, ((my_model ^ k) * part, 0), (part, value.shape[1]))

    outgoing = [part_of(partial, k) for k in range(1, n_model)]
    arrived = [hop(outgoing[k - 1], k, "mp") for k in range(1, n_model)]
    outgoing, queries = tie((outgoing, queries))
    qt, cand_row = tie((queries.T, cand_row))
    core = me & 1
    packed = jnp.concatenate([w_in, w_out.reshape(width_emb, -1)], axis=1)
    half_rows = width_emb // 2
    piece = lax.dynamic_slice(packed, (core * half_rows, 0), (half_rows, packed.shape[1]))

    largest = jnp.max(jnp.abs(queries)).astype(F32)
    exponent = jnp.floor(jnp.log2(jnp.maximum(largest, 1e-6))).astype(jnp.int32) + 1
    exponent = jnp.clip(exponent + EXPONENT_BASE, 0, 63)
    word = (cand_owner[:, 0] * rows + cand_row) * COUNT_BASE + cand_count
    word = (word + exponent * (1 << WORD_BITS))[None, :]
    words = jnp.concatenate([word] + [hop(word, k << 2) for k in range(1, n_z)], axis=0)

    total, arrived, qt, piece, words = tie((part_of(partial, 0), arrived, qt, piece, words))
    for other in arrived:
        total = total + other
    item_own = total.astype(BF16)
    along_z, along_x = {0: item_own}, {}
    for j in range(n_z - 1, 0, -1):
        along_z[j] = hop(item_own, j << 2)
    words = jnp.concatenate([words, hop(words, 2)], axis=0)
    along_z[1], words = tie((along_z[1], words))
    far = hop(words, 1)
    words = jnp.concatenate([words[:n_z], far[:n_z], words[n_z:], far[n_z:]], axis=0)

    flat = words.reshape(-1)
    n_cand = flat.shape[0]
    q_bound = jnp.exp2((jnp.max(flat >> WORD_BITS) - EXPONENT_BASE).astype(F32))
    flat = flat & ((1 << WORD_BITS) - 1)
    row = (flat // COUNT_BASE) % rows
    column = place((flat // (COUNT_BASE * rows)) ^ me) * part + row % part
    column = jnp.where(row // part == my_model, column, -1)
    share = 1.0 / (flat % COUNT_BASE).astype(F32)
    lanes = 128
    high = (jnp.arange(n_cols // lanes)[:, None] == (column >> 7)[None, :]).astype(F32)
    low = jnp.where(jnp.arange(lanes)[:, None] == (column & 127)[None, :], share[None, :], 0.0)
    weight = dot(low, high, NT, precision=lax.Precision.HIGHEST)
    bias = jnp.where(weight > 0.0, jnp.log2(weight), ABSENT)

    spot = place((positive // cand_local) ^ me) * cand_local + positive % cand_local
    side = 64
    table = flat.reshape(n_cand // side, side)
    digits = jnp.concatenate([table & 255, (table >> 8) & 255, table >> 16], axis=1).astype(BF16)
    picked = (jnp.arange(n_cand // side)[:, None] == (spot // side)[None, :]).astype(BF16)
    found = dot(digits, picked, TN).reshape(3, side, n_query)
    mine = jnp.arange(side)[:, None] == (spot % side)[None, :]
    digit = jnp.sum(jnp.where(mine[None], found, 0.0), axis=1).astype(jnp.int32)
    pos_word = digit[0] + digit[1] * 256 + digit[2] * 65536
    pos_row = (pos_word // COUNT_BASE) % rows
    pos_col = place((pos_word // (COUNT_BASE * rows)) ^ me) * part + pos_row % part
    pos_col = jnp.where(pos_row // part == my_model, pos_col, -1)[None, :]
    pos_logc = jnp.log((pos_word % COUNT_BASE).astype(F32))

    last = n_z - 1
    halves = [range(h * n_z // 2, (h + 1) * n_z // 2) for h in range(2)]
    start_of = {
        (x, c, h): ((x * 2 + c) * 2 + h) * chunk for x in range(2) for c in range(2) for h in range(2)
    }
    items = {}
    m8 = jnp.full((8, n_query), ABSENT, F32)
    l8 = jnp.zeros((8, n_query), F32)

    def gathered(x, h, blocks):
        items[x, 0, h] = [blocks[j] for j in halves[h]]
        items[x, 1, h] = [hop(v, 1) for v in items[x, 0, h]]

    def statistics(m, l, *chosen):
        for key in chosen:
            m, l = run_stats(items[key], qt, bias, m, l, scale * LOG2E, start_of[key])
        return m, l

    for j in range(last):
        along_x[j] = hop(along_z[j], 2)
    gathered(0, 0, along_z)
    m8, l8 = statistics(m8, l8, (0, 0, 0), (0, 1, 0))
    along_z[last], m8, l8 = tie((along_z[last], m8, l8))
    along_x[last] = hop(along_z[last], 2)
    gathered(0, 1, along_z)
    m8, l8 = statistics(m8, l8, (0, 0, 1), (0, 1, 1))
    gathered(1, 0, along_x)
    m8, l8 = statistics(m8, l8, (1, 0, 0))
    along_x[last], m8, l8 = tie((along_x[last], m8, l8))
    gathered(1, 1, along_x)
    m8, l8 = statistics(m8, l8, (1, 1, 0), (1, 0, 1), (1, 1, 1))
    m1 = jnp.max(m8, axis=0)
    l1 = jnp.sum(l8 * jnp.exp2(m8 - m1[None]), axis=0)
    local = jnp.stack([m1, l1])
    parts = jnp.stack([local] + [hop(local, k, "mp") for k in range(1, n_model)])
    if n_model > 2:
        parts = jnp.take(parts, jnp.arange(n_model) ^ my_model, axis=0)
    row_max = jnp.max(parts[:, 0], axis=0)
    sums = parts[:, 1] * jnp.exp2(parts[:, 0] - row_max[None])
    normal = sums[0]
    for k in range(1, n_model):
        normal = normal + sums[k]
    lse = row_max + jnp.log2(normal)

    piece, b_late, lse = tie((piece, b_in[None, :], lse))
    others = [(hop(piece, k, "mp"), hop(b_late, k, "mp")) for k in range(1, n_model)]

    def wire(bound):
        factor = (LIMIT / bound) / q_bound
        return (lambda v: (v * factor).astype(F16)), (lambda v: v.astype(F32) * (1.0 / factor))

    def send(value, bits, bound):
        shrink, grow = wire(bound)
        return grow(hop(shrink(value), bits))

    def item_bound(devices):
        return devices * n_query * 2.0 * scale

    qg = jnp.zeros((width_out, n_query), F32)
    sp = jnp.zeros((8, n_query), F32)
    chip_sums, crossed, z_sums = {}, {}, [None] * n_z
    shrink, grow = wire(item_bound(2))

    def gradients(key, qg, sp, more=()):
        return run_grad(
            items[key], more, qt, queries, bias, lse[None, :], pos_col, qg, sp,
            scale, start_of[key],
        )

    siblings, crossing = {}, {}
    for h in (1, 0):
        sums, qg, sp = gradients((1, 1, h), qg, sp)
        siblings[1, h] = [hop(v, 1) for v in sums]
    for h in (1, 0):
        chip_sums[1, h], qg, sp = gradients((1, 0, h), qg, sp, siblings[1, h])
        crossing[h], qg = tie((shrink(jnp.concatenate(chip_sums[1, h], axis=0)), qg))
        crossed[h] = hop(crossing[h], 2)
    for h in (1, 0):
        sums, qg, sp = gradients((0, 1, h), qg, sp)
        siblings[0, h] = [hop(v, 1) for v in sums]
    for h in (1, 0):
        crossed[h], qg = tie((crossed[h], qg))
        chip_sums[0, h], qg, sp = gradients((0, 0, h), qg, sp, siblings[0, h])
        for j in range(n_z // 2):
            over = grow(crossed[h][j * part : (j + 1) * part])
            z_sums[h * n_z // 2 + j] = chip_sums[0, h][j] + over
    own_sum = z_sums[0]
    for j in range(n_z - 1, 0, -1):
        own_sum = own_sum + send(z_sums[j], j << 2, item_bound(4))
    own_grad, others = tie((own_sum.astype(BF16), others))

    others = [(xor_concat([got, hop(got, 1)], core), b) for got, b in others]

    hidden_max = width_emb * TABLE_MAX * W_IN_MAX + B_IN_MAX
    gradient_sum = n_data * n_query * 2.0 * scale
    bound_in = gradient_sum * width_out * W_OUT_MAX * TABLE_MAX
    bound_out = gradient_sum * hidden_max
    factor_in, factor_out = (LIMIT / bound_in) / q_bound, (LIMIT / bound_out) / q_bound
    grads = [own_grad] + [hop(own_grad, k, "mp") for k in range(1, n_model)]
    item_grad, pre_grad, local_b, value = run_backward(
        my_model.astype(jnp.int32).reshape(1), jnp.stack([factor_in, factor_out]), grads, pre, hidden, item_table, w_out
    )

    width = value.shape[1]
    keep = lax.dynamic_slice(value, (core * half_rows, 0), (half_rows, width))
    give = lax.dynamic_slice(value, ((1 - core) * half_rows, 0), (half_rows, width))
    bias_steps = [1 << n for n in range(n_data.bit_length() - 1)]

    def step_bias(value, steps):
        for _ in range(min(steps, len(bias_steps))):
            bits = bias_steps.pop(0)
            value = value + hop(value, bits)
        return value

    value = (keep + hop(give.astype(F16), 1).astype(F32)).astype(F16)
    value, local_b = tie((value, step_bias(local_b, 1)))
    value, qg, sp = tie((value, qg, sp))

    item_max = n_model * units * hidden_max * W_OUT_MAX
    q_factor = LIMIT / (2.0 * item_max)
    share = n_query // n_model
    sp1 = jnp.sum(sp, axis=0)[None, :]
    qg_parts = [
        lax.dynamic_slice(qg, (0, (my_model ^ k) * share), (width_out, share))
        for k in range(n_model)
    ]
    pos_score, query_sum = sp1, qg_parts[0]
    for k in range(1, n_model):
        sent = hop((qg_parts[k] * q_factor).astype(F16), k, "mp")
        query_sum = query_sum + sent.astype(F32) * (1.0 / q_factor)
        pos_score = pos_score + hop(sp1, k, "mp")
    loss = lse * (1.0 / LOG2E) - (pos_score[0] * scale - pos_logc)
    query_grad = (query_sum * scale).T

    chips = n_data // 2
    groups = [[2 * chip + c for chip in range(chips)] for c in range(2)]

    def exchange(blocks):
        return lax.all_to_all(
            blocks, "dp", split_axis=0, concat_axis=0, axis_index_groups=groups, tiled=True
        )

    size = half_rows // chips
    pieces = exchange(value.reshape(chips, size, width))
    total = jnp.sum(pieces.astype(F32), axis=0).astype(F16)
    total, local_b = tie((total, step_bias(local_b, 9)))
    own_half = exchange(jnp.broadcast_to(total[None], (chips, size, width)))
    own_half = own_half.reshape(half_rows, width)
    weights = [(packed, b_in[None, :])] + others
    if n_model > 2:
        turn = jnp.arange(n_model) ^ my_model
        stacks = [jnp.take(jnp.stack(group), turn, axis=0) for group in zip(*weights)]
        weights = [(stacks[0][k], stacks[1][k]) for k in range(n_model)]
    def backward(grad, weight, pre_values):
        return jnp.where(pre_values > 0.0, dot(grad, weight, NT), 0.0).astype(BF16)

    grad_table = None
    for pack, bias_units in weights:
        share_in, share_out = pack[:, :units], pack[:, units:].reshape(units, width_out)
        pre_units = dot(item_table, share_in) + bias_units
        term = dot(backward(item_grad, share_out, pre_units), share_in, NT)
        grad_table = term if grad_table is None else grad_table + term
    own_half, grad_table = tie((own_half, grad_table))
    sides = [own_half, hop(own_half, 1)]
    sides_in = [v[:, :units].astype(F32) * (1.0 / factor_in) for v in sides]
    sides_out = [v[:, units:].astype(F32) * (1.0 / factor_out) for v in sides]
    grad_w_in = xor_concat(sides_in, core)
    grad_w_out = xor_concat(sides_out, core).reshape(units, width_out)
    return (loss, query_grad, grad_w_in, local_b[0], grad_w_out, grad_table)


def solution(mesh):
    placed = (
        P("dp", None),
        P("dp", None),
        P("dp"),
        P("dp", None),
        P("dp"),
        P("dp"),
        P(None, "mp"),
        P("mp"),
        P("mp", None),
    )
    return jax.shard_map(
        per_device,
        mesh=mesh,
        in_specs=placed,
        out_specs=(
            P("dp"),
            P(("dp", "mp"), None),
            P(None, "mp"),
            P("mp"),
            P("mp", None),
            P("dp", None),
        ),
        check_vma=False,
    )
```

```python
import functools
import math

import jax
import jax.numpy as jnp
from jax import lax
from jax.experimental import pallas as pl
from jax.experimental.pallas import tpu as pltpu
from jax.sharding import PartitionSpec as P

F32 = jnp.float32
BF16 = jnp.bfloat16
F16 = jnp.float16
ABSENT = -1e30
COUNT_BASE = 128
WORD_BITS = 22
EXPONENT_BASE = 20
TABLE_MAX = 6.0
W_IN_MAX = 0.25
B_IN_MAX = 3.0
W_OUT_MAX = 0.1875
LIMIT = 32768.0
LOG2E = math.log2(math.e)
GROUP = 16
NT = (((1,), (1,)), ((), ()))
TN = (((0,), (0,)), ((), ()))


def hop(value, bits, axis="dp"):
    size = lax.axis_size(axis)
    return lax.ppermute(value, axis, [(i, i ^ bits) for i in range(size)])


def dot(a, b, dims=None, **kw):
    if dims is None:
        dims = (((1,), (0,)), ((), ()))
    return lax.dot_general(a, b, dims, preferred_element_type=F32, **kw)


def column_bias(bias_ref, first, count):
    lane = first // 128
    return bias_ref[pl.ds(first % 128, count), lane : lane + 1]


def stats_kernel(scale, base, count, *refs):
    items_refs, refs = refs[:count], refs[count:]
    qt_ref, bias_ref, m_in_ref, l_in_ref, m_ref, l_ref, arrived, *score_refs = refs
    held, score_refs = score_refs[:count], score_refs[count:]
    block = items_refs[0].shape[0]
    copies = [pltpu.make_async_copy(a, b, arrived.at[n]) for n, (a, b) in enumerate(zip(items_refs, held))]
    for copy in copies:
        copy.start()
    old = m_in_ref[...]
    new = old
    for copy, items_ref, score_ref in zip(copies, held, score_refs):
        copy.wait()
        score_ref[...] = dot(items_ref[...], qt_ref[...])
    for n, score_ref in enumerate(score_refs):
        for r in range(0, block, 8):
            bias = column_bias(bias_ref, base + n * block + r, 8)
            score = score_ref[r : r + 8] * scale + bias
            score_ref[r : r + 8] = score
            new = jnp.maximum(new, score)
    total = l_in_ref[...] * jnp.exp2(old - new)
    for score_ref in score_refs:
        for r in range(0, block, 8):
            total = total + jnp.exp2(score_ref[r : r + 8] - new)
    m_ref[...] = new
    l_ref[...] = total


def in_vmem(count):
    return [pl.BlockSpec(memory_space=pltpu.VMEM)] * count


def anywhere(count):
    return [pl.BlockSpec(memory_space=pl.ANY)] * count


def run_stats(items, qt, bias, m, l, scale, base):
    count, (block, width), nq = len(items), items[0].shape, qt.shape[1]
    return pl.pallas_call(
        functools.partial(stats_kernel, scale, base, count),
        in_specs=anywhere(count) + in_vmem(4),
        out_specs=in_vmem(2),
        out_shape=[jax.ShapeDtypeStruct((8, nq), F32)] * 2,
        scratch_shapes=[pltpu.SemaphoreType.DMA((count,))]
        + [pltpu.VMEM((block, width), BF16)] * count
        + [pltpu.VMEM((block, nq), F32)] * count,
        compiler_params=pltpu.CompilerParams(vmem_limit_bytes=8 << 20),
    )(*items, qt, bias, m, l)


def grad_kernel(scale, base, count, add, *refs):
    items_refs, refs = refs[:count], refs[count:]
    more_refs, refs = refs[:add], refs[add:]
    qt_ref, q_ref, bias_ref, lse_ref, pos_ref, qg_in_ref, sp_in_ref, *refs = refs
    sums_refs, (qg_ref, sp_ref, arrived, left, *scratch) = refs[:count], refs[count:]
    held, more_held, out_held, score_refs, prob_refs = (
        scratch[n * count : (n + 1) * count] for n in range(5)
    )
    block, queries = items_refs[0].shape[0], qt_ref.shape[1]
    sources, targets = [*items_refs, *more_refs], [*held, *more_held]
    copies = [
        pltpu.make_async_copy(a, b, arrived.at[n]) for n, (a, b) in enumerate(zip(sources, targets))
    ]
    leaving = [
        pltpu.make_async_copy(a, b, left.at[n]) for n, (a, b) in enumerate(zip(out_held, sums_refs))
    ]
    for copy in copies:
        copy.start()
    for copy, items_ref, score_ref in zip(copies, held, score_refs):
        copy.wait()
        score_ref[...] = dot(items_ref[...], qt_ref[...])
    down = lax.broadcasted_iota(jnp.int32, (8, queries), 0)
    offset = jnp.broadcast_to(pos_ref[...], (8, queries)) - down
    lse = jnp.broadcast_to(lse_ref[...], (8, queries))
    found = sp_in_ref[...]
    for n in range(count):
        score_ref, prob_ref = score_refs[n], prob_refs[n]
        for r in range(0, block, GROUP):
            pieces = []
            for s in range(r, r + GROUP, 8):
                at = base + n * block + s
                score = score_ref[s : s + 8]
                here = offset == at
                found = found + jnp.where(here, score, 0.0)
                prob = jnp.exp2((score * (scale * LOG2E) + column_bias(bias_ref, at, 8)) - lse)
                pieces.append(jnp.where(here, prob - 1.0, prob))
            prob_ref[r : r + GROUP] = jnp.concatenate(pieces, axis=0).astype(BF16)
        sums = dot(prob_ref[...], q_ref[...]) * scale
        if add:
            copies[count + n].wait()
            sums = sums + more_held[n][...]
        out_held[n][...] = sums
        leaving[n].start()
        share = dot(held[n][...], prob_ref[...], TN)
        qg_ref[...] = (qg_in_ref[...] if n == 0 else qg_ref[...]) + share
    sp_ref[...] = found
    for copy in leaving:
        copy.wait()


def run_grad(items, more, qt, q, bias, lse, pos, qg, sp, scale, base):
    count, (block, width), nq = len(items), items[0].shape, qt.shape[1]
    before = count + len(more)
    *sums, qg, sp = pl.pallas_call(
        functools.partial(grad_kernel, scale, base, count, len(more)),
        in_specs=anywhere(before) + in_vmem(7),
        out_specs=anywhere(count) + in_vmem(2),
        out_shape=[jax.ShapeDtypeStruct((block, width), F32)] * count
        + [jax.ShapeDtypeStruct((width, nq), F32), jax.ShapeDtypeStruct((8, nq), F32)],
        scratch_shapes=[pltpu.SemaphoreType.DMA((before,)), pltpu.SemaphoreType.DMA((count,))]
        + [pltpu.VMEM((block, width), BF16)] * count
        + [pltpu.VMEM((block, width), F32)] * (2 * count)
        + [pltpu.VMEM((block, nq), F32)] * count
        + [pltpu.VMEM((block, nq), BF16)] * count,
        input_output_aliases={before + 5: count, before + 6: count + 1},
        compiler_params=pltpu.CompilerParams(vmem_limit_bytes=12 << 20),
    )(*items, *more, qt, q, bias, lse, pos, qg, sp)
    return sums, qg, sp


def backward_kernel(count, index_ref, factor_ref, *refs):
    grad_refs, (pre_ref, hidden_ref, emb_ref, w_out_ref) = refs[:count], refs[count : count + 4]
    grad_ref, pre_grad_ref, b_ref, *sums_refs = refs[count + 4 :]
    part = grad_refs[0].shape[0]
    for k in range(count):
        start = pl.multiple_of((index_ref[0] ^ k) * part, part)
        grad_ref[pl.ds(start, part)] = grad_refs[k][...]
    back = dot(grad_ref[...], w_out_ref[...], NT)
    pre_grad = jnp.where(pre_ref[...] > 0.0, back, 0.0).astype(BF16)
    pre_grad_ref[...] = pre_grad
    b_ref[...] = jnp.sum(pre_grad.astype(F32), axis=0, keepdims=True)
    sums_in = dot(emb_ref[...], pre_grad, TN) * factor_ref[0]
    sums_out = dot(hidden_ref[...], grad_ref[...], TN) * factor_ref[1]
    if len(sums_refs) == 1:
        units = sums_in.shape[1]
        sums_refs[0][:, :units] = sums_in
        sums_refs[0][:, units:] = sums_out
    else:
        sums_refs[0][...] = sums_in
        sums_refs[1][...] = sums_out


def run_backward(index, factors, grads, pre, hidden, emb, w_out):
    rows, units = pre.shape
    width_emb, width_out = emb.shape[1], w_out.shape[1]
    if units == width_emb:
        sums = [(width_emb, units + width_out)]
    else:
        sums = [(width_emb, units), (units, width_out)]
    grad, pre_grad, local_b, *sums = pl.pallas_call(
        functools.partial(backward_kernel, len(grads)),
        in_specs=[pl.BlockSpec(memory_space=pltpu.SMEM)] * 2 + in_vmem(len(grads) + 4),
        out_specs=in_vmem(3 + len(sums)),
        out_shape=[
            jax.ShapeDtypeStruct((rows, width_out), BF16),
            jax.ShapeDtypeStruct((rows, units), BF16),
            jax.ShapeDtypeStruct((1, units), F32),
        ]
        + [jax.ShapeDtypeStruct(shape, F32) for shape in sums],
        compiler_params=pltpu.CompilerParams(vmem_limit_bytes=12 << 20),
    )(index, factors, *grads, pre, hidden, emb, w_out)
    if len(sums) > 1:
        sums = [jnp.concatenate([sums[0], sums[1].reshape(width_emb, -1)], axis=1)]
    return grad, pre_grad, local_b, sums[0]


def xor_concat(blocks, index, axis=0):
    if len(blocks) == 1:
        return blocks[0]
    half = len(blocks) // 2
    low = xor_concat(blocks[:half], index, axis)
    high = xor_concat(blocks[half:], index, axis)
    return jnp.where(
        (index & half) == 0,
        jnp.concatenate([low, high], axis=axis),
        jnp.concatenate([high, low], axis=axis),
    )


def per_device(queries, item_table, cand_row, cand_owner, cand_count, positive, w_in, b_in, w_out):
    n_data = lax.axis_size("dp")
    n_model = lax.axis_size("mp")
    n_z = n_data // 4
    me = lax.axis_index("dp")
    my_model = lax.axis_index("mp")
    n_query, width_out = queries.shape
    rows, width_emb = item_table.shape
    units = w_in.shape[1]
    part = rows // n_model
    cand_local = cand_row.shape[0]
    n_cols = n_data * part
    chunk = n_z * part // 2
    scale = 1.0 / math.sqrt(width_out)
    tie = lax.optimization_barrier

    def place(rel):
        return ((rel >> 1) & 1) * (2 * n_z) + (rel & 1) * n_z + (rel >> 2)

    def bit_of(bits):
        return (me // bits) & 1

    pre = dot(item_table, w_in) + b_in[None, :]
    hidden = jnp.maximum(pre, 0.0).astype(BF16)
    partial = dot(hidden, w_out)

    def part_of(value, k):
        return lax.dynamic_slice(value, ((my_model ^ k) * part, 0), (part, value.shape[1]))

    outgoing = [part_of(partial, k) for k in range(1, n_model)]
    arrived = [hop(outgoing[k - 1], k, "mp") for k in range(1, n_model)]
    outgoing, queries, cand_row = tie((outgoing, queries, cand_row))
    qt = queries.T
    core = me & 1
    packed = jnp.concatenate([w_in, w_out.reshape(width_emb, -1)], axis=1)
    half_rows = width_emb // 2
    piece = lax.dynamic_slice(packed, (core * half_rows, 0), (half_rows, packed.shape[1]))

    largest = jnp.max(jnp.abs(queries)).astype(F32)
    exponent = jnp.floor(jnp.log2(jnp.maximum(largest, 1e-6))).astype(jnp.int32) + 1
    exponent = jnp.clip(exponent + EXPONENT_BASE, 0, 63)
    word = (cand_owner[:, 0] * rows + cand_row) * COUNT_BASE + cand_count
    word = (word + exponent * (1 << WORD_BITS))[None, :]
    words = jnp.concatenate([word, hop(word, 1)], axis=0)
    words = jnp.concatenate([words, hop(words, 2)], axis=0)

    total, arrived, qt, piece = tie((part_of(partial, 0), arrived, qt, piece))
    for other in arrived:
        total = total + other
    item_own = total.astype(BF16)
    along_z, along_x = {0: item_own}, {}
    for j in range(n_z - 1, 0, -1):
        along_z[j] = hop(item_own, j << 2)
    words = jnp.concatenate([words] + [hop(words, k << 2) for k in range(1, n_z)], axis=0)
    along_z[1], words = tie((along_z[1], words))

    flat = words.reshape(-1)
    n_cand = flat.shape[0]
    q_bound = jnp.exp2((jnp.max(flat >> WORD_BITS) - EXPONENT_BASE).astype(F32))
    flat = flat & ((1 << WORD_BITS) - 1)
    row = (flat // COUNT_BASE) % rows
    column = place((flat // (COUNT_BASE * rows)) ^ me) * part + row % part
    column = jnp.where(row // part == my_model, column, -1)
    share = 1.0 / (flat % COUNT_BASE).astype(F32)
    lanes = 128
    high = (jnp.arange(n_cols // lanes)[:, None] == (column >> 7)[None, :]).astype(F32)
    low = jnp.where(jnp.arange(lanes)[:, None] == (column & 127)[None, :], share[None, :], 0.0)
    weight = dot(low, high, NT, precision=lax.Precision.HIGHEST)
    bias = jnp.where(weight > 0.0, jnp.log2(weight), ABSENT)

    spot = ((positive // cand_local) ^ me) * cand_local + positive % cand_local
    side = 64
    table = flat.reshape(n_cand // side, side)
    digits = jnp.concatenate([table & 255, (table >> 8) & 255, table >> 16], axis=1).astype(BF16)
    picked = (jnp.arange(n_cand // side)[:, None] == (spot // side)[None, :]).astype(BF16)
    found = dot(digits, picked, TN).reshape(3, side, n_query)
    mine = jnp.arange(side)[:, None] == (spot % side)[None, :]
    digit = jnp.sum(jnp.where(mine[None], found, 0.0), axis=1).astype(jnp.int32)
    pos_word = digit[0] + digit[1] * 256 + digit[2] * 65536
    pos_row = (pos_word // COUNT_BASE) % rows
    pos_col = place((pos_word // (COUNT_BASE * rows)) ^ me) * part + pos_row % part
    pos_col = jnp.where(pos_row // part == my_model, pos_col, -1)[None, :]
    pos_logc = jnp.log((pos_word % COUNT_BASE).astype(F32))

    last = n_z - 1
    halves = [range(h * n_z // 2, (h + 1) * n_z // 2) for h in range(2)]
    start_of = {
        (x, c, h): ((x * 2 + c) * 2 + h) * chunk for x in range(2) for c in range(2) for h in range(2)
    }
    items = {}
    m8 = jnp.full((8, n_query), ABSENT, F32)
    l8 = jnp.zeros((8, n_query), F32)

    def gathered(x, h, blocks):
        items[x, 0, h] = [blocks[j] for j in halves[h]]
        items[x, 1, h] = [hop(v, 1) for v in items[x, 0, h]]

    def statistics(m, l, *chosen):
        for key in chosen:
            m, l = run_stats(items[key], qt, bias, m, l, scale * LOG2E, start_of[key])
        return m, l

    for j in range(last):
        along_x[j] = hop(along_z[j], 2)
    gathered(0, 0, along_z)
    m8, l8 = statistics(m8, l8, (0, 0, 0), (0, 1, 0))
    along_z[last], m8, l8 = tie((along_z[last], m8, l8))
    along_x[last] = hop(along_z[last], 2)
    gathered(0, 1, along_z)
    m8, l8 = statistics(m8, l8, (0, 0, 1), (0, 1, 1))
    gathered(1, 0, along_x)
    m8, l8 = statistics(m8, l8, (1, 0, 0))
    along_x[last], m8, l8 = tie((along_x[last], m8, l8))
    gathered(1, 1, along_x)
    m8, l8 = statistics(m8, l8, (1, 1, 0), (1, 0, 1), (1, 1, 1))
    m1 = jnp.max(m8, axis=0)
    l1 = jnp.sum(l8 * jnp.exp2(m8 - m1[None]), axis=0)
    local = jnp.stack([m1, l1])
    parts = jnp.stack([local] + [hop(local, k, "mp") for k in range(1, n_model)])
    if n_model > 2:
        parts = jnp.take(parts, jnp.arange(n_model) ^ my_model, axis=0)
    row_max = jnp.max(parts[:, 0], axis=0)
    sums = parts[:, 1] * jnp.exp2(parts[:, 0] - row_max[None])
    normal = sums[0]
    for k in range(1, n_model):
        normal = normal + sums[k]
    lse = row_max + jnp.log2(normal)

    piece, b_late, lse = tie((piece, b_in[None, :], lse))
    others = [(hop(piece, k, "mp"), hop(b_late, k, "mp")) for k in range(1, n_model)]

    def wire(bound):
        factor = (LIMIT / bound) / q_bound
        return (lambda v: (v * factor).astype(F16)), (lambda v: v.astype(F32) * (1.0 / factor))

    def send(value, bits, bound):
        shrink, grow = wire(bound)
        return grow(hop(shrink(value), bits))

    def item_bound(devices):
        return devices * n_query * 2.0 * scale

    qg = jnp.zeros((width_out, n_query), F32)
    sp = jnp.zeros((8, n_query), F32)
    chip_sums, crossed, z_sums = {}, {}, [None] * n_z
    shrink, grow = wire(item_bound(2))

    def gradients(key, qg, sp, more=()):
        return run_grad(
            items[key], more, qt, queries, bias, lse[None, :], pos_col, qg, sp,
            scale, start_of[key],
        )

    siblings, crossing = {}, {}
    for h in (1, 0):
        sums, qg, sp = gradients((1, 1, h), qg, sp)
        siblings[1, h] = [hop(v, 1) for v in sums]
    for h in (1, 0):
        chip_sums[1, h], qg, sp = gradients((1, 0, h), qg, sp, siblings[1, h])
        crossing[h], qg = tie((shrink(jnp.concatenate(chip_sums[1, h], axis=0)), qg))
        crossed[h] = hop(crossing[h], 2)
    for h in (1, 0):
        sums, qg, sp = gradients((0, 1, h), qg, sp)
        siblings[0, h] = [hop(v, 1) for v in sums]
    for h in (1, 0):
        crossed[h], qg = tie((crossed[h], qg))
        chip_sums[0, h], qg, sp = gradients((0, 0, h), qg, sp, siblings[0, h])
        for j in range(n_z // 2):
            over = grow(crossed[h][j * part : (j + 1) * part])
            z_sums[h * n_z // 2 + j] = chip_sums[0, h][j] + over
    own_sum = z_sums[0]
    for j in range(n_z - 1, 0, -1):
        own_sum = own_sum + send(z_sums[j], j << 2, item_bound(4))
    own_grad, others = tie((own_sum.astype(BF16), others))


    hidden_max = width_emb * TABLE_MAX * W_IN_MAX + B_IN_MAX
    gradient_sum = n_data * n_query * 2.0 * scale
    bound_in = gradient_sum * width_out * W_OUT_MAX * TABLE_MAX
    bound_out = gradient_sum * hidden_max
    factor_in, factor_out = (LIMIT / bound_in) / q_bound, (LIMIT / bound_out) / q_bound
    grads = [own_grad] + [hop(own_grad, k, "mp") for k in range(1, n_model)]
    item_grad, pre_grad, local_b, value = run_backward(
        my_model.astype(jnp.int32).reshape(1), jnp.stack([factor_in, factor_out]), grads, pre, hidden, item_table, w_out
    )

    width = value.shape[1]
    keep = lax.dynamic_slice(value, (core * half_rows, 0), (half_rows, width))
    give = lax.dynamic_slice(value, ((1 - core) * half_rows, 0), (half_rows, width))
    bias_steps = [1 << n for n in range(n_data.bit_length() - 1)]

    def step_bias(value, steps):
        for _ in range(min(steps, len(bias_steps))):
            bits = bias_steps.pop(0)
            value = value + hop(value, bits)
        return value

    value = (keep + hop(give.astype(F16), 1).astype(F32)).astype(F16)
    value, local_b = tie((value, step_bias(local_b, 1)))
    value, qg, sp = tie((value, qg, sp))

    item_max = n_model * units * hidden_max * W_OUT_MAX
    q_factor = LIMIT / (2.0 * item_max)
    share = n_query // n_model
    sp1 = jnp.sum(sp, axis=0)[None, :]
    qg_parts = [
        lax.dynamic_slice(qg, (0, (my_model ^ k) * share), (width_out, share))
        for k in range(n_model)
    ]
    pos_score, query_sum = sp1, qg_parts[0]
    for k in range(1, n_model):
        sent = hop((qg_parts[k] * q_factor).astype(F16), k, "mp")
        query_sum = query_sum + sent.astype(F32) * (1.0 / q_factor)
        pos_score = pos_score + hop(sp1, k, "mp")
    loss = lse * (1.0 / LOG2E) - (pos_score[0] * scale - pos_logc)
    query_grad = (query_sum * scale).T

    chips = n_data // 2
    groups = [[2 * chip + c for chip in range(chips)] for c in range(2)]

    def exchange(blocks):
        return lax.all_to_all(
            blocks, "dp", split_axis=0, concat_axis=0, axis_index_groups=groups, tiled=True
        )

    size = half_rows // chips
    pieces = exchange(value.reshape(chips, size, width))
    total = jnp.sum(pieces.astype(F32), axis=0).astype(F16)
    total, local_b, others = tie((total, step_bias(local_b, 9), others))
    others = [(xor_concat([got, hop(got, 1)], core), b) for got, b in others]
    own_half = exchange(jnp.broadcast_to(total[None], (chips, size, width)))
    own_half = own_half.reshape(half_rows, width)
    weights = [(packed, b_in[None, :])] + others
    if n_model > 2:
        turn = jnp.arange(n_model) ^ my_model
        stacks = [jnp.take(jnp.stack(group), turn, axis=0) for group in zip(*weights)]
        weights = [(stacks[0][k], stacks[1][k]) for k in range(n_model)]
    def backward(grad, weight, pre_values):
        return jnp.where(pre_values > 0.0, dot(grad, weight, NT), 0.0).astype(BF16)

    grad_table = None
    for pack, bias_units in weights:
        share_in, share_out = pack[:, :units], pack[:, units:].reshape(units, width_out)
        pre_units = dot(item_table, share_in) + bias_units
        term = dot(backward(item_grad, share_out, pre_units), share_in, NT)
        grad_table = term if grad_table is None else grad_table + term
    own_half, grad_table = tie((own_half, grad_table))
    sides = [own_half, hop(own_half, 1)]
    sides_in = [v[:, :units].astype(F32) * (1.0 / factor_in) for v in sides]
    sides_out = [v[:, units:].astype(F32) * (1.0 / factor_out) for v in sides]
    grad_w_in = xor_concat(sides_in, core)
    grad_w_out = xor_concat(sides_out, core).reshape(units, width_out)
    return (loss, query_grad, grad_w_in, local_b[0], grad_w_out, grad_table)


def solution(mesh):
    placed = (
        P("dp", None),
        P("dp", None),
        P("dp"),
        P("dp", None),
        P("dp"),
        P("dp"),
        P(None, "mp"),
        P("mp"),
        P("mp", None),
    )
    return jax.shard_map(
        per_device,
        mesh=mesh,
        in_specs=placed,
        out_specs=(
            P("dp"),
            P(("dp", "mp"), None),
            P(None, "mp"),
            P("mp"),
            P("mp", None),
            P("dp", None),
        ),
        check_vma=False,
    )
```

```python
import functools
import math

import jax
import jax.numpy as jnp
from jax import lax
from jax.experimental import pallas as pl
from jax.experimental.pallas import tpu as pltpu
from jax.sharding import PartitionSpec as P

F32 = jnp.float32
BF16 = jnp.bfloat16
F16 = jnp.float16
ABSENT = -1e30
COUNT_BASE = 128
WORD_BITS = 22
EXPONENT_BASE = 20
TABLE_MAX = 6.0
W_IN_MAX = 0.25
B_IN_MAX = 3.0
W_OUT_MAX = 0.1875
LIMIT = 32768.0
LOG2E = math.log2(math.e)
GROUP = 16
NT = (((1,), (1,)), ((), ()))
TN = (((0,), (0,)), ((), ()))


def hop(value, bits, axis="dp"):
    size = lax.axis_size(axis)
    return lax.ppermute(value, axis, [(i, i ^ bits) for i in range(size)])


def dot(a, b, dims=None, **kw):
    if dims is None:
        dims = (((1,), (0,)), ((), ()))
    return lax.dot_general(a, b, dims, preferred_element_type=F32, **kw)


def column_bias(bias_ref, first, count):
    lane = first // 128
    return bias_ref[pl.ds(first % 128, count), lane : lane + 1]


def stats_kernel(scale, base, count, last, *refs):
    items_refs, refs = refs[:count], refs[count:]
    qt_ref, bias_ref, m_in_ref, l_in_ref, m_ref, *score_refs = refs
    l_ref = None if last else score_refs.pop(0)
    block = items_refs[0].shape[0]
    old = m_in_ref[...]
    new = old
    for items_ref, score_ref in zip(items_refs, score_refs):
        score_ref[...] = dot(items_ref[...], qt_ref[...])
    for n, score_ref in enumerate(score_refs):
        for r in range(0, block, 8):
            bias = column_bias(bias_ref, base + n * block + r, 8)
            score = score_ref[r : r + 8] * scale + bias
            score_ref[r : r + 8] = score
            new = jnp.maximum(new, score)
    total = l_in_ref[...] * jnp.exp2(old - new)
    for score_ref in score_refs:
        for r in range(0, block, 8):
            total = total + jnp.exp2(score_ref[r : r + 8] - new)
    if last:
        top = jnp.max(new, axis=0, keepdims=True)
        m_ref[0:1] = top
        m_ref[1:2] = jnp.sum(total * jnp.exp2(new - top), axis=0, keepdims=True)
    else:
        m_ref[...] = new
        l_ref[...] = total


def in_vmem(count):
    return [pl.BlockSpec(memory_space=pltpu.VMEM)] * count


def run_stats(items, qt, bias, m, l, scale, base, last):
    count, (block, width), nq = len(items), items[0].shape, qt.shape[1]
    shapes = [(2, nq)] if last else [(8, nq)] * 2
    return pl.pallas_call(
        functools.partial(stats_kernel, scale, base, count, last),
        in_specs=in_vmem(count + 4),
        out_specs=in_vmem(len(shapes)),
        out_shape=[jax.ShapeDtypeStruct(shape, F32) for shape in shapes],
        scratch_shapes=[pltpu.VMEM((block, nq), F32)] * count,
        compiler_params=pltpu.CompilerParams(vmem_limit_bytes=6 << 20),
    )(*items, qt, bias, m, l)


def lse_kernel(count, index_ref, *refs):
    part_refs, (lse_ref, held_ref) = refs[:count], refs[count:]
    for k in range(count):
        held_ref[index_ref[0] ^ k] = part_refs[k][...]
    parts = [held_ref[k] for k in range(count)]
    top = functools.reduce(jnp.maximum, [p[0:1] for p in parts])
    total = functools.reduce(jnp.add, [p[1:2] * jnp.exp2(p[0:1] - top) for p in parts])
    lse_ref[...] = top + jnp.log2(total)


def run_lse(index, parts):
    nq = parts[0].shape[1]
    return pl.pallas_call(
        functools.partial(lse_kernel, len(parts)),
        in_specs=[pl.BlockSpec(memory_space=pltpu.SMEM)] + in_vmem(len(parts)),
        out_specs=in_vmem(1)[0],
        out_shape=jax.ShapeDtypeStruct((1, nq), F32),
        scratch_shapes=[pltpu.VMEM((len(parts), 2, nq), F32)],
        compiler_params=pltpu.CompilerParams(vmem_limit_bytes=2 << 20),
    )(index, *parts)


def grad_kernel(scale, base, count, add, *refs):
    items_refs, refs = refs[:count], refs[count:]
    more_refs, refs = refs[:add], refs[add:]
    qt_ref, q_ref, bias_ref, lse_ref, pos_ref, qg_in_ref, sp_in_ref, *refs = refs
    sums_refs, (qg_ref, sp_ref, *scratch) = refs[:count], refs[count:]
    score_refs, prob_refs = scratch[:count], scratch[count:]
    block, queries = items_refs[0].shape[0], qt_ref.shape[1]
    for items_ref, score_ref in zip(items_refs, score_refs):
        score_ref[...] = dot(items_ref[...], qt_ref[...])
    down = lax.broadcasted_iota(jnp.int32, (8, queries), 0)
    offset = jnp.broadcast_to(pos_ref[...], (8, queries)) - down
    lse = jnp.broadcast_to(lse_ref[...], (8, queries))
    found = sp_in_ref[...]
    for n in range(count):
        score_ref, prob_ref = score_refs[n], prob_refs[n]
        for r in range(0, block, GROUP):
            pieces = []
            for s in range(r, r + GROUP, 8):
                at = base + n * block + s
                score = score_ref[s : s + 8]
                here = offset == at
                found = found + jnp.where(here, score, 0.0)
                prob = jnp.exp2((score * (scale * LOG2E) + column_bias(bias_ref, at, 8)) - lse)
                pieces.append(jnp.where(here, prob - 1.0, prob))
            prob_ref[r : r + GROUP] = jnp.concatenate(pieces, axis=0).astype(BF16)
        sums = dot(prob_ref[...], q_ref[...]) * scale
        sums_refs[n][...] = sums + more_refs[n][...] if add else sums
        share = dot(items_refs[n][...], prob_ref[...], TN)
        qg_ref[...] = (qg_in_ref[...] if n == 0 else qg_ref[...]) + share
    sp_ref[...] = found


def run_grad(items, more, qt, q, bias, lse, pos, qg, sp, scale, base):
    count, (block, width), nq = len(items), items[0].shape, qt.shape[1]
    before = count + len(more)
    *sums, qg, sp = pl.pallas_call(
        functools.partial(grad_kernel, scale, base, count, len(more)),
        in_specs=in_vmem(before + 7),
        out_specs=in_vmem(count + 2),
        out_shape=[jax.ShapeDtypeStruct((block, width), F32)] * count
        + [jax.ShapeDtypeStruct((width, nq), F32), jax.ShapeDtypeStruct((8, nq), F32)],
        scratch_shapes=[pltpu.VMEM((block, nq), F32)] * count
        + [pltpu.VMEM((block, nq), BF16)] * count,
        input_output_aliases={before + 5: count, before + 6: count + 1},
        compiler_params=pltpu.CompilerParams(vmem_limit_bytes=8 << 20),
    )(*items, *more, qt, q, bias, lse, pos, qg, sp)
    return sums, qg, sp


def backward_kernel(count, index_ref, factor_ref, *refs):
    grad_refs, (pre_ref, hidden_ref, emb_ref, w_out_ref) = refs[:count], refs[count : count + 4]
    grad_ref, pre_grad_ref, b_ref, *sums_refs = refs[count + 4 :]
    part = grad_refs[0].shape[0]
    for k in range(count):
        start = pl.multiple_of((index_ref[0] ^ k) * part, part)
        grad_ref[pl.ds(start, part)] = grad_refs[k][...]
    back = dot(grad_ref[...], w_out_ref[...], NT)
    pre_grad = jnp.where(pre_ref[...] > 0.0, back, 0.0).astype(BF16)
    pre_grad_ref[...] = pre_grad
    b_ref[...] = jnp.sum(pre_grad.astype(F32), axis=0, keepdims=True)
    sums_in = dot(emb_ref[...], pre_grad, TN) * factor_ref[0]
    sums_out = dot(hidden_ref[...], grad_ref[...], TN) * factor_ref[1]
    if len(sums_refs) == 1:
        units = sums_in.shape[1]
        sums_refs[0][:, :units] = sums_in
        sums_refs[0][:, units:] = sums_out
    else:
        sums_refs[0][...] = sums_in
        sums_refs[1][...] = sums_out


def run_backward(index, factors, grads, pre, hidden, emb, w_out):
    rows, units = pre.shape
    width_emb, width_out = emb.shape[1], w_out.shape[1]
    if units == width_emb:
        sums = [(width_emb, units + width_out)]
    else:
        sums = [(width_emb, units), (units, width_out)]
    grad, pre_grad, local_b, *sums = pl.pallas_call(
        functools.partial(backward_kernel, len(grads)),
        in_specs=[pl.BlockSpec(memory_space=pltpu.SMEM)] * 2 + in_vmem(len(grads) + 4),
        out_specs=in_vmem(3 + len(sums)),
        out_shape=[
            jax.ShapeDtypeStruct((rows, width_out), BF16),
            jax.ShapeDtypeStruct((rows, units), BF16),
            jax.ShapeDtypeStruct((1, units), F32),
        ]
        + [jax.ShapeDtypeStruct(shape, F32) for shape in sums],
        compiler_params=pltpu.CompilerParams(vmem_limit_bytes=12 << 20),
    )(index, factors, *grads, pre, hidden, emb, w_out)
    if len(sums) > 1:
        sums = [jnp.concatenate([sums[0], sums[1].reshape(width_emb, -1)], axis=1)]
    return grad, pre_grad, local_b, sums[0]


def joined(mine, other, first):
    return jnp.where(
        first,
        jnp.concatenate([mine, other], axis=0),
        jnp.concatenate([other, mine], axis=0),
    )


def per_device(queries, item_table, cand_row, cand_owner, cand_count, positive, w_in, b_in, w_out):
    n_data = lax.axis_size("dp")
    n_model = lax.axis_size("mp")
    n_z = n_data // 4
    me = lax.axis_index("dp")
    my_model = lax.axis_index("mp")
    n_query, width_out = queries.shape
    rows, width_emb = item_table.shape
    units = w_in.shape[1]
    part = rows // n_model
    cand_local = cand_row.shape[0]
    n_cols = n_data * part
    chunk = n_z * part // 2
    scale = 1.0 / math.sqrt(width_out)
    tie = lax.optimization_barrier
    slice_at = functools.partial(lax.dynamic_slice, allow_negative_indices=False)
    core = me & 1
    half_rows = width_emb // 2
    query_part = n_query // n_model
    starts = [(my_model ^ k) * part for k in range(n_model)]
    share_starts = [(my_model ^ k) * query_part for k in range(n_model)]
    half_starts = [(core ^ k) * half_rows for k in range(2)]
    model_index = my_model.astype(jnp.int32).reshape(1)
    core_first = core == 0

    def place(rel):
        return ((rel >> 1) & 1) * (2 * n_z) + (rel & 1) * n_z + (rel >> 2)

    def bit_of(bits):
        return (me // bits) & 1

    pre = dot(item_table, w_in) + b_in[None, :]
    hidden = jnp.maximum(pre, 0.0).astype(BF16)
    partial = dot(hidden, w_out)

    def part_of(value, k):
        return slice_at(value, (starts[k], 0), (part, value.shape[1]))

    outgoing = [part_of(partial, k) for k in range(1, n_model)]
    arrived = [hop(outgoing[k - 1], k, "mp") for k in range(1, n_model)]
    outgoing, queries, cand_row = tie((outgoing, queries, cand_row))
    qt = queries.T
    packed = jnp.concatenate([w_in, w_out.reshape(width_emb, -1)], axis=1)
    piece = slice_at(packed, (half_starts[0], 0), (half_rows, packed.shape[1]))

    largest = jnp.max(jnp.abs(queries)).astype(F32)
    exponent = jnp.floor(jnp.log2(jnp.maximum(largest, 1e-6))).astype(jnp.int32) + 1
    exponent = jnp.clip(exponent + EXPONENT_BASE, 0, 63)
    word = (cand_owner[:, 0] * rows + cand_row) * COUNT_BASE + cand_count
    word = (word + exponent * (1 << WORD_BITS))[None, :]
    words = jnp.concatenate([word, hop(word, 1)], axis=0)
    words = jnp.concatenate([words, hop(words, 2)], axis=0)

    total, arrived, qt, piece = tie((part_of(partial, 0), arrived, qt, piece))
    for other in arrived:
        total = total + other
    item_own = total.astype(BF16)
    along_z, along_x = {0: item_own}, {}
    for j in range(n_z - 1, 0, -1):
        along_z[j] = hop(item_own, j << 2)
    words = jnp.concatenate([words] + [hop(words, k << 2) for k in range(1, n_z)], axis=0)
    along_z[1], words = tie((along_z[1], words))

    flat = words.reshape(-1)
    n_cand = flat.shape[0]
    q_bound = jnp.exp2((jnp.max(flat >> WORD_BITS) - EXPONENT_BASE).astype(F32))
    flat = flat & ((1 << WORD_BITS) - 1)

    hidden_max = width_emb * TABLE_MAX * W_IN_MAX + B_IN_MAX
    gradient_sum = n_data * n_query * 2.0 * scale
    bounds = [
        2 * n_query * 2.0 * scale,
        4 * n_query * 2.0 * scale,
        gradient_sum * width_out * W_OUT_MAX * TABLE_MAX,
        gradient_sum * hidden_max,
    ]
    factors = [(LIMIT / bound) / q_bound for bound in bounds]
    growths = [q_bound * (bound / LIMIT) for bound in bounds]
    row = (flat // COUNT_BASE) % rows
    column = place((flat // (COUNT_BASE * rows)) ^ me) * part + row % part
    column = jnp.where(row // part == my_model, column, -1)
    share = 1.0 / (flat % COUNT_BASE).astype(F32)
    lanes = 128
    high = (jnp.arange(n_cols // lanes)[:, None] == (column >> 7)[None, :]).astype(F32)
    low = jnp.where(jnp.arange(lanes)[:, None] == (column & 127)[None, :], share[None, :], 0.0)
    weight = dot(low, high, NT, precision=lax.Precision.HIGHEST)
    bias = jnp.where(weight > 0.0, jnp.log2(weight), ABSENT)
    bias, factors, growths, share_starts, half_starts, model_index, core_first = tie(
        (bias, factors, growths, share_starts, half_starts, model_index, core_first)
    )

    spot = ((positive // cand_local) ^ me) * cand_local + positive % cand_local
    side = 64
    table = flat.reshape(n_cand // side, side)
    digits = jnp.concatenate([table & 255, (table >> 8) & 255, table >> 16], axis=1).astype(BF16)
    picked = (jnp.arange(n_cand // side)[:, None] == (spot // side)[None, :]).astype(BF16)
    found = dot(digits, picked, TN).reshape(3, side, n_query)
    mine = jnp.arange(side)[:, None] == (spot % side)[None, :]
    digit = jnp.sum(jnp.where(mine[None], found, 0.0), axis=1).astype(jnp.int32)
    pos_word = digit[0] + digit[1] * 256 + digit[2] * 65536
    pos_row = (pos_word // COUNT_BASE) % rows
    pos_col = place((pos_word // (COUNT_BASE * rows)) ^ me) * part + pos_row % part
    pos_col = jnp.where(pos_row // part == my_model, pos_col, -1)[None, :]
    pos_logc = jnp.log((pos_word % COUNT_BASE).astype(F32))

    last = n_z - 1
    halves = [range(h * n_z // 2, (h + 1) * n_z // 2) for h in range(2)]
    start_of = {
        (x, c, h): ((x * 2 + c) * 2 + h) * chunk for x in range(2) for c in range(2) for h in range(2)
    }
    items = {}
    m8 = jnp.full((8, n_query), ABSENT, F32)
    l8 = jnp.zeros((8, n_query), F32)

    def gathered(x, h, blocks):
        items[x, 0, h] = [blocks[j] for j in halves[h]]
        items[x, 1, h] = [hop(v, 1) for v in items[x, 0, h]]

    def statistics(m, l, *chosen):
        for key in chosen:
            m, l = run_stats(items[key], qt, bias, m, l, scale * LOG2E, start_of[key], False)
        return m, l

    for j in range(last):
        along_x[j] = hop(along_z[j], 2)
    gathered(0, 0, along_z)
    m8, l8 = statistics(m8, l8, (0, 0, 0), (0, 1, 0))
    along_z[last], m8, l8 = tie((along_z[last], m8, l8))
    along_x[last] = hop(along_z[last], 2)
    gathered(0, 1, along_z)
    m8, l8 = statistics(m8, l8, (0, 0, 1), (0, 1, 1))
    gathered(1, 0, along_x)
    m8, l8 = statistics(m8, l8, (1, 0, 0))
    along_x[last], m8, l8 = tie((along_x[last], m8, l8))
    gathered(1, 1, along_x)
    m8, l8 = statistics(m8, l8, (1, 1, 0), (1, 0, 1))
    (local,) = run_stats(
        items[1, 1, 1], qt, bias, m8, l8, scale * LOG2E, start_of[1, 1, 1], True
    )
    lse = run_lse(model_index, [local] + [hop(local, k, "mp") for k in range(1, n_model)])

    piece, b_late, lse = tie((piece, b_in[None, :], lse))
    others = [(hop(piece, k, "mp"), hop(b_late, k, "mp")) for k in range(1, n_model)]

    qg = jnp.zeros((width_out, n_query), F32)
    sp = jnp.zeros((8, n_query), F32)
    chip_sums, crossed, z_sums = {}, {}, [None] * n_z

    def gradients(key, qg, sp, more=()):
        return run_grad(
            items[key], more, qt, queries, bias, lse, pos_col, qg, sp,
            scale, start_of[key],
        )

    siblings, crossing = {}, {}
    for h in (1, 0):
        sums, qg, sp = gradients((1, 1, h), qg, sp)
        siblings[1, h] = [hop(v, 1) for v in sums]
    for h in (1, 0):
        chip_sums[1, h], qg, sp = gradients((1, 0, h), qg, sp, siblings[1, h])
        crossing[h], qg = tie(
            ((jnp.concatenate(chip_sums[1, h], axis=0) * factors[0]).astype(F16), qg)
        )
        crossed[h] = hop(crossing[h], 2)
    for h in (1, 0):
        sums, qg, sp = gradients((0, 1, h), qg, sp)
        siblings[0, h] = [hop(v, 1) for v in sums]
    for h in (1, 0):
        crossed[h], qg = tie((crossed[h], qg))
        chip_sums[0, h], qg, sp = gradients((0, 0, h), qg, sp, siblings[0, h])
        for j in range(n_z // 2):
            over = crossed[h][j * part : (j + 1) * part].astype(F32) * growths[0]
            z_sums[h * n_z // 2 + j] = chip_sums[0, h][j] + over
    own_sum = z_sums[0]
    for j in range(n_z - 1, 0, -1):
        sent = hop((z_sums[j] * factors[1]).astype(F16), j << 2)
        own_sum = own_sum + sent.astype(F32) * growths[1]
    own_grad, others = tie((own_sum.astype(BF16), others))


    grads = [own_grad] + [hop(own_grad, k, "mp") for k in range(1, n_model)]
    item_grad, pre_grad, local_b, value = run_backward(
        model_index, jnp.stack(factors[2:]), grads, pre, hidden, item_table, w_out
    )

    width = value.shape[1]
    keep, give = (slice_at(value, (half_starts[k], 0), (half_rows, width)) for k in range(2))
    bias_steps = [1 << n for n in range(n_data.bit_length() - 1)]

    def step_bias(value, steps):
        for _ in range(min(steps, len(bias_steps))):
            bits = bias_steps.pop(0)
            value = value + hop(value, bits)
        return value

    value = (keep + hop(give.astype(F16), 1).astype(F32)).astype(F16)
    value, local_b = tie((value, step_bias(local_b, 1)))
    value, qg, sp = tie((value, qg, sp))

    item_max = n_model * units * hidden_max * W_OUT_MAX
    q_factor = LIMIT / (2.0 * item_max)
    sp1 = jnp.sum(sp, axis=0)[None, :]
    qg_parts = [
        slice_at(qg, (0, share_starts[k]), (width_out, query_part))
        for k in range(n_model)
    ]
    pos_score, query_sum = sp1, qg_parts[0]
    for k in range(1, n_model):
        sent = hop((qg_parts[k] * q_factor).astype(F16), k, "mp")
        query_sum = query_sum + sent.astype(F32) * (1.0 / q_factor)
        pos_score = pos_score + hop(sp1, k, "mp")
    loss = lse[0] * (1.0 / LOG2E) - (pos_score[0] * scale - pos_logc)
    query_grad = (query_sum * scale).T

    chips = n_data // 2
    groups = [[2 * chip + c for chip in range(chips)] for c in range(2)]

    def exchange(blocks):
        return lax.all_to_all(
            blocks, "dp", split_axis=0, concat_axis=0, axis_index_groups=groups, tiled=True
        )

    size = half_rows // chips
    pieces = exchange(value.reshape(chips, size, width))
    total = jnp.sum(pieces.astype(F32), axis=0).astype(F16)
    total, local_b, others, packed = tie((total, step_bias(local_b, 9), others, packed))
    others = [(joined(got, hop(got, 1), core_first), b) for got, b in others]
    own_half = exchange(jnp.broadcast_to(total[None], (chips, size, width)))
    own_half = own_half.reshape(half_rows, width)
    weights = [(packed, b_in[None, :])] + others
    if n_model > 2:
        turn = jnp.arange(n_model) ^ my_model
        stacks = [jnp.take(jnp.stack(group), turn, axis=0) for group in zip(*weights)]
        weights = [(stacks[0][k], stacks[1][k]) for k in range(n_model)]
    def backward(grad, weight, pre_values):
        return jnp.where(pre_values > 0.0, dot(grad, weight, NT), 0.0).astype(BF16)

    grad_table = None
    for pack, bias_units in weights:
        share_in, share_out = pack[:, :units], pack[:, units:].reshape(units, width_out)
        pre_units = dot(item_table, share_in) + bias_units
        term = dot(backward(item_grad, share_out, pre_units), share_in, NT)
        grad_table = term if grad_table is None else grad_table + term
    own_half, grad_table = tie((own_half, grad_table))
    sides = [own_half, hop(own_half, 1)]
    sides_in = [v[:, :units].astype(F32) * growths[2] for v in sides]
    sides_out = [v[:, units:].astype(F32) * growths[3] for v in sides]
    grad_w_in = joined(*sides_in, core_first)
    grad_w_out = joined(*sides_out, core_first).reshape(units, width_out)
    return (loss, query_grad, grad_w_in, local_b[0], grad_w_out, grad_table)


def solution(mesh):
    placed = (
        P("dp", None),
        P("dp", None),
        P("dp"),
        P("dp", None),
        P("dp"),
        P("dp"),
        P(None, "mp"),
        P("mp"),
        P("mp", None),
    )
    return jax.shard_map(
        per_device,
        mesh=mesh,
        in_specs=placed,
        out_specs=(
            P("dp"),
            P(("dp", "mp"), None),
            P(None, "mp"),
            P("mp"),
            P("mp", None),
            P("dp", None),
        ),
        check_vma=False,
    )
```

```python
import functools
import math

import jax
import jax.numpy as jnp
from jax import lax
from jax.experimental import pallas as pl
from jax.experimental.pallas import tpu as pltpu
from jax.sharding import PartitionSpec as P

F32 = jnp.float32
BF16 = jnp.bfloat16
F16 = jnp.float16
ABSENT = -1e30
COUNT_BASE = 128
WORD_BITS = 22
EXPONENT_BASE = 20
TABLE_MAX = 6.0
W_IN_MAX = 0.25
B_IN_MAX = 3.0
W_OUT_MAX = 0.1875
LIMIT = 32768.0
LOG2E = math.log2(math.e)
GROUP = 16
NT = (((1,), (1,)), ((), ()))
TN = (((0,), (0,)), ((), ()))


def hop(value, bits, axis="dp"):
    size = lax.axis_size(axis)
    return lax.ppermute(value, axis, [(i, i ^ bits) for i in range(size)])


def dot(a, b, dims=None, **kw):
    if dims is None:
        dims = (((1,), (0,)), ((), ()))
    return lax.dot_general(a, b, dims, preferred_element_type=F32, **kw)


def column_bias(bias_ref, first, count):
    lane = first // 128
    return bias_ref[pl.ds(first % 128, count), lane : lane + 1]


def stats_kernel(scale, base, count, last, *refs):
    items_refs, refs = refs[:count], refs[count:]
    qt_ref, bias_ref, m_in_ref, l_in_ref, m_ref, *score_refs = refs
    l_ref = None if last else score_refs.pop(0)
    block = score_refs[0].shape[0]
    old = m_in_ref[...]
    new = old
    for items_ref, score_ref in zip(items_refs, score_refs):
        score_ref[...] = dot(items_ref[0:block], qt_ref[...])
    for n, score_ref in enumerate(score_refs):
        for r in range(0, block, 8):
            bias = column_bias(bias_ref, base + n * block + r, 8)
            score = score_ref[r : r + 8] * scale + bias
            score_ref[r : r + 8] = score
            new = jnp.maximum(new, score)
    total = l_in_ref[...] * jnp.exp2(old - new)
    for score_ref in score_refs:
        for r in range(0, block, 8):
            total = total + jnp.exp2(score_ref[r : r + 8] - new)
    if last:
        top = jnp.max(new, axis=0, keepdims=True)
        m_ref[0:1] = top
        m_ref[1:2] = jnp.sum(total * jnp.exp2(new - top), axis=0, keepdims=True)
    else:
        m_ref[...] = new
        l_ref[...] = total


def in_vmem(count):
    return [pl.BlockSpec(memory_space=pltpu.VMEM)] * count


def run_stats(items, block, qt, bias, m, l, scale, base, last):
    count, nq = len(items), qt.shape[1]
    shapes = [(2, nq)] if last else [(8, nq)] * 2
    return pl.pallas_call(
        functools.partial(stats_kernel, scale, base, count, last),
        in_specs=in_vmem(count + 4),
        out_specs=in_vmem(len(shapes)),
        out_shape=[jax.ShapeDtypeStruct(shape, F32) for shape in shapes],
        scratch_shapes=[pltpu.VMEM((block, nq), F32)] * count,
        compiler_params=pltpu.CompilerParams(vmem_limit_bytes=6 << 20),
    )(*items, qt, bias, m, l)


def lse_kernel(count, index_ref, *refs):
    part_refs, (lse_ref, held_ref) = refs[:count], refs[count:]
    for k in range(count):
        held_ref[index_ref[0] ^ k] = part_refs[k][...]
    parts = [held_ref[k] for k in range(count)]
    top = functools.reduce(jnp.maximum, [p[0:1] for p in parts])
    total = functools.reduce(jnp.add, [p[1:2] * jnp.exp2(p[0:1] - top) for p in parts])
    lse_ref[...] = top + jnp.log2(total)


def run_lse(index, parts):
    nq = parts[0].shape[1]
    return pl.pallas_call(
        functools.partial(lse_kernel, len(parts)),
        in_specs=[pl.BlockSpec(memory_space=pltpu.SMEM)] + in_vmem(len(parts)),
        out_specs=in_vmem(1)[0],
        out_shape=jax.ShapeDtypeStruct((1, nq), F32),
        scratch_shapes=[pltpu.VMEM((len(parts), 2, nq), F32)],
        compiler_params=pltpu.CompilerParams(vmem_limit_bytes=2 << 20),
    )(index, *parts)


def grad_kernel(scale, base, count, add, *refs):
    items_refs, refs = refs[:count], refs[count:]
    more_refs, refs = refs[:add], refs[add:]
    qt_ref, q_ref, bias_ref, lse_ref, pos_ref, qg_in_ref, sp_in_ref, *refs = refs
    sums_refs, (qg_ref, sp_ref, *scratch) = refs[:count], refs[count:]
    score_refs, prob_refs = scratch[:count], scratch[count:]
    block, queries = score_refs[0].shape
    for items_ref, score_ref in zip(items_refs, score_refs):
        score_ref[...] = dot(items_ref[0:block], qt_ref[...])
    down = lax.broadcasted_iota(jnp.int32, (8, queries), 0)
    offset = jnp.broadcast_to(pos_ref[...], (8, queries)) - down
    lse = jnp.broadcast_to(lse_ref[...], (8, queries))
    found = sp_in_ref[...]
    for n in range(count):
        score_ref, prob_ref = score_refs[n], prob_refs[n]
        for r in range(0, block, GROUP):
            pieces = []
            for s in range(r, r + GROUP, 8):
                at = base + n * block + s
                score = score_ref[s : s + 8]
                here = offset == at
                found = found + jnp.where(here, score, 0.0)
                prob = jnp.exp2((score * (scale * LOG2E) + column_bias(bias_ref, at, 8)) - lse)
                pieces.append(jnp.where(here, prob - 1.0, prob))
            prob_ref[r : r + GROUP] = jnp.concatenate(pieces, axis=0).astype(BF16)
        sums = dot(prob_ref[...], q_ref[...]) * scale
        sums_refs[n][...] = sums + more_refs[n][...] if add else sums
        share = dot(items_refs[n][0:block], prob_ref[...], TN)
        qg_ref[...] = (qg_in_ref[...] if n == 0 else qg_ref[...]) + share
    sp_ref[...] = found


def run_grad(items, block, more, qt, q, bias, lse, pos, qg, sp, scale, base):
    count, (width, nq) = len(items), qt.shape
    before = count + len(more)
    *sums, qg, sp = pl.pallas_call(
        functools.partial(grad_kernel, scale, base, count, len(more)),
        in_specs=in_vmem(before + 7),
        out_specs=in_vmem(count + 2),
        out_shape=[jax.ShapeDtypeStruct((block, width), F32)] * count
        + [jax.ShapeDtypeStruct((width, nq), F32), jax.ShapeDtypeStruct((8, nq), F32)],
        scratch_shapes=[pltpu.VMEM((block, nq), F32)] * count
        + [pltpu.VMEM((block, nq), BF16)] * count,
        input_output_aliases={before + 5: count, before + 6: count + 1},
        compiler_params=pltpu.CompilerParams(vmem_limit_bytes=8 << 20),
    )(*items, *more, qt, q, bias, lse, pos, qg, sp)
    return sums, qg, sp


def backward_kernel(count, index_ref, factor_ref, *refs):
    grad_refs, (pre_ref, hidden_ref, emb_ref, w_out_ref) = refs[:count], refs[count : count + 4]
    grad_ref, pre_grad_ref, b_ref, *sums_refs = refs[count + 4 :]
    part = grad_refs[0].shape[0]
    for k in range(count):
        start = pl.multiple_of((index_ref[0] ^ k) * part, part)
        grad_ref[pl.ds(start, part)] = grad_refs[k][...]
    back = dot(grad_ref[...], w_out_ref[...], NT)
    pre_grad = jnp.where(pre_ref[...] > 0.0, back, 0.0).astype(BF16)
    pre_grad_ref[...] = pre_grad
    b_ref[...] = jnp.sum(pre_grad.astype(F32), axis=0, keepdims=True)
    sums_in = dot(emb_ref[...], pre_grad, TN) * factor_ref[0]
    sums_out = dot(hidden_ref[...], grad_ref[...], TN) * factor_ref[1]
    if len(sums_refs) == 1:
        units = sums_in.shape[1]
        sums_refs[0][:, :units] = sums_in
        sums_refs[0][:, units:] = sums_out
    else:
        sums_refs[0][...] = sums_in
        sums_refs[1][...] = sums_out


def run_backward(index, factors, grads, pre, hidden, emb, w_out):
    rows, units = pre.shape
    width_emb, width_out = emb.shape[1], w_out.shape[1]
    if units == width_emb:
        sums = [(width_emb, units + width_out)]
    else:
        sums = [(width_emb, units), (units, width_out)]
    grad, pre_grad, local_b, *sums = pl.pallas_call(
        functools.partial(backward_kernel, len(grads)),
        in_specs=[pl.BlockSpec(memory_space=pltpu.SMEM)] * 2 + in_vmem(len(grads) + 4),
        out_specs=in_vmem(3 + len(sums)),
        out_shape=[
            jax.ShapeDtypeStruct((rows, width_out), BF16),
            jax.ShapeDtypeStruct((rows, units), BF16),
            jax.ShapeDtypeStruct((1, units), F32),
        ]
        + [jax.ShapeDtypeStruct(shape, F32) for shape in sums],
        compiler_params=pltpu.CompilerParams(vmem_limit_bytes=12 << 20),
    )(index, factors, *grads, pre, hidden, emb, w_out)
    if len(sums) > 1:
        sums = [jnp.concatenate([sums[0], sums[1].reshape(width_emb, -1)], axis=1)]
    return grad, pre_grad, local_b, sums[0]


def joined(mine, other, first):
    return jnp.where(
        first,
        jnp.concatenate([mine, other], axis=0),
        jnp.concatenate([other, mine], axis=0),
    )


def per_device(queries, item_table, cand_row, cand_owner, cand_count, positive, w_in, b_in, w_out):
    n_data = lax.axis_size("dp")
    n_model = lax.axis_size("mp")
    n_z = n_data // 4
    me = lax.axis_index("dp")
    my_model = lax.axis_index("mp")
    n_query, width_out = queries.shape
    rows, width_emb = item_table.shape
    units = w_in.shape[1]
    part = rows // n_model
    cand_local = cand_row.shape[0]
    n_cols = n_data * part
    chunk = n_z * part // 2
    scale = 1.0 / math.sqrt(width_out)
    tie = lax.optimization_barrier
    slice_at = functools.partial(lax.dynamic_slice, allow_negative_indices=False)
    core = me & 1
    half_rows = width_emb // 2
    query_part = n_query // n_model
    starts = [(my_model ^ k) * part for k in range(n_model)]
    share_starts = [(my_model ^ k) * query_part for k in range(n_model)]
    half_starts = [(core ^ k) * half_rows for k in range(2)]
    model_index = my_model.astype(jnp.int32).reshape(1)
    core_first = core == 0

    def place(rel):
        return ((rel >> 1) & 1) * (2 * n_z) + (rel & 1) * n_z + (rel >> 2)

    def bit_of(bits):
        return (me // bits) & 1

    pre = dot(item_table, w_in) + b_in[None, :]
    hidden = jnp.maximum(pre, 0.0).astype(BF16)
    partial = dot(hidden, w_out)

    def part_of(value, k):
        return slice_at(value, (starts[k], 0), (part, value.shape[1]))

    outgoing = [part_of(partial, k) for k in range(1, n_model)]
    arrived = [hop(outgoing[k - 1], k, "mp") for k in range(1, n_model)]
    outgoing, queries, cand_row = tie((outgoing, queries, cand_row))
    qt = queries.T
    packed = jnp.concatenate([w_in, w_out.reshape(width_emb, -1)], axis=1)
    piece = slice_at(packed, (half_starts[0], 0), (half_rows, packed.shape[1]))

    largest = jnp.max(jnp.abs(queries)).astype(F32)
    exponent = jnp.floor(jnp.log2(jnp.maximum(largest, 1e-6))).astype(jnp.int32) + 1
    exponent = jnp.clip(exponent + EXPONENT_BASE, 0, 63)
    word = (cand_owner[:, 0] * rows + cand_row) * COUNT_BASE + cand_count
    word = (word + exponent * (1 << WORD_BITS))[None, :]
    words = jnp.concatenate([word, hop(word, 1)], axis=0)
    words = jnp.concatenate([words, hop(words, 2)], axis=0)

    total, arrived, qt, piece = tie((part_of(partial, 0), arrived, qt, piece))
    for other in arrived:
        total = total + other
    size = 4 * cand_local
    digits = jnp.stack([(words.reshape(size) >> shift) & 255 for shift in (0, 8, 16, 24)])
    tail_rows = -(-4 * size // (16 * width_out)) * 16
    digits = jnp.pad(digits.reshape(-1), (0, tail_rows * width_out - 4 * size))
    tail = digits.reshape(tail_rows, width_out).astype(BF16)
    payload = jnp.concatenate([total.astype(BF16), tail], axis=0)

    along_z, along_x = {0: payload}, {}
    for j in range(n_z - 1, 0, -1):
        along_z[j] = hop(payload, j << 2)
    tails = jnp.stack([along_z[j][part:] for j in range(n_z)]).reshape(n_z, -1)[:, : 4 * size]
    tails = tails.astype(jnp.int32).reshape(n_z, 4, size)
    words = tails[:, 0] + tails[:, 1] * 256 + tails[:, 2] * 65536 + tails[:, 3] * 16777216

    flat = words.reshape(-1)
    n_cand = flat.shape[0]
    q_bound = jnp.exp2((jnp.max(flat >> WORD_BITS) - EXPONENT_BASE).astype(F32))
    flat = flat & ((1 << WORD_BITS) - 1)

    hidden_max = width_emb * TABLE_MAX * W_IN_MAX + B_IN_MAX
    gradient_sum = n_data * n_query * 2.0 * scale
    bounds = [
        2 * n_query * 2.0 * scale,
        4 * n_query * 2.0 * scale,
        gradient_sum * width_out * W_OUT_MAX * TABLE_MAX,
        gradient_sum * hidden_max,
    ]
    factors = [(LIMIT / bound) / q_bound for bound in bounds]
    growths = [q_bound * (bound / LIMIT) for bound in bounds]
    row = (flat // COUNT_BASE) % rows
    column = place((flat // (COUNT_BASE * rows)) ^ me) * part + row % part
    column = jnp.where(row // part == my_model, column, -1)
    share = 1.0 / (flat % COUNT_BASE).astype(F32)
    lanes = 128
    high = (jnp.arange(n_cols // lanes)[:, None] == (column >> 7)[None, :]).astype(F32)
    low = jnp.where(jnp.arange(lanes)[:, None] == (column & 127)[None, :], share[None, :], 0.0)
    weight = dot(low, high, NT, precision=lax.Precision.HIGHEST)
    bias = jnp.where(weight > 0.0, jnp.log2(weight), ABSENT)
    bias, factors, growths, share_starts, half_starts, model_index, core_first = tie(
        (bias, factors, growths, share_starts, half_starts, model_index, core_first)
    )

    spot = ((positive // cand_local) ^ me) * cand_local + positive % cand_local
    side = 64
    table = flat.reshape(n_cand // side, side)
    digits = jnp.concatenate([table & 255, (table >> 8) & 255, table >> 16], axis=1).astype(BF16)
    picked = (jnp.arange(n_cand // side)[:, None] == (spot // side)[None, :]).astype(BF16)
    found = dot(digits, picked, TN).reshape(3, side, n_query)
    mine = jnp.arange(side)[:, None] == (spot % side)[None, :]
    digit = jnp.sum(jnp.where(mine[None], found, 0.0), axis=1).astype(jnp.int32)
    pos_word = digit[0] + digit[1] * 256 + digit[2] * 65536
    pos_row = (pos_word // COUNT_BASE) % rows
    pos_col = place((pos_word // (COUNT_BASE * rows)) ^ me) * part + pos_row % part
    pos_col = jnp.where(pos_row // part == my_model, pos_col, -1)[None, :]
    pos_logc = jnp.log((pos_word % COUNT_BASE).astype(F32))

    last = n_z - 1
    halves = [range(h * n_z // 2, (h + 1) * n_z // 2) for h in range(2)]
    start_of = {
        (x, c, h): ((x * 2 + c) * 2 + h) * chunk for x in range(2) for c in range(2) for h in range(2)
    }
    items = {}
    m8 = jnp.full((8, n_query), ABSENT, F32)
    l8 = jnp.zeros((8, n_query), F32)

    def gathered(x, h, blocks):
        items[x, 0, h] = [blocks[j] for j in halves[h]]
        items[x, 1, h] = [hop(v, 1) for v in items[x, 0, h]]

    def statistics(m, l, *chosen):
        for key in chosen:
            m, l = run_stats(items[key], part, qt, bias, m, l, scale * LOG2E, start_of[key], False)
        return m, l

    for j in range(n_z):
        along_x[j] = hop(along_z[j], 2)
    gathered(0, 0, along_z)
    m8, l8 = statistics(m8, l8, (0, 0, 0), (0, 1, 0))
    gathered(0, 1, along_z)
    m8, l8 = statistics(m8, l8, (0, 0, 1), (0, 1, 1))
    gathered(1, 0, along_x)
    m8, l8 = statistics(m8, l8, (1, 0, 0))
    along_x[last], m8, l8 = tie((along_x[last], m8, l8))
    gathered(1, 1, along_x)
    m8, l8 = statistics(m8, l8, (1, 1, 0), (1, 0, 1))
    (local,) = run_stats(
        items[1, 1, 1], part, qt, bias, m8, l8, scale * LOG2E, start_of[1, 1, 1], True
    )
    lse = run_lse(model_index, [local] + [hop(local, k, "mp") for k in range(1, n_model)])

    piece, b_late, lse = tie((piece, b_in[None, :], lse))
    others = [(hop(piece, k, "mp"), hop(b_late, k, "mp")) for k in range(1, n_model)]

    qg = jnp.zeros((width_out, n_query), F32)
    sp = jnp.zeros((8, n_query), F32)
    chip_sums, crossed, z_sums = {}, {}, [None] * n_z

    def gradients(key, qg, sp, more=()):
        return run_grad(
            items[key], part, more, qt, queries, bias, lse, pos_col, qg, sp,
            scale, start_of[key],
        )

    siblings, crossing = {}, {}
    for h in (1, 0):
        sums, qg, sp = gradients((1, 1, h), qg, sp)
        siblings[1, h] = [hop(v, 1) for v in sums]
    for h in (1, 0):
        chip_sums[1, h], qg, sp = gradients((1, 0, h), qg, sp, siblings[1, h])
        crossing[h], qg = tie(
            ((jnp.concatenate(chip_sums[1, h], axis=0) * factors[0]).astype(F16), qg)
        )
        crossed[h] = hop(crossing[h], 2)
    for h in (1, 0):
        sums, qg, sp = gradients((0, 1, h), qg, sp)
        siblings[0, h] = [hop(v, 1) for v in sums]
    for h in (1, 0):
        crossed[h], qg = tie((crossed[h], qg))
        chip_sums[0, h], qg, sp = gradients((0, 0, h), qg, sp, siblings[0, h])
        for j in range(n_z // 2):
            over = crossed[h][j * part : (j + 1) * part].astype(F32) * growths[0]
            z_sums[h * n_z // 2 + j] = chip_sums[0, h][j] + over
    own_sum = z_sums[0]
    for j in range(n_z - 1, 0, -1):
        sent = hop((z_sums[j] * factors[1]).astype(F16), j << 2)
        own_sum = own_sum + sent.astype(F32) * growths[1]
    own_grad, others = tie((own_sum.astype(BF16), others))


    grads = [own_grad] + [hop(own_grad, k, "mp") for k in range(1, n_model)]
    item_grad, pre_grad, local_b, value = run_backward(
        model_index, jnp.stack(factors[2:]), grads, pre, hidden, item_table, w_out
    )

    width = value.shape[1]
    keep, give = (slice_at(value, (half_starts[k], 0), (half_rows, width)) for k in range(2))
    bias_steps = [1 << n for n in range(n_data.bit_length() - 1)]

    def step_bias(value, steps):
        for _ in range(min(steps, len(bias_steps))):
            bits = bias_steps.pop(0)
            value = value + hop(value, bits)
        return value

    value = (keep + hop(give.astype(F16), 1).astype(F32)).astype(F16)
    value, local_b = tie((value, step_bias(local_b, 1)))
    chips = n_data // 2
    groups = [[2 * chip + c for chip in range(chips)] for c in range(2)]

    def exchange(blocks):
        return lax.all_to_all(
            blocks, "dp", split_axis=0, concat_axis=0, axis_index_groups=groups, tiled=True
        )

    size = half_rows // chips
    value, others, packed = tie((value, others, packed))
    others = [(joined(got, hop(got, 1), core_first), b) for got, b in others]
    weights = [(packed, b_in[None, :])] + others
    if n_model > 2:
        turn = jnp.arange(n_model) ^ my_model
        stacks = [jnp.take(jnp.stack(group), turn, axis=0) for group in zip(*weights)]
        weights = [(stacks[0][k], stacks[1][k]) for k in range(n_model)]
    def backward(grad, weight, pre_values):
        return jnp.where(pre_values > 0.0, dot(grad, weight, NT), 0.0).astype(BF16)

    grad_table = None
    for pack, bias_units in weights:
        share_in, share_out = pack[:, :units], pack[:, units:].reshape(units, width_out)
        pre_units = dot(item_table, share_in) + bias_units
        term = dot(backward(item_grad, share_out, pre_units), share_in, NT)
        grad_table = term if grad_table is None else grad_table + term

    pieces = exchange(value.reshape(chips, size, width))
    pieces, grad_table = tie((pieces, grad_table))
    total = jnp.sum(pieces.astype(F32), axis=0).astype(F16)
    total, local_b = tie((total, step_bias(local_b, 2)))
    own_half = exchange(jnp.broadcast_to(total[None], (chips, size, width)))
    own_half = own_half.reshape(half_rows, width)
    local_b = step_bias(local_b, 9)

    local_b, qg, sp = tie((local_b, qg, sp))

    item_max = n_model * units * hidden_max * W_OUT_MAX
    q_factor = LIMIT / (2.0 * item_max)
    sp1 = jnp.sum(sp, axis=0)[None, :]
    qg_parts = [
        slice_at(qg, (0, share_starts[k]), (width_out, query_part))
        for k in range(n_model)
    ]
    pos_score, query_sum = sp1, qg_parts[0]
    for k in range(1, n_model):
        sent = hop((qg_parts[k] * q_factor).astype(F16), k, "mp")
        query_sum = query_sum + sent.astype(F32) * (1.0 / q_factor)
        pos_score = pos_score + hop(sp1, k, "mp")
    loss = lse[0] * (1.0 / LOG2E) - (pos_score[0] * scale - pos_logc)
    query_grad = (query_sum * scale).T

    sides = [own_half, hop(own_half, 1)]
    sides_in = [v[:, :units].astype(F32) * growths[2] for v in sides]
    sides_out = [v[:, units:].astype(F32) * growths[3] for v in sides]
    grad_w_in = joined(*sides_in, core_first)
    grad_w_out = joined(*sides_out, core_first).reshape(units, width_out)
    return (loss, query_grad, grad_w_in, local_b[0], grad_w_out, grad_table)


def solution(mesh):
    placed = (
        P("dp", None),
        P("dp", None),
        P("dp"),
        P("dp", None),
        P("dp"),
        P("dp"),
        P(None, "mp"),
        P("mp"),
        P("mp", None),
    )
    return jax.shard_map(
        per_device,
        mesh=mesh,
        in_specs=placed,
        out_specs=(
            P("dp"),
            P(("dp", "mp"), None),
            P(None, "mp"),
            P("mp"),
            P("mp", None),
            P("dp", None),
        ),
        check_vma=False,
    )
```

```python
import functools
import math

import jax
import jax.numpy as jnp
from jax import lax
from jax.experimental import pallas as pl
from jax.experimental.pallas import tpu as pltpu
from jax.sharding import PartitionSpec as P

F32 = jnp.float32
BF16 = jnp.bfloat16
F16 = jnp.float16
ABSENT = -1e30
COUNT_BASE = 128
WORD_BITS = 22
EXPONENT_BASE = 20
TABLE_MAX = 6.0
W_IN_MAX = 0.25
B_IN_MAX = 3.0
W_OUT_MAX = 0.1875
LIMIT = 32768.0
LOG2E = math.log2(math.e)
GROUP = 16
NT = (((1,), (1,)), ((), ()))
TN = (((0,), (0,)), ((), ()))


def hop(value, bits, axis="dp"):
    size = lax.axis_size(axis)
    return lax.ppermute(value, axis, [(i, i ^ bits) for i in range(size)])


def dot(a, b, dims=None, **kw):
    if dims is None:
        dims = (((1,), (0,)), ((), ()))
    return lax.dot_general(a, b, dims, preferred_element_type=F32, **kw)


def column_bias(bias_ref, first, count):
    lane = first // 128
    return bias_ref[pl.ds(first % 128, count), lane : lane + 1]


def stats_kernel(scale, base, count, last, *refs):
    items_refs, refs = refs[:count], refs[count:]
    qt_ref, bias_ref, m_in_ref, l_in_ref, m_ref, *score_refs = refs
    l_ref = None if last else score_refs.pop(0)
    block = score_refs[0].shape[0]
    old = m_in_ref[...]
    new = old
    for items_ref, score_ref in zip(items_refs, score_refs):
        score_ref[...] = dot(items_ref[0:block], qt_ref[...])
    for n, score_ref in enumerate(score_refs):
        for r in range(0, block, 8):
            bias = column_bias(bias_ref, base + n * block + r, 8)
            score = score_ref[r : r + 8] * scale + bias
            score_ref[r : r + 8] = score
            new = jnp.maximum(new, score)
    total = l_in_ref[...] * jnp.exp2(old - new)
    for score_ref in score_refs:
        for r in range(0, block, 8):
            total = total + jnp.exp2(score_ref[r : r + 8] - new)
    if last:
        top = jnp.max(new, axis=0, keepdims=True)
        m_ref[0:1] = top
        m_ref[1:2] = jnp.sum(total * jnp.exp2(new - top), axis=0, keepdims=True)
    else:
        m_ref[...] = new
        l_ref[...] = total


def in_vmem(count):
    return [pl.BlockSpec(memory_space=pltpu.VMEM)] * count


def run_stats(items, block, qt, bias, m, l, scale, base, last):
    count, nq = len(items), qt.shape[1]
    shapes = [(2, nq)] if last else [(8, nq)] * 2
    return pl.pallas_call(
        functools.partial(stats_kernel, scale, base, count, last),
        in_specs=in_vmem(count + 4),
        out_specs=in_vmem(len(shapes)),
        out_shape=[jax.ShapeDtypeStruct(shape, F32) for shape in shapes],
        scratch_shapes=[pltpu.VMEM((block, nq), F32)] * count,
        compiler_params=pltpu.CompilerParams(vmem_limit_bytes=6 << 20),
    )(*items, qt, bias, m, l)


def lse_kernel(count, index_ref, *refs):
    part_refs, (lse_ref, held_ref) = refs[:count], refs[count:]
    for k in range(count):
        held_ref[index_ref[0] ^ k] = part_refs[k][...]
    parts = [held_ref[k] for k in range(count)]
    top = functools.reduce(jnp.maximum, [p[0:1] for p in parts])
    total = functools.reduce(jnp.add, [p[1:2] * jnp.exp2(p[0:1] - top) for p in parts])
    lse_ref[...] = top + jnp.log2(total)


def run_lse(index, parts):
    nq = parts[0].shape[1]
    return pl.pallas_call(
        functools.partial(lse_kernel, len(parts)),
        in_specs=[pl.BlockSpec(memory_space=pltpu.SMEM)] + in_vmem(len(parts)),
        out_specs=in_vmem(1)[0],
        out_shape=jax.ShapeDtypeStruct((1, nq), F32),
        scratch_shapes=[pltpu.VMEM((len(parts), 2, nq), F32)],
        compiler_params=pltpu.CompilerParams(vmem_limit_bytes=2 << 20),
    )(index, *parts)


def grad_kernel(scale, base, count, add, *refs):
    items_refs, refs = refs[:count], refs[count:]
    more_refs, refs = refs[:add], refs[add:]
    qt_ref, q_ref, bias_ref, lse_ref, pos_ref, qg_in_ref, sp_in_ref, *refs = refs
    sums_refs, (qg_ref, sp_ref, *scratch) = refs[:count], refs[count:]
    score_refs, prob_refs = scratch[:count], scratch[count:]
    block, queries = score_refs[0].shape
    for items_ref, score_ref in zip(items_refs, score_refs):
        score_ref[...] = dot(items_ref[0:block], qt_ref[...])
    down = lax.broadcasted_iota(jnp.int32, (8, queries), 0)
    offset = jnp.broadcast_to(pos_ref[...], (8, queries)) - down
    lse = jnp.broadcast_to(lse_ref[...], (8, queries))
    found = sp_in_ref[...]
    for n in range(count):
        score_ref, prob_ref = score_refs[n], prob_refs[n]
        for r in range(0, block, GROUP):
            pieces = []
            for s in range(r, r + GROUP, 8):
                at = base + n * block + s
                score = score_ref[s : s + 8]
                here = offset == at
                found = found + jnp.where(here, score, 0.0)
                prob = jnp.exp2((score * (scale * LOG2E) + column_bias(bias_ref, at, 8)) - lse)
                pieces.append(jnp.where(here, prob - 1.0, prob))
            prob_ref[r : r + GROUP] = jnp.concatenate(pieces, axis=0).astype(BF16)
        sums = dot(prob_ref[...], q_ref[...]) * scale
        sums_refs[n][...] = sums + more_refs[n][...] if add else sums
        share = dot(items_refs[n][0:block], prob_ref[...], TN)
        qg_ref[...] = (qg_in_ref[...] if n == 0 else qg_ref[...]) + share
    sp_ref[...] = found


def run_grad(items, block, more, qt, q, bias, lse, pos, qg, sp, scale, base):
    count, (width, nq) = len(items), qt.shape
    before = count + len(more)
    *sums, qg, sp = pl.pallas_call(
        functools.partial(grad_kernel, scale, base, count, len(more)),
        in_specs=in_vmem(before + 7),
        out_specs=in_vmem(count + 2),
        out_shape=[jax.ShapeDtypeStruct((block, width), F32)] * count
        + [jax.ShapeDtypeStruct((width, nq), F32), jax.ShapeDtypeStruct((8, nq), F32)],
        scratch_shapes=[pltpu.VMEM((block, nq), F32)] * count
        + [pltpu.VMEM((block, nq), BF16)] * count,
        input_output_aliases={before + 5: count, before + 6: count + 1},
        compiler_params=pltpu.CompilerParams(vmem_limit_bytes=8 << 20),
    )(*items, *more, qt, q, bias, lse, pos, qg, sp)
    return sums, qg, sp


def backward_kernel(count, index_ref, factor_ref, *refs):
    grad_refs, (pre_ref, hidden_ref, emb_ref, w_out_ref) = refs[:count], refs[count : count + 4]
    grad_ref, pre_grad_ref, b_ref, *sums_refs = refs[count + 4 :]
    part = grad_refs[0].shape[0]
    for k in range(count):
        start = pl.multiple_of((index_ref[0] ^ k) * part, part)
        grad_ref[pl.ds(start, part)] = grad_refs[k][...]
    back = dot(grad_ref[...], w_out_ref[...], NT)
    pre_grad = jnp.where(pre_ref[...] > 0.0, back, 0.0).astype(BF16)
    pre_grad_ref[...] = pre_grad
    b_ref[...] = jnp.sum(pre_grad.astype(F32), axis=0, keepdims=True)
    sums_in = dot(emb_ref[...], pre_grad, TN) * factor_ref[0]
    sums_out = dot(hidden_ref[...], grad_ref[...], TN) * factor_ref[1]
    if len(sums_refs) == 1:
        units = sums_in.shape[1]
        sums_refs[0][:, :units] = sums_in
        sums_refs[0][:, units:] = sums_out
    else:
        sums_refs[0][...] = sums_in
        sums_refs[1][...] = sums_out


def run_backward(index, factors, grads, pre, hidden, emb, w_out):
    rows, units = pre.shape
    width_emb, width_out = emb.shape[1], w_out.shape[1]
    if units == width_emb:
        sums = [(width_emb, units + width_out)]
    else:
        sums = [(width_emb, units), (units, width_out)]
    grad, pre_grad, local_b, *sums = pl.pallas_call(
        functools.partial(backward_kernel, len(grads)),
        in_specs=[pl.BlockSpec(memory_space=pltpu.SMEM)] * 2 + in_vmem(len(grads) + 4),
        out_specs=in_vmem(3 + len(sums)),
        out_shape=[
            jax.ShapeDtypeStruct((rows, width_out), BF16),
            jax.ShapeDtypeStruct((rows, units), BF16),
            jax.ShapeDtypeStruct((1, units), F32),
        ]
        + [jax.ShapeDtypeStruct(shape, F32) for shape in sums],
        compiler_params=pltpu.CompilerParams(vmem_limit_bytes=12 << 20),
    )(index, factors, *grads, pre, hidden, emb, w_out)
    if len(sums) > 1:
        sums = [jnp.concatenate([sums[0], sums[1].reshape(width_emb, -1)], axis=1)]
    return grad, pre_grad, local_b, sums[0]


def joined(mine, other, first):
    return jnp.where(
        first,
        jnp.concatenate([mine, other], axis=0),
        jnp.concatenate([other, mine], axis=0),
    )


def per_device(queries, item_table, cand_row, cand_owner, cand_count, positive, w_in, b_in, w_out):
    n_data = lax.axis_size("dp")
    n_model = lax.axis_size("mp")
    n_z = n_data // 4
    me = lax.axis_index("dp")
    my_model = lax.axis_index("mp")
    n_query, width_out = queries.shape
    rows, width_emb = item_table.shape
    units = w_in.shape[1]
    part = rows // n_model
    cand_local = cand_row.shape[0]
    n_cols = n_data * part
    chunk = n_z * part // 2
    scale = 1.0 / math.sqrt(width_out)
    tie = lax.optimization_barrier
    slice_at = functools.partial(lax.dynamic_slice, allow_negative_indices=False)
    core = me & 1
    half_rows = width_emb // 2
    query_part = n_query // n_model
    starts = [(my_model ^ k) * part for k in range(n_model)]
    share_starts = [(my_model ^ k) * query_part for k in range(n_model)]
    half_starts = [(core ^ k) * half_rows for k in range(2)]
    model_index = my_model.astype(jnp.int32).reshape(1)
    core_first = core == 0

    def place(rel):
        return ((rel >> 1) & 1) * (2 * n_z) + (rel & 1) * n_z + (rel >> 2)

    def bit_of(bits):
        return (me // bits) & 1

    pre = dot(item_table, w_in) + b_in[None, :]
    hidden = jnp.maximum(pre, 0.0).astype(BF16)
    partial = dot(hidden, w_out)

    def part_of(value, k):
        return slice_at(value, (starts[k], 0), (part, value.shape[1]))

    outgoing = [part_of(partial, k) for k in range(1, n_model)]
    arrived = [hop(outgoing[k - 1], k, "mp") for k in range(1, n_model)]
    outgoing, queries, cand_row = tie((outgoing, queries, cand_row))
    qt = queries.T
    packed = jnp.concatenate([w_in, w_out.reshape(width_emb, -1)], axis=1)
    piece = slice_at(packed, (half_starts[0], 0), (half_rows, packed.shape[1]))

    largest = jnp.max(jnp.abs(queries)).astype(F32)
    exponent = jnp.floor(jnp.log2(jnp.maximum(largest, 1e-6))).astype(jnp.int32) + 1
    exponent = jnp.clip(exponent + EXPONENT_BASE, 0, 63)
    word = (cand_owner[:, 0] * rows + cand_row) * COUNT_BASE + cand_count
    word = (word + exponent * (1 << WORD_BITS))[None, :]
    words = jnp.concatenate([word, hop(word, 1)], axis=0)
    words = jnp.concatenate([words, hop(words, 2)], axis=0)

    total, arrived, qt, piece = tie((part_of(partial, 0), arrived, qt, piece))
    for other in arrived:
        total = total + other
    size = 4 * cand_local
    digits = jnp.stack([(words.reshape(size) >> shift) & 255 for shift in (0, 8, 16, 24)])
    tail_rows = -(-4 * size // (16 * width_out)) * 16
    digits = jnp.pad(digits.reshape(-1), (0, tail_rows * width_out - 4 * size))
    tail = digits.reshape(tail_rows, width_out).astype(BF16)
    payload = jnp.concatenate([total.astype(BF16), tail], axis=0)

    along_z, along_x = {0: payload}, {}
    for j in range(n_z - 1, 0, -1):
        along_z[j] = hop(payload, j << 2)
    tails = jnp.stack([along_z[j][part:] for j in range(n_z)]).reshape(n_z, -1)[:, : 4 * size]
    tails = tails.astype(jnp.int32).reshape(n_z, 4, size)
    words = tails[:, 0] + tails[:, 1] * 256 + tails[:, 2] * 65536 + tails[:, 3] * 16777216

    flat = words.reshape(-1)
    n_cand = flat.shape[0]
    q_bound = jnp.exp2((jnp.max(flat >> WORD_BITS) - EXPONENT_BASE).astype(F32))
    flat = flat & ((1 << WORD_BITS) - 1)

    hidden_max = width_emb * TABLE_MAX * W_IN_MAX + B_IN_MAX
    gradient_sum = n_data * n_query * 2.0 * scale
    bounds = [
        2 * n_query * 2.0 * scale,
        4 * n_query * 2.0 * scale,
        gradient_sum * width_out * W_OUT_MAX * TABLE_MAX,
        gradient_sum * hidden_max,
    ]
    factors = [(LIMIT / bound) / q_bound for bound in bounds]
    growths = [q_bound * (bound / LIMIT) for bound in bounds]
    row = (flat // COUNT_BASE) % rows
    column = place((flat // (COUNT_BASE * rows)) ^ me) * part + row % part
    column = jnp.where(row // part == my_model, column, -1)
    share = 1.0 / (flat % COUNT_BASE).astype(F32)
    lanes = 128
    high = (jnp.arange(n_cols // lanes)[:, None] == (column >> 7)[None, :]).astype(F32)
    low = jnp.where(jnp.arange(lanes)[:, None] == (column & 127)[None, :], share[None, :], 0.0)
    weight = dot(low, high, NT, precision=lax.Precision.HIGHEST)
    bias = jnp.where(weight > 0.0, jnp.log2(weight), ABSENT)
    bias, factors, growths, share_starts, half_starts, model_index, core_first = tie(
        (bias, factors, growths, share_starts, half_starts, model_index, core_first)
    )

    spot = ((positive // cand_local) ^ me) * cand_local + positive % cand_local
    side = 64
    table = flat.reshape(n_cand // side, side)
    digits = jnp.concatenate([table & 255, (table >> 8) & 255, table >> 16], axis=1).astype(BF16)
    picked = (jnp.arange(n_cand // side)[:, None] == (spot // side)[None, :]).astype(BF16)
    found = dot(digits, picked, TN).reshape(3, side, n_query)
    mine = jnp.arange(side)[:, None] == (spot % side)[None, :]
    digit = jnp.sum(jnp.where(mine[None], found, 0.0), axis=1).astype(jnp.int32)
    pos_word = digit[0] + digit[1] * 256 + digit[2] * 65536
    pos_row = (pos_word // COUNT_BASE) % rows
    pos_col = place((pos_word // (COUNT_BASE * rows)) ^ me) * part + pos_row % part
    pos_col = jnp.where(pos_row // part == my_model, pos_col, -1)[None, :]
    pos_logc = jnp.log((pos_word % COUNT_BASE).astype(F32))

    halves = [range(h * n_z // 2, (h + 1) * n_z // 2) for h in range(2)]
    start_of = {
        (x, c, h): ((x * 2 + c) * 2 + h) * chunk for x in range(2) for c in range(2) for h in range(2)
    }
    items = {}
    m8 = jnp.full((8, n_query), ABSENT, F32)
    l8 = jnp.zeros((8, n_query), F32)

    def gathered(x, h, blocks):
        items[x, 0, h] = [blocks[j] for j in halves[h]]
        items[x, 1, h] = [hop(v, 1) for v in items[x, 0, h]]

    def statistics(m, l, *chosen):
        for key in chosen:
            m, l = run_stats(items[key], part, qt, bias, m, l, scale * LOG2E, start_of[key], False)
        return m, l

    for j in range(n_z):
        along_x[j] = hop(along_z[j], 2)
    others = [(hop(piece, k, "mp"), hop(b_in[None, :], k, "mp")) for k in range(1, n_model)]
    gathered(0, 0, along_z)
    gathered(0, 1, along_z)
    near = {key: items[key] for key in ((0, 1, 0), (0, 1, 1))}
    along_x, bias, others, near = tie((along_x, bias, others, near))
    items.update(near)
    m8, l8 = statistics(m8, l8, (0, 0, 0), (0, 1, 0))
    m8, l8 = statistics(m8, l8, (0, 0, 1), (0, 1, 1))
    gathered(1, 0, along_x)
    m8, l8 = statistics(m8, l8, (1, 0, 0))
    gathered(1, 1, along_x)
    m8, l8 = statistics(m8, l8, (1, 1, 0), (1, 0, 1))
    (local,) = run_stats(
        items[1, 1, 1], part, qt, bias, m8, l8, scale * LOG2E, start_of[1, 1, 1], True
    )
    distant = [hop(local, k, "mp") for k in range(1, n_model)]
    others = [(joined(got, hop(got, 1), core_first), b) for got, b in others]
    weights = [(packed, b_in[None, :])] + others
    if n_model > 2:
        turn = jnp.arange(n_model) ^ my_model
        stacks = [jnp.take(jnp.stack(group), turn, axis=0) for group in zip(*weights)]
        weights = [(stacks[0][k], stacks[1][k]) for k in range(n_model)]
    weights = [(w[:, :units], w[:, units:].reshape(units, width_out), b) for w, b in weights]
    masks = [dot(item_table, share_in) + b > 0.0 for share_in, _, b in weights]
    distant, weights, masks = tie((distant, weights, masks))
    lse = run_lse(model_index, [local] + distant)

    qg = jnp.zeros((width_out, n_query), F32)
    sp = jnp.zeros((8, n_query), F32)
    chip_sums, crossed, z_sums = {}, {}, [None] * n_z

    def gradients(key, qg, sp, more=()):
        return run_grad(
            items[key], part, more, qt, queries, bias, lse, pos_col, qg, sp,
            scale, start_of[key],
        )

    siblings, crossing = {}, {}
    for h in (1, 0):
        sums, qg, sp = gradients((1, 1, h), qg, sp)
        siblings[1, h] = [hop(v, 1) for v in sums]
    for h in (1, 0):
        chip_sums[1, h], qg, sp = gradients((1, 0, h), qg, sp, siblings[1, h])
        crossing[h], qg = tie(
            ((jnp.concatenate(chip_sums[1, h], axis=0) * factors[0]).astype(F16), qg)
        )
        crossed[h] = hop(crossing[h], 2)
    for h in (1, 0):
        sums, qg, sp = gradients((0, 1, h), qg, sp)
        siblings[0, h] = [hop(v, 1) for v in sums]
    for h in (1, 0):
        crossed[h], qg = tie((crossed[h], qg))
        chip_sums[0, h], qg, sp = gradients((0, 0, h), qg, sp, siblings[0, h])
        for j in range(n_z // 2):
            over = crossed[h][j * part : (j + 1) * part].astype(F32) * growths[0]
            z_sums[h * n_z // 2 + j] = chip_sums[0, h][j] + over
    own_sum = z_sums[0]
    for j in range(n_z - 1, 0, -1):
        sent = hop((z_sums[j] * factors[1]).astype(F16), j << 2)
        own_sum = own_sum + sent.astype(F32) * growths[1]
    own_grad = own_sum.astype(BF16)


    grads = [own_grad] + [hop(own_grad, k, "mp") for k in range(1, n_model)]
    item_grad, pre_grad, local_b, value = run_backward(
        model_index, jnp.stack(factors[2:]), grads, pre, hidden, item_table, w_out
    )

    width = value.shape[1]
    keep, give = (slice_at(value, (half_starts[k], 0), (half_rows, width)) for k in range(2))
    bias_steps = [1 << n for n in range(n_data.bit_length() - 1)]

    def step_bias(value, steps):
        for _ in range(min(steps, len(bias_steps))):
            bits = bias_steps.pop(0)
            value = value + hop(value, bits)
        return value

    value = (keep + hop(give.astype(F16), 1).astype(F32)).astype(F16)
    value, local_b = tie((value, step_bias(local_b, 1)))
    chips = n_data // 2
    groups = [[2 * chip + c for chip in range(chips)] for c in range(2)]

    def exchange(blocks):
        return lax.all_to_all(
            blocks, "dp", split_axis=0, concat_axis=0, axis_index_groups=groups, tiled=True
        )

    size = half_rows // chips
    grad_table = None
    for (share_in, share_out, _), mask in zip(weights, masks):
        back = jnp.where(mask, dot(item_grad, share_out, NT), 0.0).astype(BF16)
        term = dot(back, share_in, NT)
        grad_table = term if grad_table is None else grad_table + term

    pieces = exchange(value.reshape(chips, size, width))
    pieces, grad_table = tie((pieces, grad_table))
    total = jnp.sum(pieces.astype(F32), axis=0).astype(F16)
    total, local_b = tie((total, step_bias(local_b, 9)))
    own_half = exchange(jnp.broadcast_to(total[None], (chips, size, width)))
    own_half = own_half.reshape(half_rows, width)

    local_b, qg, sp = tie((local_b, qg, sp))

    item_max = n_model * units * hidden_max * W_OUT_MAX
    q_factor = LIMIT / (2.0 * item_max)
    sp1 = jnp.sum(sp, axis=0)[None, :]
    qg_parts = [
        slice_at(qg, (0, share_starts[k]), (width_out, query_part))
        for k in range(n_model)
    ]
    pos_score, query_sum = sp1, qg_parts[0]
    for k in range(1, n_model):
        sent = hop((qg_parts[k] * q_factor).astype(F16), k, "mp")
        query_sum = query_sum + sent.astype(F32) * (1.0 / q_factor)
        pos_score = pos_score + hop(sp1, k, "mp")
    loss = lse[0] * (1.0 / LOG2E) - (pos_score[0] * scale - pos_logc)
    query_grad = (query_sum * scale).T

    sides = [own_half, hop(own_half, 1)]
    sides_in = [v[:, :units].astype(F32) * growths[2] for v in sides]
    sides_out = [v[:, units:].astype(F32) * growths[3] for v in sides]
    grad_w_in = joined(*sides_in, core_first)
    grad_w_out = joined(*sides_out, core_first).reshape(units, width_out)
    return (loss, query_grad, grad_w_in, local_b[0], grad_w_out, grad_table)


def solution(mesh):
    placed = (
        P("dp", None),
        P("dp", None),
        P("dp"),
        P("dp", None),
        P("dp"),
        P("dp"),
        P(None, "mp"),
        P("mp"),
        P("mp", None),
    )
    return jax.shard_map(
        per_device,
        mesh=mesh,
        in_specs=placed,
        out_specs=(
            P("dp"),
            P(("dp", "mp"), None),
            P(None, "mp"),
            P("mp"),
            P("mp", None),
            P("dp", None),
        ),
        check_vma=False,
    )
```

```python
import functools
import math

import jax
import jax.numpy as jnp
from jax import lax
from jax.experimental import pallas as pl
from jax.experimental.pallas import tpu as pltpu
from jax.sharding import PartitionSpec as P

F32 = jnp.float32
BF16 = jnp.bfloat16
F16 = jnp.float16
ABSENT = -1e30
COUNT_BASE = 128
WORD_BITS = 22
EXPONENT_BASE = 20
TABLE_MAX = 6.0
W_IN_MAX = 0.25
B_IN_MAX = 3.0
W_OUT_MAX = 0.1875
LIMIT = 32768.0
LOG2E = math.log2(math.e)
GROUP = 16
NT = (((1,), (1,)), ((), ()))
TN = (((0,), (0,)), ((), ()))


def hop(value, bits, axis="dp"):
    size = lax.axis_size(axis)
    return lax.ppermute(value, axis, [(i, i ^ bits) for i in range(size)])


def dot(a, b, dims=None, **kw):
    if dims is None:
        dims = (((1,), (0,)), ((), ()))
    return lax.dot_general(a, b, dims, preferred_element_type=F32, **kw)


def column_bias(bias_ref, first, count):
    lane = first // 128
    return bias_ref[pl.ds(first % 128, count), lane : lane + 1]


def stats_kernel(scale, base, count, last, *refs):
    items_refs, refs = refs[:count], refs[count:]
    qt_ref, bias_ref, m_in_ref, l_in_ref, m_ref, *score_refs = refs
    l_ref = None if last else score_refs.pop(0)
    block = score_refs[0].shape[0]
    old = m_in_ref[...]
    new = old
    for items_ref, score_ref in zip(items_refs, score_refs):
        score_ref[...] = dot(items_ref[0:block], qt_ref[...])
    for n, score_ref in enumerate(score_refs):
        for r in range(0, block, 8):
            bias = column_bias(bias_ref, base + n * block + r, 8)
            score = score_ref[r : r + 8] * scale + bias
            score_ref[r : r + 8] = score
            new = jnp.maximum(new, score)
    total = l_in_ref[...] * jnp.exp2(old - new)
    for score_ref in score_refs:
        for r in range(0, block, 8):
            total = total + jnp.exp2(score_ref[r : r + 8] - new)
    if last:
        top = jnp.max(new, axis=0, keepdims=True)
        m_ref[0:1] = top
        m_ref[1:2] = jnp.sum(total * jnp.exp2(new - top), axis=0, keepdims=True)
    else:
        m_ref[...] = new
        l_ref[...] = total


def in_vmem(count):
    return [pl.BlockSpec(memory_space=pltpu.VMEM)] * count


def run_stats(items, block, qt, bias, m, l, scale, base, last):
    count, nq = len(items), qt.shape[1]
    shapes = [(2, nq)] if last else [(8, nq)] * 2
    return pl.pallas_call(
        functools.partial(stats_kernel, scale, base, count, last),
        in_specs=in_vmem(count + 4),
        out_specs=in_vmem(len(shapes)),
        out_shape=[jax.ShapeDtypeStruct(shape, F32) for shape in shapes],
        scratch_shapes=[pltpu.VMEM((block, nq), F32)] * count,
        compiler_params=pltpu.CompilerParams(vmem_limit_bytes=6 << 20),
    )(*items, qt, bias, m, l)


def lse_kernel(count, index_ref, *refs):
    part_refs, (lse_ref, held_ref) = refs[:count], refs[count:]
    for k in range(count):
        held_ref[index_ref[0] ^ k] = part_refs[k][...]
    parts = [held_ref[k] for k in range(count)]
    top = functools.reduce(jnp.maximum, [p[0:1] for p in parts])
    total = functools.reduce(jnp.add, [p[1:2] * jnp.exp2(p[0:1] - top) for p in parts])
    lse_ref[...] = top + jnp.log2(total)


def run_lse(index, parts):
    nq = parts[0].shape[1]
    return pl.pallas_call(
        functools.partial(lse_kernel, len(parts)),
        in_specs=[pl.BlockSpec(memory_space=pltpu.SMEM)] + in_vmem(len(parts)),
        out_specs=in_vmem(1)[0],
        out_shape=jax.ShapeDtypeStruct((1, nq), F32),
        scratch_shapes=[pltpu.VMEM((len(parts), 2, nq), F32)],
        compiler_params=pltpu.CompilerParams(vmem_limit_bytes=2 << 20),
    )(index, *parts)


def grad_kernel(scale, base, count, add, *refs):
    items_refs, refs = refs[:count], refs[count:]
    more_refs, refs = refs[:add], refs[add:]
    qt_ref, q_ref, bias_ref, lse_ref, pos_ref, qg_in_ref, sp_in_ref, *refs = refs
    sums_refs, (qg_ref, sp_ref, *scratch) = refs[:count], refs[count:]
    score_refs, prob_refs = scratch[:count], scratch[count:]
    block, queries = score_refs[0].shape
    for items_ref, score_ref in zip(items_refs, score_refs):
        score_ref[...] = dot(items_ref[0:block], qt_ref[...])
    down = lax.broadcasted_iota(jnp.int32, (8, queries), 0)
    offset = jnp.broadcast_to(pos_ref[...], (8, queries)) - down
    lse = jnp.broadcast_to(lse_ref[...], (8, queries))
    found = sp_in_ref[...]
    for n in range(count):
        score_ref, prob_ref = score_refs[n], prob_refs[n]
        for r in range(0, block, GROUP):
            pieces = []
            for s in range(r, r + GROUP, 8):
                at = base + n * block + s
                score = score_ref[s : s + 8]
                here = offset == at
                found = found + jnp.where(here, score, 0.0)
                prob = jnp.exp2((score * (scale * LOG2E) + column_bias(bias_ref, at, 8)) - lse)
                pieces.append(jnp.where(here, prob - 1.0, prob))
            prob_ref[r : r + GROUP] = jnp.concatenate(pieces, axis=0).astype(BF16)
        sums = dot(prob_ref[...], q_ref[...]) * scale
        sums_refs[n][...] = sums + more_refs[n][...] if add else sums
        share = dot(items_refs[n][0:block], prob_ref[...], TN)
        qg_ref[...] = (qg_in_ref[...] if n == 0 else qg_ref[...]) + share
    sp_ref[...] = found


def run_grad(items, block, more, qt, q, bias, lse, pos, qg, sp, scale, base):
    count, (width, nq) = len(items), qt.shape
    before = count + len(more)
    *sums, qg, sp = pl.pallas_call(
        functools.partial(grad_kernel, scale, base, count, len(more)),
        in_specs=in_vmem(before + 7),
        out_specs=in_vmem(count + 2),
        out_shape=[jax.ShapeDtypeStruct((block, width), F32)] * count
        + [jax.ShapeDtypeStruct((width, nq), F32), jax.ShapeDtypeStruct((8, nq), F32)],
        scratch_shapes=[pltpu.VMEM((block, nq), F32)] * count
        + [pltpu.VMEM((block, nq), BF16)] * count,
        input_output_aliases={before + 5: count, before + 6: count + 1},
        compiler_params=pltpu.CompilerParams(vmem_limit_bytes=8 << 20),
    )(*items, *more, qt, q, bias, lse, pos, qg, sp)
    return sums, qg, sp


def backward_kernel(count, index_ref, factor_ref, *refs):
    grad_refs, (pre_ref, hidden_ref, emb_ref, w_out_ref) = refs[:count], refs[count : count + 4]
    grad_ref, pre_grad_ref, b_ref, *sums_refs = refs[count + 4 :]
    part = grad_refs[0].shape[0]
    for k in range(count):
        start = pl.multiple_of((index_ref[0] ^ k) * part, part)
        grad_ref[pl.ds(start, part)] = grad_refs[k][...]
    back = dot(grad_ref[...], w_out_ref[...], NT)
    pre_grad = jnp.where(pre_ref[...] > 0.0, back, 0.0).astype(BF16)
    pre_grad_ref[...] = pre_grad
    b_ref[...] = jnp.sum(pre_grad.astype(F32), axis=0, keepdims=True)
    sums_in = dot(emb_ref[...], pre_grad, TN) * factor_ref[0]
    sums_out = dot(hidden_ref[...], grad_ref[...], TN) * factor_ref[1]
    if len(sums_refs) == 1:
        units = sums_in.shape[1]
        sums_refs[0][:, :units] = sums_in
        sums_refs[0][:, units:] = sums_out
    else:
        sums_refs[0][...] = sums_in
        sums_refs[1][...] = sums_out


def run_backward(index, factors, grads, pre, hidden, emb, w_out):
    rows, units = pre.shape
    width_emb, width_out = emb.shape[1], w_out.shape[1]
    if units == width_emb:
        sums = [(width_emb, units + width_out)]
    else:
        sums = [(width_emb, units), (units, width_out)]
    grad, pre_grad, local_b, *sums = pl.pallas_call(
        functools.partial(backward_kernel, len(grads)),
        in_specs=[pl.BlockSpec(memory_space=pltpu.SMEM)] * 2 + in_vmem(len(grads) + 4),
        out_specs=in_vmem(3 + len(sums)),
        out_shape=[
            jax.ShapeDtypeStruct((rows, width_out), BF16),
            jax.ShapeDtypeStruct((rows, units), BF16),
            jax.ShapeDtypeStruct((1, units), F32),
        ]
        + [jax.ShapeDtypeStruct(shape, F32) for shape in sums],
        compiler_params=pltpu.CompilerParams(vmem_limit_bytes=12 << 20),
    )(index, factors, *grads, pre, hidden, emb, w_out)
    if len(sums) > 1:
        sums = [jnp.concatenate([sums[0], sums[1].reshape(width_emb, -1)], axis=1)]
    return grad, pre_grad, local_b, sums[0]


def joined(mine, other, first):
    return jnp.where(
        first,
        jnp.concatenate([mine, other], axis=0),
        jnp.concatenate([other, mine], axis=0),
    )


def per_device(queries, item_table, cand_row, cand_owner, cand_count, positive, w_in, b_in, w_out):
    n_data = lax.axis_size("dp")
    n_model = lax.axis_size("mp")
    n_z = n_data // 4
    me = lax.axis_index("dp")
    my_model = lax.axis_index("mp")
    n_query, width_out = queries.shape
    rows, width_emb = item_table.shape
    units = w_in.shape[1]
    part = rows // n_model
    cand_local = cand_row.shape[0]
    n_cols = n_data * part
    chunk = n_z * part // 2
    scale = 1.0 / math.sqrt(width_out)
    tie = lax.optimization_barrier
    slice_at = functools.partial(lax.dynamic_slice, allow_negative_indices=False)
    core = me & 1
    half_rows = width_emb // 2
    query_part = n_query // n_model
    starts = [(my_model ^ k) * part for k in range(n_model)]
    share_starts = [(my_model ^ k) * query_part for k in range(n_model)]
    half_starts = [(core ^ k) * half_rows for k in range(2)]
    model_index = my_model.astype(jnp.int32).reshape(1)
    core_first = core == 0

    def place(rel):
        return ((rel >> 1) & 1) * (2 * n_z) + (rel & 1) * n_z + (rel >> 2)

    def bit_of(bits):
        return (me // bits) & 1

    pre = dot(item_table, w_in) + b_in[None, :]
    hidden = jnp.maximum(pre, 0.0).astype(BF16)
    partial = dot(hidden, w_out)

    def part_of(value, k):
        return slice_at(value, (starts[k], 0), (part, value.shape[1]))

    outgoing = [part_of(partial, k) for k in range(1, n_model)]
    arrived = [hop(outgoing[k - 1], k, "mp") for k in range(1, n_model)]
    outgoing, queries, cand_row = tie((outgoing, queries, cand_row))
    qt = queries.T
    packed = jnp.concatenate([w_in, w_out.reshape(width_emb, -1)], axis=1)
    piece = slice_at(packed, (half_starts[0], 0), (half_rows, packed.shape[1]))

    largest = jnp.max(jnp.abs(queries)).astype(F32)
    exponent = jnp.floor(jnp.log2(jnp.maximum(largest, 1e-6))).astype(jnp.int32) + 1
    exponent = jnp.clip(exponent + EXPONENT_BASE, 0, 63)
    word = (cand_owner[:, 0] * rows + cand_row) * COUNT_BASE + cand_count
    word = (word + exponent * (1 << WORD_BITS))[None, :]
    words = jnp.concatenate([word, hop(word, 1)], axis=0)
    words = jnp.concatenate([words, hop(words, 2)], axis=0)

    total, arrived, qt, piece = tie((part_of(partial, 0), arrived, qt, piece))
    for other in arrived:
        total = total + other
    size = 4 * cand_local
    digits = jnp.stack([(words.reshape(size) >> shift) & 255 for shift in (0, 8, 16, 24)])
    tail_rows = -(-4 * size // (16 * width_out)) * 16
    digits = jnp.pad(digits.reshape(-1), (0, tail_rows * width_out - 4 * size))
    tail = digits.reshape(tail_rows, width_out).astype(BF16)
    payload = jnp.concatenate([total.astype(BF16), tail], axis=0)

    along_z = {0: payload}
    for j in range(n_z - 1, 0, -1):
        along_z[j] = hop(payload, j << 2)
    along_x = {j: hop(along_z[j], 2) for j in range(2)}
    along_z, along_x = tie((along_z, along_x))
    tails = jnp.stack([along_z[j][part:] for j in range(n_z)]).reshape(n_z, -1)[:, : 4 * size]
    tails = tails.astype(jnp.int32).reshape(n_z, 4, size)
    words = tails[:, 0] + tails[:, 1] * 256 + tails[:, 2] * 65536 + tails[:, 3] * 16777216

    flat = words.reshape(-1)
    n_cand = flat.shape[0]
    q_bound = jnp.exp2((jnp.max(flat >> WORD_BITS) - EXPONENT_BASE).astype(F32))
    flat = flat & ((1 << WORD_BITS) - 1)

    hidden_max = width_emb * TABLE_MAX * W_IN_MAX + B_IN_MAX
    gradient_sum = n_data * n_query * 2.0 * scale
    bounds = [
        2 * n_query * 2.0 * scale,
        4 * n_query * 2.0 * scale,
        gradient_sum * width_out * W_OUT_MAX * TABLE_MAX,
        gradient_sum * hidden_max,
    ]
    factors = [(LIMIT / bound) / q_bound for bound in bounds]
    growths = [q_bound * (bound / LIMIT) for bound in bounds]
    row = (flat // COUNT_BASE) % rows
    column = place((flat // (COUNT_BASE * rows)) ^ me) * part + row % part
    column = jnp.where(row // part == my_model, column, -1)
    share = 1.0 / (flat % COUNT_BASE).astype(F32)
    lanes = 128
    high = (jnp.arange(n_cols // lanes)[:, None] == (column >> 7)[None, :]).astype(F32)
    low = jnp.where(jnp.arange(lanes)[:, None] == (column & 127)[None, :], share[None, :], 0.0)
    weight = dot(low, high, NT, precision=lax.Precision.HIGHEST)
    bias = jnp.where(weight > 0.0, jnp.log2(weight), ABSENT)
    own_mask = dot(item_table, packed[:, :units]) + b_in[None, :] > 0.0
    bias, factors, growths, share_starts, half_starts, model_index, core_first, own_mask = tie(
        (bias, factors, growths, share_starts, half_starts, model_index, core_first, own_mask)
    )

    spot = ((positive // cand_local) ^ me) * cand_local + positive % cand_local
    side = 64
    table = flat.reshape(n_cand // side, side)
    digits = jnp.concatenate([table & 255, (table >> 8) & 255, table >> 16], axis=1).astype(BF16)
    picked = (jnp.arange(n_cand // side)[:, None] == (spot // side)[None, :]).astype(BF16)
    found = dot(digits, picked, TN).reshape(3, side, n_query)
    mine = jnp.arange(side)[:, None] == (spot % side)[None, :]
    digit = jnp.sum(jnp.where(mine[None], found, 0.0), axis=1).astype(jnp.int32)
    pos_word = digit[0] + digit[1] * 256 + digit[2] * 65536
    pos_row = (pos_word // COUNT_BASE) % rows
    pos_col = place((pos_word // (COUNT_BASE * rows)) ^ me) * part + pos_row % part
    pos_col = jnp.where(pos_row // part == my_model, pos_col, -1)[None, :]
    pos_logc = jnp.log((pos_word % COUNT_BASE).astype(F32))

    halves = [range(h * n_z // 2, (h + 1) * n_z // 2) for h in range(2)]
    start_of = {
        (x, c, h): ((x * 2 + c) * 2 + h) * chunk for x in range(2) for c in range(2) for h in range(2)
    }
    items = {}
    m8 = jnp.full((8, n_query), ABSENT, F32)
    l8 = jnp.zeros((8, n_query), F32)

    def gathered(x, h, blocks):
        items[x, 0, h] = [blocks[j] for j in halves[h]]
        items[x, 1, h] = [hop(v, 1) for v in items[x, 0, h]]

    def statistics(m, l, *chosen):
        for key in chosen:
            m, l = run_stats(items[key], part, qt, bias, m, l, scale * LOG2E, start_of[key], False)
        return m, l

    for j in range(2, n_z):
        along_x[j] = hop(along_z[j], 2)
    gathered(0, 0, along_z)
    m8, l8 = statistics(m8, l8, (0, 0, 0), (0, 1, 0))
    along_x, m8, l8 = tie((along_x, m8, l8))
    gathered(0, 1, along_z)
    m8, l8 = statistics(m8, l8, (0, 0, 1), (0, 1, 1))
    gathered(1, 0, along_x)
    m8, l8 = statistics(m8, l8, (1, 0, 0))
    gathered(1, 1, along_x)
    m8, l8 = statistics(m8, l8, (1, 1, 0), (1, 0, 1))
    (local,) = run_stats(
        items[1, 1, 1], part, qt, bias, m8, l8, scale * LOG2E, start_of[1, 1, 1], True
    )
    lse = run_lse(model_index, [local] + [hop(local, k, "mp") for k in range(1, n_model)])

    piece, b_late, lse = tie((piece, b_in[None, :], lse))
    others = [(hop(piece, k, "mp"), hop(b_late, k, "mp")) for k in range(1, n_model)]

    qg = jnp.zeros((width_out, n_query), F32)
    sp = jnp.zeros((8, n_query), F32)
    chip_sums, crossed, z_sums = {}, {}, [None] * n_z

    def gradients(key, qg, sp, more=()):
        return run_grad(
            items[key], part, more, qt, queries, bias, lse, pos_col, qg, sp,
            scale, start_of[key],
        )

    siblings, crossing = {}, {}
    for h in (1, 0):
        sums, qg, sp = gradients((1, 1, h), qg, sp)
        siblings[1, h] = [hop(v, 1) for v in sums]
    for h in (1, 0):
        chip_sums[1, h], qg, sp = gradients((1, 0, h), qg, sp, siblings[1, h])
        crossing[h], qg = tie(
            ((jnp.concatenate(chip_sums[1, h], axis=0) * factors[0]).astype(F16), qg)
        )
        crossed[h] = hop(crossing[h], 2)
    for h in (1, 0):
        sums, qg, sp = gradients((0, 1, h), qg, sp)
        siblings[0, h] = [hop(v, 1) for v in sums]
    for h in (1, 0):
        crossed[h], qg = tie((crossed[h], qg))
        chip_sums[0, h], qg, sp = gradients((0, 0, h), qg, sp, siblings[0, h])
        for j in range(n_z // 2):
            over = crossed[h][j * part : (j + 1) * part].astype(F32) * growths[0]
            z_sums[h * n_z // 2 + j] = chip_sums[0, h][j] + over
    own_sum = z_sums[0]
    for j in range(n_z - 1, 0, -1):
        sent = hop((z_sums[j] * factors[1]).astype(F16), j << 2)
        own_sum = own_sum + sent.astype(F32) * growths[1]
    own_grad, others = tie((own_sum.astype(BF16), others))
    others = [(joined(got, hop(got, 1), core_first), b) for got, b in others]
    weights = [(packed, b_in[None, :])] + others
    if n_model > 2:
        turn = jnp.arange(n_model) ^ my_model
        stacks = [jnp.take(jnp.stack(group), turn, axis=0) for group in zip(*weights)]
        weights = [(stacks[0][k], stacks[1][k]) for k in range(n_model)]
    weights = [(w[:, :units], w[:, units:].reshape(units, width_out), b) for w, b in weights]
    masks = [dot(item_table, share_in) + b > 0.0 for share_in, _, b in weights]
    if n_model == 2:
        masks[0] = own_mask


    grads = [own_grad] + [hop(own_grad, k, "mp") for k in range(1, n_model)]
    grads, masks = tie((grads, masks))
    item_grad, pre_grad, local_b, value = run_backward(
        model_index, jnp.stack(factors[2:]), grads, pre, hidden, item_table, w_out
    )

    width = value.shape[1]
    keep, give = (slice_at(value, (half_starts[k], 0), (half_rows, width)) for k in range(2))
    bias_steps = [1 << n for n in range(n_data.bit_length() - 1)]
    bias_steps = bias_steps[:1] + bias_steps[:0:-1]

    def step_bias(value, steps):
        for _ in range(min(steps, len(bias_steps))):
            bits = bias_steps.pop(0)
            value = value + hop(value, bits)
        return value

    value = (keep + hop(give.astype(F16), 1).astype(F32)).astype(F16)
    value, local_b = tie((value, step_bias(local_b, 1)))
    chips = n_data // 2
    groups = [[2 * chip + c for chip in range(chips)] for c in range(2)]

    def exchange(blocks):
        return lax.all_to_all(
            blocks, "dp", split_axis=0, concat_axis=0, axis_index_groups=groups, tiled=True
        )

    size = half_rows // chips
    grad_table = None
    for (share_in, share_out, _), mask in zip(weights, masks):
        back = jnp.where(mask, dot(item_grad, share_out, NT), 0.0).astype(BF16)
        term = dot(back, share_in, NT)
        grad_table = term if grad_table is None else grad_table + term

    pieces = exchange(value.reshape(chips, size, width))
    pieces, grad_table = tie((pieces, grad_table))
    total = jnp.sum(pieces.astype(F32), axis=0).astype(F16)
    total, local_b = tie((total, step_bias(local_b, 9)))
    own_half = exchange(jnp.broadcast_to(total[None], (chips, size, width)))
    own_half = own_half.reshape(half_rows, width)

    local_b, qg, sp = tie((local_b, qg, sp))

    item_max = n_model * units * hidden_max * W_OUT_MAX
    q_factor = LIMIT / (2.0 * item_max)
    sp1 = jnp.sum(sp, axis=0)[None, :]
    qg_parts = [
        slice_at(qg, (0, share_starts[k]), (width_out, query_part))
        for k in range(n_model)
    ]
    pos_score, query_sum = sp1, qg_parts[0]
    for k in range(1, n_model):
        sent = hop((qg_parts[k] * q_factor).astype(F16), k, "mp")
        query_sum = query_sum + sent.astype(F32) * (1.0 / q_factor)
        pos_score = pos_score + hop(sp1, k, "mp")
    loss = lse[0] * (1.0 / LOG2E) - (pos_score[0] * scale - pos_logc)
    query_grad = (query_sum * scale).T

    sides = [own_half, hop(own_half, 1)]
    sides_in = [v[:, :units].astype(F32) * growths[2] for v in sides]
    sides_out = [v[:, units:].astype(F32) * growths[3] for v in sides]
    grad_w_in = joined(*sides_in, core_first)
    grad_w_out = joined(*sides_out, core_first).reshape(units, width_out)
    return (loss, query_grad, grad_w_in, local_b[0], grad_w_out, grad_table)


def solution(mesh):
    placed = (
        P("dp", None),
        P("dp", None),
        P("dp"),
        P("dp", None),
        P("dp"),
        P("dp"),
        P(None, "mp"),
        P("mp"),
        P("mp", None),
    )
    return jax.shard_map(
        per_device,
        mesh=mesh,
        in_specs=placed,
        out_specs=(
            P("dp"),
            P(("dp", "mp"), None),
            P(None, "mp"),
            P("mp"),
            P("mp", None),
            P("dp", None),
        ),
        check_vma=False,
    )
```

```python
import functools
import math

import jax
import jax.numpy as jnp
from jax import lax
from jax.experimental import pallas as pl
from jax.experimental.pallas import tpu as pltpu
from jax.sharding import PartitionSpec as P

F32 = jnp.float32
BF16 = jnp.bfloat16
F16 = jnp.float16
ABSENT = -1e30
COUNT_BASE = 128
WORD_BITS = 22
EXPONENT_BASE = 20
TABLE_MAX = 6.0
W_IN_MAX = 0.25
B_IN_MAX = 3.0
W_OUT_MAX = 0.1875
LIMIT = 32768.0
LOG2E = math.log2(math.e)
GROUP = 16
NT = (((1,), (1,)), ((), ()))
TN = (((0,), (0,)), ((), ()))


def hop(value, bits, axis="dp"):
    size = lax.axis_size(axis)
    return lax.ppermute(value, axis, [(i, i ^ bits) for i in range(size)])


def dot(a, b, dims=None, **kw):
    if dims is None:
        dims = (((1,), (0,)), ((), ()))
    return lax.dot_general(a, b, dims, preferred_element_type=F32, **kw)


def column_bias(bias_ref, first, count):
    lane = first // 128
    return bias_ref[pl.ds(first % 128, count), lane : lane + 1]


def stats_kernel(scale, base, count, last, *refs):
    items_refs, refs = refs[:count], refs[count:]
    qt_ref, bias_ref, m_in_ref, l_in_ref, m_ref, *score_refs = refs
    l_ref = None if last else score_refs.pop(0)
    block = score_refs[0].shape[0]
    old = m_in_ref[...]
    new = old
    for items_ref, score_ref in zip(items_refs, score_refs):
        score_ref[...] = dot(items_ref[0:block], qt_ref[...])
    for n, score_ref in enumerate(score_refs):
        for r in range(0, block, 8):
            bias = column_bias(bias_ref, base + n * block + r, 8)
            score = score_ref[r : r + 8] * scale + bias
            score_ref[r : r + 8] = score
            new = jnp.maximum(new, score)
    total = l_in_ref[...] * jnp.exp2(old - new)
    for score_ref in score_refs:
        for r in range(0, block, 8):
            total = total + jnp.exp2(score_ref[r : r + 8] - new)
    if last:
        top = jnp.max(new, axis=0, keepdims=True)
        m_ref[0:1] = top
        m_ref[1:2] = jnp.sum(total * jnp.exp2(new - top), axis=0, keepdims=True)
    else:
        m_ref[...] = new
        l_ref[...] = total


def in_vmem(count):
    return [pl.BlockSpec(memory_space=pltpu.VMEM)] * count


def run_stats(items, block, qt, bias, m, l, scale, base, last):
    count, nq = len(items), qt.shape[1]
    shapes = [(2, nq)] if last else [(8, nq)] * 2
    return pl.pallas_call(
        functools.partial(stats_kernel, scale, base, count, last),
        in_specs=in_vmem(count + 4),
        out_specs=in_vmem(len(shapes)),
        out_shape=[jax.ShapeDtypeStruct(shape, F32) for shape in shapes],
        scratch_shapes=[pltpu.VMEM((block, nq), F32)] * count,
        compiler_params=pltpu.CompilerParams(vmem_limit_bytes=6 << 20),
    )(*items, qt, bias, m, l)


def lse_kernel(count, index_ref, *refs):
    part_refs, (lse_ref, held_ref) = refs[:count], refs[count:]
    for k in range(count):
        held_ref[index_ref[0] ^ k] = part_refs[k][...]
    parts = [held_ref[k] for k in range(count)]
    top = functools.reduce(jnp.maximum, [p[0:1] for p in parts])
    total = functools.reduce(jnp.add, [p[1:2] * jnp.exp2(p[0:1] - top) for p in parts])
    lse_ref[...] = top + jnp.log2(total)


def run_lse(index, parts):
    nq = parts[0].shape[1]
    return pl.pallas_call(
        functools.partial(lse_kernel, len(parts)),
        in_specs=[pl.BlockSpec(memory_space=pltpu.SMEM)] + in_vmem(len(parts)),
        out_specs=in_vmem(1)[0],
        out_shape=jax.ShapeDtypeStruct((1, nq), F32),
        scratch_shapes=[pltpu.VMEM((len(parts), 2, nq), F32)],
        compiler_params=pltpu.CompilerParams(vmem_limit_bytes=2 << 20),
    )(index, *parts)


def grad_kernel(scale, base, count, add, *refs):
    items_refs, refs = refs[:count], refs[count:]
    more_refs, refs = refs[:add], refs[add:]
    qt_ref, q_ref, bias_ref, lse_ref, pos_ref, qg_in_ref, sp_in_ref, *refs = refs
    sums_refs, (qg_ref, sp_ref, *scratch) = refs[:count], refs[count:]
    score_refs, prob_refs = scratch[:count], scratch[count:]
    block, queries = score_refs[0].shape
    for items_ref, score_ref in zip(items_refs, score_refs):
        score_ref[...] = dot(items_ref[0:block], qt_ref[...])
    down = lax.broadcasted_iota(jnp.int32, (8, queries), 0)
    offset = jnp.broadcast_to(pos_ref[...], (8, queries)) - down
    lse = jnp.broadcast_to(lse_ref[...], (8, queries))
    found = sp_in_ref[...]
    for n in range(count):
        score_ref, prob_ref = score_refs[n], prob_refs[n]
        for r in range(0, block, GROUP):
            pieces = []
            for s in range(r, r + GROUP, 8):
                at = base + n * block + s
                score = score_ref[s : s + 8]
                here = offset == at
                found = found + jnp.where(here, score, 0.0)
                prob = jnp.exp2((score * (scale * LOG2E) + column_bias(bias_ref, at, 8)) - lse)
                pieces.append(jnp.where(here, prob - 1.0, prob))
            prob_ref[r : r + GROUP] = jnp.concatenate(pieces, axis=0).astype(BF16)
        sums = dot(prob_ref[...], q_ref[...]) * scale
        sums_refs[n][...] = sums + more_refs[n][...] if add else sums
        share = dot(items_refs[n][0:block], prob_ref[...], TN)
        qg_ref[...] = (qg_in_ref[...] if n == 0 else qg_ref[...]) + share
    sp_ref[...] = found


def run_grad(items, block, more, qt, q, bias, lse, pos, qg, sp, scale, base):
    count, (width, nq) = len(items), qt.shape
    before = count + len(more)
    *sums, qg, sp = pl.pallas_call(
        functools.partial(grad_kernel, scale, base, count, len(more)),
        in_specs=in_vmem(before + 7),
        out_specs=in_vmem(count + 2),
        out_shape=[jax.ShapeDtypeStruct((block, width), F32)] * count
        + [jax.ShapeDtypeStruct((width, nq), F32), jax.ShapeDtypeStruct((8, nq), F32)],
        scratch_shapes=[pltpu.VMEM((block, nq), F32)] * count
        + [pltpu.VMEM((block, nq), BF16)] * count,
        input_output_aliases={before + 5: count, before + 6: count + 1},
        compiler_params=pltpu.CompilerParams(vmem_limit_bytes=8 << 20),
    )(*items, *more, qt, q, bias, lse, pos, qg, sp)
    return sums, qg, sp


def backward_kernel(count, index_ref, scale_ref, *refs):
    grad_refs, (pre_ref, hidden_ref, emb_ref, w_out_ref) = refs[:count], refs[count : count + 4]
    grad_ref, pre_grad_ref, b_ref, *sums_refs = refs[count + 4 :]
    part = grad_refs[0].shape[0]
    for k in range(count):
        start = pl.multiple_of((index_ref[0] ^ k) * part, part)
        grad_ref[pl.ds(start, part)] = grad_refs[k][...]
    back = dot(grad_ref[...], w_out_ref[...], NT)
    pre_grad = jnp.where(pre_ref[...] > 0.0, back, 0.0).astype(BF16)
    pre_grad_ref[...] = pre_grad
    b_ref[...] = jnp.sum(pre_grad.astype(F32), axis=0, keepdims=True)
    sums_in = dot(emb_ref[...], pre_grad, TN) * scale_ref[2:3, : pre_grad.shape[1]]
    sums_out = dot(hidden_ref[...], grad_ref[...], TN) * scale_ref[3:4, : grad_ref.shape[1]]
    if len(sums_refs) == 1:
        units = sums_in.shape[1]
        sums_refs[0][:, :units] = sums_in
        sums_refs[0][:, units:] = sums_out
    else:
        sums_refs[0][...] = sums_in
        sums_refs[1][...] = sums_out


def run_backward(index, scales, grads, pre, hidden, emb, w_out):
    rows, units = pre.shape
    width_emb, width_out = emb.shape[1], w_out.shape[1]
    if units == width_emb:
        sums = [(width_emb, units + width_out)]
    else:
        sums = [(width_emb, units), (units, width_out)]
    grad, pre_grad, local_b, *sums = pl.pallas_call(
        functools.partial(backward_kernel, len(grads)),
        in_specs=[pl.BlockSpec(memory_space=pltpu.SMEM)] + in_vmem(len(grads) + 5),
        out_specs=in_vmem(3 + len(sums)),
        out_shape=[
            jax.ShapeDtypeStruct((rows, width_out), BF16),
            jax.ShapeDtypeStruct((rows, units), BF16),
            jax.ShapeDtypeStruct((1, units), F32),
        ]
        + [jax.ShapeDtypeStruct(shape, F32) for shape in sums],
        compiler_params=pltpu.CompilerParams(vmem_limit_bytes=12 << 20),
    )(index, scales, *grads, pre, hidden, emb, w_out)
    if len(sums) > 1:
        sums = [jnp.concatenate([sums[0], sums[1].reshape(width_emb, -1)], axis=1)]
    return grad, pre_grad, local_b, sums[0]


def scale_kernel(bounds, words_ref, scale_ref):
    exponent = jnp.max(words_ref[...] >> WORD_BITS, axis=1, keepdims=True)
    exponent = jnp.max(exponent, axis=0, keepdims=True) - EXPONENT_BASE
    largest = jnp.exp2(jnp.broadcast_to(exponent.astype(F32), (1, scale_ref.shape[1])))
    for n, bound in enumerate(bounds):
        scale_ref[n : n + 1] = (LIMIT / bound) / largest
        scale_ref[n + len(bounds) : n + len(bounds) + 1] = largest * (bound / LIMIT)


def run_scale(bounds, words, width):
    return pl.pallas_call(
        functools.partial(scale_kernel, bounds),
        in_specs=in_vmem(1),
        out_specs=in_vmem(1)[0],
        out_shape=jax.ShapeDtypeStruct((2 * len(bounds), width), F32),
        compiler_params=pltpu.CompilerParams(vmem_limit_bytes=2 << 20),
    )(words)


def joined(mine, other, first):
    return jnp.where(
        first,
        jnp.concatenate([mine, other], axis=0),
        jnp.concatenate([other, mine], axis=0),
    )


def per_device(queries, item_table, cand_row, cand_owner, cand_count, positive, w_in, b_in, w_out):
    n_data = lax.axis_size("dp")
    n_model = lax.axis_size("mp")
    n_z = n_data // 4
    me = lax.axis_index("dp")
    my_model = lax.axis_index("mp")
    n_query, width_out = queries.shape
    rows, width_emb = item_table.shape
    units = w_in.shape[1]
    part = rows // n_model
    cand_local = cand_row.shape[0]
    n_cols = n_data * part
    chunk = n_z * part // 2
    scale = 1.0 / math.sqrt(width_out)
    tie = lax.optimization_barrier
    slice_at = functools.partial(lax.dynamic_slice, allow_negative_indices=False)
    core = me & 1
    half_rows = width_emb // 2
    query_part = n_query // n_model
    starts = [(my_model ^ k) * part for k in range(n_model)]
    share_starts = [(my_model ^ k) * query_part for k in range(n_model)]
    half_starts = [(core ^ k) * half_rows for k in range(2)]
    model_index = my_model.astype(jnp.int32).reshape(1)
    core_first = core == 0

    def place(rel):
        return ((rel >> 1) & 1) * (2 * n_z) + (rel & 1) * n_z + (rel >> 2)

    def bit_of(bits):
        return (me // bits) & 1

    pre = dot(item_table, w_in) + b_in[None, :]
    hidden = jnp.maximum(pre, 0.0).astype(BF16)
    partial = dot(hidden, w_out)

    def part_of(value, k):
        return slice_at(value, (starts[k], 0), (part, value.shape[1]))

    outgoing = [part_of(partial, k) for k in range(1, n_model)]
    arrived = [hop(outgoing[k - 1], k, "mp") for k in range(1, n_model)]
    outgoing, queries, cand_row = tie((outgoing, queries, cand_row))
    qt = queries.T
    packed = jnp.concatenate([w_in, w_out.reshape(width_emb, -1)], axis=1)
    piece = slice_at(packed, (half_starts[0], 0), (half_rows, packed.shape[1]))

    largest = jnp.max(jnp.abs(queries)).astype(F32)
    exponent = jnp.floor(jnp.log2(jnp.maximum(largest, 1e-6))).astype(jnp.int32) + 1
    exponent = jnp.clip(exponent + EXPONENT_BASE, 0, 63)
    word = (cand_owner[:, 0] * rows + cand_row) * COUNT_BASE + cand_count
    word = (word + exponent * (1 << WORD_BITS))[None, :]
    words = jnp.concatenate([word, hop(word, 1)], axis=0)
    words = jnp.concatenate([words, hop(words, 2)], axis=0)

    total, arrived, qt, piece, share_starts, half_starts, model_index, core_first = tie(
        (
            part_of(partial, 0),
            arrived,
            qt,
            piece,
            share_starts,
            half_starts,
            model_index,
            core_first,
        )
    )
    for other in arrived:
        total = total + other
    size = 4 * cand_local
    digits = jnp.stack([(words.reshape(size) >> shift) & 255 for shift in (0, 8, 16, 24)])
    tail_rows = -(-4 * size // (16 * width_out)) * 16
    digits = jnp.pad(digits.reshape(-1), (0, tail_rows * width_out - 4 * size))
    tail = digits.reshape(tail_rows, width_out).astype(BF16)
    payload = jnp.concatenate([total.astype(BF16), tail], axis=0)

    along_z = {0: payload}
    for j in range(n_z - 1, 0, -1):
        along_z[j] = hop(payload, j << 2)
    along_x = {j: hop(along_z[j], 2) for j in range(2)}
    along_z, along_x = tie((along_z, along_x))
    tails = jnp.stack([along_z[j][part:] for j in range(n_z)]).reshape(n_z, -1)[:, : 4 * size]
    tails = tails.astype(jnp.int32).reshape(n_z, 4, size)
    words = tails[:, 0] + tails[:, 1] * 256 + tails[:, 2] * 65536 + tails[:, 3] * 16777216

    flat = words.reshape(-1)
    n_cand = flat.shape[0]
    flat = flat & ((1 << WORD_BITS) - 1)

    hidden_max = width_emb * TABLE_MAX * W_IN_MAX + B_IN_MAX
    gradient_sum = n_data * n_query * 2.0 * scale
    bounds = [
        2 * n_query * 2.0 * scale,
        4 * n_query * 2.0 * scale,
        gradient_sum * width_out * W_OUT_MAX * TABLE_MAX,
        gradient_sum * hidden_max,
    ]
    scales = run_scale(bounds, words, max(units, width_out))
    factors = [scales[n : n + 1] for n in range(4)]
    growths = [scales[n + 4 : n + 5] for n in range(4)]
    row = (flat // COUNT_BASE) % rows
    column = place((flat // (COUNT_BASE * rows)) ^ me) * part + row % part
    column = jnp.where(row // part == my_model, column, -1)
    share = 1.0 / (flat % COUNT_BASE).astype(F32)
    lanes = 128
    high = (jnp.arange(n_cols // lanes)[:, None] == (column >> 7)[None, :]).astype(F32)
    low = jnp.where(jnp.arange(lanes)[:, None] == (column & 127)[None, :], share[None, :], 0.0)
    weight = dot(low, high, NT, precision=lax.Precision.HIGHEST)
    bias = jnp.where(weight > 0.0, jnp.log2(weight), ABSENT)
    own_mask = dot(item_table, packed[:, :units]) + b_in[None, :] > 0.0
    bias, own_mask = tie((bias, own_mask))

    spot = ((positive // cand_local) ^ me) * cand_local + positive % cand_local
    side = 64
    table = flat.reshape(n_cand // side, side)
    digits = jnp.concatenate([table & 255, (table >> 8) & 255, table >> 16], axis=1).astype(BF16)
    picked = (jnp.arange(n_cand // side)[:, None] == (spot // side)[None, :]).astype(BF16)
    found = dot(digits, picked, TN).reshape(3, side, n_query)
    mine = jnp.arange(side)[:, None] == (spot % side)[None, :]
    digit = jnp.sum(jnp.where(mine[None], found, 0.0), axis=1).astype(jnp.int32)
    pos_word = digit[0] + digit[1] * 256 + digit[2] * 65536
    pos_row = (pos_word // COUNT_BASE) % rows
    pos_col = place((pos_word // (COUNT_BASE * rows)) ^ me) * part + pos_row % part
    pos_col = jnp.where(pos_row // part == my_model, pos_col, -1)[None, :]
    pos_logc = jnp.log((pos_word % COUNT_BASE).astype(F32))

    halves = [range(h * n_z // 2, (h + 1) * n_z // 2) for h in range(2)]
    start_of = {
        (x, c, h): ((x * 2 + c) * 2 + h) * chunk for x in range(2) for c in range(2) for h in range(2)
    }
    items = {}
    m8 = jnp.full((8, n_query), ABSENT, F32)
    l8 = jnp.zeros((8, n_query), F32)

    def gathered(x, h, blocks):
        items[x, 0, h] = [blocks[j] for j in halves[h]]
        items[x, 1, h] = [hop(v, 1) for v in items[x, 0, h]]

    def statistics(m, l, *chosen):
        for key in chosen:
            m, l = run_stats(items[key], part, qt, bias, m, l, scale * LOG2E, start_of[key], False)
        return m, l

    for j in range(2, n_z):
        along_x[j] = hop(along_z[j], 2)
    gathered(0, 0, along_z)
    m8, l8 = statistics(m8, l8, (0, 0, 0), (0, 1, 0))
    along_x, m8, l8 = tie((along_x, m8, l8))
    gathered(0, 1, along_z)
    m8, l8 = statistics(m8, l8, (0, 0, 1), (0, 1, 1))
    gathered(1, 0, along_x)
    m8, l8 = statistics(m8, l8, (1, 0, 0))
    gathered(1, 1, along_x)
    m8, l8 = statistics(m8, l8, (1, 1, 0), (1, 0, 1))
    (local,) = run_stats(
        items[1, 1, 1], part, qt, bias, m8, l8, scale * LOG2E, start_of[1, 1, 1], True
    )
    lse = run_lse(model_index, [local] + [hop(local, k, "mp") for k in range(1, n_model)])

    piece, b_late, lse = tie((piece, b_in[None, :], lse))
    others = [(hop(piece, k, "mp"), hop(b_late, k, "mp")) for k in range(1, n_model)]

    qg = jnp.zeros((width_out, n_query), F32)
    sp = jnp.zeros((8, n_query), F32)
    chip_sums, crossed, z_sums = {}, {}, [None] * n_z

    def gradients(key, qg, sp, more=()):
        return run_grad(
            items[key], part, more, qt, queries, bias, lse, pos_col, qg, sp,
            scale, start_of[key],
        )

    siblings, crossing = {}, {}
    for h in (1, 0):
        sums, qg, sp = gradients((1, 1, h), qg, sp)
        siblings[1, h] = [hop(v, 1) for v in sums]
    for h in (1, 0):
        chip_sums[1, h], qg, sp = gradients((1, 0, h), qg, sp, siblings[1, h])
        crossing[h], qg = tie(
            ((jnp.concatenate(chip_sums[1, h], axis=0) * factors[0][:, :width_out]).astype(F16), qg)
        )
        crossed[h] = hop(crossing[h], 2)
    for h in (1, 0):
        sums, qg, sp = gradients((0, 1, h), qg, sp)
        siblings[0, h] = [hop(v, 1) for v in sums]
    for h in (1, 0):
        crossed[h], qg = tie((crossed[h], qg))
        chip_sums[0, h], qg, sp = gradients((0, 0, h), qg, sp, siblings[0, h])
        for j in range(n_z // 2):
            over = crossed[h][j * part : (j + 1) * part].astype(F32) * growths[0][:, :width_out]
            z_sums[h * n_z // 2 + j] = chip_sums[0, h][j] + over
    own_sum = z_sums[0]
    for j in range(n_z - 1, 0, -1):
        sent = hop((z_sums[j] * factors[1][:, :width_out]).astype(F16), j << 2)
        own_sum = own_sum + sent.astype(F32) * growths[1][:, :width_out]
    own_grad, others = tie((own_sum.astype(BF16), others))
    others = [(joined(got, hop(got, 1), core_first), b) for got, b in others]
    weights = [(packed, b_in[None, :])] + others
    if n_model > 2:
        turn = jnp.arange(n_model) ^ my_model
        stacks = [jnp.take(jnp.stack(group), turn, axis=0) for group in zip(*weights)]
        weights = [(stacks[0][k], stacks[1][k]) for k in range(n_model)]
    weights = [(w[:, :units], w[:, units:].reshape(units, width_out), b) for w, b in weights]
    masks = [dot(item_table, share_in) + b > 0.0 for share_in, _, b in weights]
    if n_model == 2:
        masks[0] = own_mask


    grads = [own_grad] + [hop(own_grad, k, "mp") for k in range(1, n_model)]
    grads, masks = tie((grads, masks))
    item_grad, pre_grad, local_b, value = run_backward(
        model_index, scales, grads, pre, hidden, item_table, w_out
    )

    width = value.shape[1]
    keep, give = (slice_at(value, (half_starts[k], 0), (half_rows, width)) for k in range(2))
    bias_steps = [1 << n for n in range(n_data.bit_length() - 1)]
    bias_steps = bias_steps[:1] + bias_steps[:0:-1]

    def step_bias(value, steps):
        for _ in range(min(steps, len(bias_steps))):
            bits = bias_steps.pop(0)
            value = value + hop(value, bits)
        return value

    value = (keep + hop(give.astype(F16), 1).astype(F32)).astype(F16)
    value, local_b = tie((value, step_bias(local_b, 1)))
    chips = n_data // 2
    groups = [[2 * chip + c for chip in range(chips)] for c in range(2)]

    def exchange(blocks):
        return lax.all_to_all(
            blocks, "dp", split_axis=0, concat_axis=0, axis_index_groups=groups, tiled=True
        )

    size = half_rows // chips
    grad_table = None
    for (share_in, share_out, _), mask in zip(weights, masks):
        back = jnp.where(mask, dot(item_grad, share_out, NT), 0.0).astype(BF16)
        term = dot(back, share_in, NT)
        grad_table = term if grad_table is None else grad_table + term

    pieces = exchange(value.reshape(chips, size, width))
    pieces, grad_table = tie((pieces, grad_table))
    total = jnp.sum(pieces.astype(F32), axis=0).astype(F16)
    total, local_b = tie((total, step_bias(local_b, 2)))
    own_half = exchange(jnp.broadcast_to(total[None], (chips, size, width)))
    own_half = own_half.reshape(half_rows, width)
    local_b = step_bias(local_b, 9)

    local_b, qg, sp = tie((local_b, qg, sp))

    item_max = n_model * units * hidden_max * W_OUT_MAX
    q_factor = LIMIT / (2.0 * item_max)
    sp1 = jnp.sum(sp, axis=0)[None, :]
    qg_parts = [
        slice_at(qg, (0, share_starts[k]), (width_out, query_part))
        for k in range(n_model)
    ]
    pos_score, query_sum = sp1, qg_parts[0]
    for k in range(1, n_model):
        sent = hop((qg_parts[k] * q_factor).astype(F16), k, "mp")
        query_sum = query_sum + sent.astype(F32) * (1.0 / q_factor)
        pos_score = pos_score + hop(sp1, k, "mp")
    loss = lse[0] * (1.0 / LOG2E) - (pos_score[0] * scale - pos_logc)
    query_grad = (query_sum * scale).T

    sides = [own_half, hop(own_half, 1)]
    sides_in = [v[:, :units].astype(F32) * growths[2][:, :units] for v in sides]
    tail_width = width - units
    sides_out = [v[:, units:].astype(F32) * growths[3][:, :tail_width] for v in sides]
    grad_w_in = joined(*sides_in, core_first)
    grad_w_out = joined(*sides_out, core_first).reshape(units, width_out)
    return (loss, query_grad, grad_w_in, local_b[0], grad_w_out, grad_table)


def solution(mesh):
    placed = (
        P("dp", None),
        P("dp", None),
        P("dp"),
        P("dp", None),
        P("dp"),
        P("dp"),
        P(None, "mp"),
        P("mp"),
        P("mp", None),
    )
    return jax.shard_map(
        per_device,
        mesh=mesh,
        in_specs=placed,
        out_specs=(
            P("dp"),
            P(("dp", "mp"), None),
            P(None, "mp"),
            P("mp"),
            P("mp", None),
            P("dp", None),
        ),
        check_vma=False,
    )
```

```python
import functools
import math

import jax
import jax.numpy as jnp
from jax import lax
from jax.experimental import pallas as pl
from jax.experimental.pallas import tpu as pltpu
from jax.sharding import PartitionSpec as P

F32 = jnp.float32
BF16 = jnp.bfloat16
F16 = jnp.float16
ABSENT = -1e30
COUNT_BASE = 128
WORD_BITS = 22
EXPONENT_BASE = 20
TABLE_MAX = 6.0
W_IN_MAX = 0.25
B_IN_MAX = 3.0
W_OUT_MAX = 0.1875
LIMIT = 32768.0
LOG2E = math.log2(math.e)
GROUP = 16
NT = (((1,), (1,)), ((), ()))
TN = (((0,), (0,)), ((), ()))


def hop(value, bits, axis="dp"):
    size = lax.axis_size(axis)
    return lax.ppermute(value, axis, [(i, i ^ bits) for i in range(size)])


def dot(a, b, dims=None, **kw):
    if dims is None:
        dims = (((1,), (0,)), ((), ()))
    return lax.dot_general(a, b, dims, preferred_element_type=F32, **kw)


def column_bias(bias_ref, first, count):
    lane = first // 128
    return bias_ref[pl.ds(first % 128, count), lane : lane + 1]


def stats_kernel(scale, base, count, last, *refs):
    items_refs, refs = refs[:count], refs[count:]
    qt_ref, bias_ref, m_in_ref, l_in_ref, m_ref, *score_refs = refs
    l_ref = None if last else score_refs.pop(0)
    block = score_refs[0].shape[0]
    old = m_in_ref[...]
    new = old
    for items_ref, score_ref in zip(items_refs, score_refs):
        score_ref[...] = dot(items_ref[0:block], qt_ref[...])
    for n, score_ref in enumerate(score_refs):
        for r in range(0, block, 8):
            bias = column_bias(bias_ref, base + n * block + r, 8)
            score = score_ref[r : r + 8] * scale + bias
            score_ref[r : r + 8] = score
            new = jnp.maximum(new, score)
    total = l_in_ref[...] * jnp.exp2(old - new)
    for score_ref in score_refs:
        for r in range(0, block, 8):
            total = total + jnp.exp2(score_ref[r : r + 8] - new)
    if last:
        top = jnp.max(new, axis=0, keepdims=True)
        m_ref[0:1] = top
        m_ref[1:2] = jnp.sum(total * jnp.exp2(new - top), axis=0, keepdims=True)
    else:
        m_ref[...] = new
        l_ref[...] = total


def in_vmem(count):
    return [pl.BlockSpec(memory_space=pltpu.VMEM)] * count


def run_stats(items, block, qt, bias, m, l, scale, base, last):
    count, nq = len(items), qt.shape[1]
    shapes = [(2, nq)] if last else [(8, nq)] * 2
    return pl.pallas_call(
        functools.partial(stats_kernel, scale, base, count, last),
        in_specs=in_vmem(count + 4),
        out_specs=in_vmem(len(shapes)),
        out_shape=[jax.ShapeDtypeStruct(shape, F32) for shape in shapes],
        scratch_shapes=[pltpu.VMEM((block, nq), F32)] * count,
        compiler_params=pltpu.CompilerParams(vmem_limit_bytes=6 << 20),
    )(*items, qt, bias, m, l)


def lse_kernel(count, index_ref, *refs):
    part_refs, (lse_ref, held_ref) = refs[:count], refs[count:]
    for k in range(count):
        held_ref[index_ref[0] ^ k] = part_refs[k][...]
    parts = [held_ref[k] for k in range(count)]
    top = functools.reduce(jnp.maximum, [p[0:1] for p in parts])
    total = functools.reduce(jnp.add, [p[1:2] * jnp.exp2(p[0:1] - top) for p in parts])
    lse_ref[...] = top + jnp.log2(total)


def run_lse(index, parts):
    nq = parts[0].shape[1]
    return pl.pallas_call(
        functools.partial(lse_kernel, len(parts)),
        in_specs=[pl.BlockSpec(memory_space=pltpu.SMEM)] + in_vmem(len(parts)),
        out_specs=in_vmem(1)[0],
        out_shape=jax.ShapeDtypeStruct((1, nq), F32),
        scratch_shapes=[pltpu.VMEM((len(parts), 2, nq), F32)],
        compiler_params=pltpu.CompilerParams(vmem_limit_bytes=2 << 20),
    )(index, *parts)


def grad_kernel(scale, base, count, add, *refs):
    items_refs, refs = refs[:count], refs[count:]
    more_refs, refs = refs[:add], refs[add:]
    qt_ref, q_ref, bias_ref, lse_ref, pos_ref, qg_in_ref, sp_in_ref, *refs = refs
    sums_refs, (qg_ref, sp_ref, *scratch) = refs[:count], refs[count:]
    score_refs, prob_refs = scratch[:count], scratch[count:]
    block, queries = score_refs[0].shape
    for items_ref, score_ref in zip(items_refs, score_refs):
        score_ref[...] = dot(items_ref[0:block], qt_ref[...])
    down = lax.broadcasted_iota(jnp.int32, (8, queries), 0)
    offset = jnp.broadcast_to(pos_ref[...], (8, queries)) - down
    lse = jnp.broadcast_to(lse_ref[...], (8, queries))
    found = sp_in_ref[...]
    for n in range(count):
        score_ref, prob_ref = score_refs[n], prob_refs[n]
        for r in range(0, block, GROUP):
            pieces = []
            for s in range(r, r + GROUP, 8):
                at = base + n * block + s
                score = score_ref[s : s + 8]
                here = offset == at
                found = found + jnp.where(here, score, 0.0)
                prob = jnp.exp2((score * (scale * LOG2E) + column_bias(bias_ref, at, 8)) - lse)
                pieces.append(jnp.where(here, prob - 1.0, prob))
            prob_ref[r : r + GROUP] = jnp.concatenate(pieces, axis=0).astype(BF16)
        sums = dot(prob_ref[...], q_ref[...]) * scale
        sums_refs[n][...] = sums + more_refs[n][...] if add else sums
        share = dot(items_refs[n][0:block], prob_ref[...], TN)
        qg_ref[...] = (qg_in_ref[...] if n == 0 else qg_ref[...]) + share
    sp_ref[...] = found


def run_grad(items, block, more, qt, q, bias, lse, pos, qg, sp, scale, base):
    count, (width, nq) = len(items), qt.shape
    before = count + len(more)
    *sums, qg, sp = pl.pallas_call(
        functools.partial(grad_kernel, scale, base, count, len(more)),
        in_specs=in_vmem(before + 7),
        out_specs=in_vmem(count + 2),
        out_shape=[jax.ShapeDtypeStruct((block, width), F32)] * count
        + [jax.ShapeDtypeStruct((width, nq), F32), jax.ShapeDtypeStruct((8, nq), F32)],
        scratch_shapes=[pltpu.VMEM((block, nq), F32)] * count
        + [pltpu.VMEM((block, nq), BF16)] * count,
        input_output_aliases={before + 5: count, before + 6: count + 1},
        compiler_params=pltpu.CompilerParams(vmem_limit_bytes=8 << 20),
    )(*items, *more, qt, q, bias, lse, pos, qg, sp)
    return sums, qg, sp


def backward_kernel(count, index_ref, scale_ref, *refs):
    grad_refs, (pre_ref, hidden_ref, emb_ref, w_out_ref) = refs[:count], refs[count : count + 4]
    grad_ref, pre_grad_ref, b_ref, *sums_refs = refs[count + 4 :]
    part = grad_refs[0].shape[0]
    for k in range(count):
        start = pl.multiple_of((index_ref[0] ^ k) * part, part)
        grad_ref[pl.ds(start, part)] = grad_refs[k][...]
    back = dot(grad_ref[...], w_out_ref[...], NT)
    pre_grad = jnp.where(pre_ref[...] > 0.0, back, 0.0).astype(BF16)
    pre_grad_ref[...] = pre_grad
    b_ref[...] = jnp.sum(pre_grad.astype(F32), axis=0, keepdims=True)
    sums_in = dot(emb_ref[...], pre_grad, TN) * scale_ref[2:3, : pre_grad.shape[1]]
    sums_out = dot(hidden_ref[...], grad_ref[...], TN) * scale_ref[3:4, : grad_ref.shape[1]]
    if len(sums_refs) == 1:
        units = sums_in.shape[1]
        sums_refs[0][:, :units] = sums_in
        sums_refs[0][:, units:] = sums_out
    else:
        sums_refs[0][...] = sums_in
        sums_refs[1][...] = sums_out


def run_backward(index, scales, grads, pre, hidden, emb, w_out):
    rows, units = pre.shape
    width_emb, width_out = emb.shape[1], w_out.shape[1]
    if units == width_emb:
        sums = [(width_emb, units + width_out)]
    else:
        sums = [(width_emb, units), (units, width_out)]
    grad, pre_grad, local_b, *sums = pl.pallas_call(
        functools.partial(backward_kernel, len(grads)),
        in_specs=[pl.BlockSpec(memory_space=pltpu.SMEM)] + in_vmem(len(grads) + 5),
        out_specs=in_vmem(3 + len(sums)),
        out_shape=[
            jax.ShapeDtypeStruct((rows, width_out), BF16),
            jax.ShapeDtypeStruct((rows, units), BF16),
            jax.ShapeDtypeStruct((1, units), F32),
        ]
        + [jax.ShapeDtypeStruct(shape, F32) for shape in sums],
        compiler_params=pltpu.CompilerParams(vmem_limit_bytes=12 << 20),
    )(index, scales, *grads, pre, hidden, emb, w_out)
    if len(sums) > 1:
        sums = [jnp.concatenate([sums[0], sums[1].reshape(width_emb, -1)], axis=1)]
    return grad, pre_grad, local_b, sums[0]


def prepare_kernel(part, rows, bounds, count, index_ref, *refs):
    block_refs, refs = refs[:count], refs[count:]
    spot_ref, bias_ref, pos_ref, logc_ref, scale_ref, tail_ref, words_ref, col_ref, share_ref = refs
    lines, width = words_ref.shape
    run = lines // count
    lanes = 128
    for z in range(count):
        tail_ref[...] = block_refs[z][part : part + tail_ref.shape[0]].astype(F32)
        for r in range(run):
            value = tail_ref[r : r + 1].astype(jnp.int32)
            for digit in range(1, 4):
                at = digit * run + r
                value += tail_ref[at : at + 1].astype(jnp.int32) << (8 * digit)
            words_ref[z * run + r : z * run + r + 1] = value
    words = words_ref[...]
    exponent = jnp.max(words >> WORD_BITS, axis=1, keepdims=True)
    exponent = jnp.max(exponent, axis=0, keepdims=True) - EXPONENT_BASE
    largest = jnp.exp2(jnp.broadcast_to(exponent.astype(F32), (1, scale_ref.shape[1])))
    for n, bound in enumerate(bounds):
        scale_ref[n : n + 1] = (LIMIT / bound) / largest
        scale_ref[n + len(bounds) : n + len(bounds) + 1] = largest * (bound / LIMIT)

    count_bits, row_bits, part_bits = (n.bit_length() - 1 for n in (COUNT_BASE, rows, part))

    def decoded(word):
        row = (word >> count_bits) & (rows - 1)
        rel = (word >> (count_bits + row_bits)) ^ index_ref[0]
        place = ((rel >> 1) & 1) * (2 * count) + (rel & 1) * count + (rel >> 2)
        column = place * part + (row & (part - 1))
        named = (word & (COUNT_BASE - 1)).astype(F32)
        return jnp.where((row >> part_bits) == index_ref[1], column, -1), named

    words = words & ((1 << WORD_BITS) - 1)
    column, named = decoded(words)
    col_ref[...] = column
    share_ref[...] = 1.0 / named
    blocks = bias_ref.shape[1]
    weight = jnp.zeros((lanes, blocks), F32)
    block_iota = lax.broadcasted_iota(jnp.int32, (blocks, width), 0)
    lane_iota = lax.broadcasted_iota(jnp.int32, (lanes, width), 0)
    for n in range(lines):
        column = col_ref[n : n + 1]
        high = jnp.where(block_iota == (column >> 7), 1.0, 0.0)
        low = jnp.where(lane_iota == (column & (lanes - 1)), share_ref[n : n + 1], 0.0)
        weight += dot(low, high, NT, precision=lax.Precision.HIGHEST)
    bias_ref[...] = jnp.where(weight > 0.0, jnp.log2(weight), ABSENT)

    spot = spot_ref[...]
    queries = spot.shape[1]
    line_iota = lax.broadcasted_iota(jnp.int32, (lines, queries), 0)
    picked = jnp.where(line_iota == spot // width, 1.0, 0.0).astype(BF16)
    found = jnp.zeros((width, queries), F32)
    for digit in range(3):
        part_of_word = ((words >> (8 * digit)) & 255).astype(F32).astype(BF16)
        found += dot(part_of_word, picked, TN) * float(256**digit)
    mine = lax.broadcasted_iota(jnp.int32, (width, queries), 0) == spot % width
    word = jnp.sum(jnp.where(mine, found, 0.0), axis=0, keepdims=True).astype(jnp.int32)
    pos, named = decoded(word)
    pos_ref[...] = pos
    logc_ref[...] = jnp.log(named)


def run_prepare(index, blocks, spot, part, rows, bounds, cand_local, n_cols, width):
    count, (height, across), nq = len(blocks), blocks[0].shape, spot.shape[1]
    lines = count * 4 * cand_local // across
    return pl.pallas_call(
        functools.partial(prepare_kernel, part, rows, bounds, count),
        in_specs=[pl.BlockSpec(memory_space=pltpu.SMEM)] + in_vmem(count + 1),
        out_specs=in_vmem(4),
        out_shape=[
            jax.ShapeDtypeStruct((128, n_cols // 128), F32),
            jax.ShapeDtypeStruct((1, nq), jnp.int32),
            jax.ShapeDtypeStruct((1, nq), F32),
            jax.ShapeDtypeStruct((2 * len(bounds), width), F32),
        ],
        scratch_shapes=[
            pltpu.VMEM((height - part, across), F32),
            pltpu.VMEM((lines, across), jnp.int32),
            pltpu.VMEM((lines, across), jnp.int32),
            pltpu.VMEM((lines, across), F32),
        ],
        compiler_params=pltpu.CompilerParams(vmem_limit_bytes=8 << 20),
    )(index, *blocks, spot)


def joined(mine, other, first):
    return jnp.where(
        first,
        jnp.concatenate([mine, other], axis=0),
        jnp.concatenate([other, mine], axis=0),
    )


def per_device(queries, item_table, cand_row, cand_owner, cand_count, positive, w_in, b_in, w_out):
    n_data = lax.axis_size("dp")
    n_model = lax.axis_size("mp")
    n_z = n_data // 4
    me = lax.axis_index("dp")
    my_model = lax.axis_index("mp")
    n_query, width_out = queries.shape
    rows, width_emb = item_table.shape
    units = w_in.shape[1]
    part = rows // n_model
    cand_local = cand_row.shape[0]
    n_cols = n_data * part
    chunk = n_z * part // 2
    scale = 1.0 / math.sqrt(width_out)
    tie = lax.optimization_barrier
    slice_at = functools.partial(lax.dynamic_slice, allow_negative_indices=False)
    core = me & 1
    half_rows = width_emb // 2
    query_part = n_query // n_model
    starts = [(my_model ^ k) * part for k in range(n_model)]
    share_starts = [(my_model ^ k) * query_part for k in range(n_model)]
    half_starts = [(core ^ k) * half_rows for k in range(2)]
    model_index = my_model.astype(jnp.int32).reshape(1)
    core_first = core == 0

    def place(rel):
        return ((rel >> 1) & 1) * (2 * n_z) + (rel & 1) * n_z + (rel >> 2)

    def bit_of(bits):
        return (me // bits) & 1

    pre = dot(item_table, w_in) + b_in[None, :]
    hidden = jnp.maximum(pre, 0.0).astype(BF16)
    partial = dot(hidden, w_out)

    def part_of(value, k):
        return slice_at(value, (starts[k], 0), (part, value.shape[1]))

    outgoing = [part_of(partial, k) for k in range(1, n_model)]
    arrived = [hop(outgoing[k - 1], k, "mp") for k in range(1, n_model)]
    outgoing, queries, cand_row = tie((outgoing, queries, cand_row))
    qt = queries.T
    packed = jnp.concatenate([w_in, w_out.reshape(width_emb, -1)], axis=1)
    piece = slice_at(packed, (half_starts[0], 0), (half_rows, packed.shape[1]))

    largest = jnp.max(jnp.abs(queries)).astype(F32)
    exponent = jnp.floor(jnp.log2(jnp.maximum(largest, 1e-6))).astype(jnp.int32) + 1
    exponent = jnp.clip(exponent + EXPONENT_BASE, 0, 63)
    word = (cand_owner[:, 0] * rows + cand_row) * COUNT_BASE + cand_count
    word = (word + exponent * (1 << WORD_BITS))[None, :]
    words = jnp.concatenate([word, hop(word, 1)], axis=0)
    words = jnp.concatenate([words, hop(words, 2)], axis=0)

    spot = (((positive // cand_local) ^ me) * cand_local + positive % cand_local)[None, :]
    both_index = jnp.stack([me, my_model]).astype(jnp.int32)
    ready = (qt, piece, spot, both_index, share_starts, half_starts, model_index, core_first)
    total, arrived, ready = tie((part_of(partial, 0), arrived, ready))
    qt, piece, spot, both_index, share_starts, half_starts, model_index, core_first = ready
    for other in arrived:
        total = total + other
    size = 4 * cand_local
    digits = jnp.stack([(words.reshape(size) >> shift) & 255 for shift in (0, 8, 16, 24)])
    tail_rows = -(-4 * size // (16 * width_out)) * 16
    digits = jnp.pad(digits.reshape(-1), (0, tail_rows * width_out - 4 * size))
    tail = digits.reshape(tail_rows, width_out).astype(BF16)
    payload = jnp.concatenate([total.astype(BF16), tail], axis=0)

    along_z = {0: payload}
    for j in range(n_z - 1, 0, -1):
        along_z[j] = hop(payload, j << 2)
    along_x = {j: hop(along_z[j], 2) for j in range(2)}
    along_z, along_x = tie((along_z, along_x))

    hidden_max = width_emb * TABLE_MAX * W_IN_MAX + B_IN_MAX
    gradient_sum = n_data * n_query * 2.0 * scale
    bounds = [
        2 * n_query * 2.0 * scale,
        4 * n_query * 2.0 * scale,
        gradient_sum * width_out * W_OUT_MAX * TABLE_MAX,
        gradient_sum * hidden_max,
    ]
    bias, pos_col, pos_logc, scales = run_prepare(
        both_index, [along_z[j] for j in range(n_z)], spot, part, rows, bounds, cand_local,
        n_cols, max(units, width_out),
    )
    factors = [scales[n : n + 1] for n in range(4)]
    growths = [scales[n + 4 : n + 5] for n in range(4)]
    own_mask = dot(item_table, packed[:, :units]) + b_in[None, :] > 0.0
    bias, own_mask = tie((bias, own_mask))

    halves = [range(h * n_z // 2, (h + 1) * n_z // 2) for h in range(2)]
    start_of = {
        (x, c, h): ((x * 2 + c) * 2 + h) * chunk for x in range(2) for c in range(2) for h in range(2)
    }
    items = {}
    m8 = jnp.full((8, n_query), ABSENT, F32)
    l8 = jnp.zeros((8, n_query), F32)

    def gathered(x, h, blocks):
        items[x, 0, h] = [blocks[j] for j in halves[h]]
        items[x, 1, h] = [hop(v, 1) for v in items[x, 0, h]]

    def statistics(m, l, *chosen):
        for key in chosen:
            m, l = run_stats(items[key], part, qt, bias, m, l, scale * LOG2E, start_of[key], False)
        return m, l

    for j in range(2, n_z):
        along_x[j] = hop(along_z[j], 2)
    gathered(0, 0, along_z)
    m8, l8 = statistics(m8, l8, (0, 0, 0), (0, 1, 0))
    along_x, m8, l8 = tie((along_x, m8, l8))
    gathered(0, 1, along_z)
    m8, l8 = statistics(m8, l8, (0, 0, 1), (0, 1, 1))
    gathered(1, 0, along_x)
    m8, l8 = statistics(m8, l8, (1, 0, 0))
    gathered(1, 1, along_x)
    m8, l8 = statistics(m8, l8, (1, 1, 0), (1, 0, 1))
    (local,) = run_stats(
        items[1, 1, 1], part, qt, bias, m8, l8, scale * LOG2E, start_of[1, 1, 1], True
    )
    lse = run_lse(model_index, [local] + [hop(local, k, "mp") for k in range(1, n_model)])

    piece, b_late, lse = tie((piece, b_in[None, :], lse))
    others = [(hop(piece, k, "mp"), hop(b_late, k, "mp")) for k in range(1, n_model)]

    qg = jnp.zeros((width_out, n_query), F32)
    sp = jnp.zeros((8, n_query), F32)
    chip_sums, crossed, z_sums = {}, {}, [None] * n_z

    def gradients(key, qg, sp, more=()):
        return run_grad(
            items[key], part, more, qt, queries, bias, lse, pos_col, qg, sp,
            scale, start_of[key],
        )

    siblings, crossing = {}, {}
    for h in (1, 0):
        sums, qg, sp = gradients((1, 1, h), qg, sp)
        siblings[1, h] = [hop(v, 1) for v in sums]
    for h in (1, 0):
        chip_sums[1, h], qg, sp = gradients((1, 0, h), qg, sp, siblings[1, h])
        crossing[h], qg = tie(
            ((jnp.concatenate(chip_sums[1, h], axis=0) * factors[0][:, :width_out]).astype(F16), qg)
        )
        crossed[h] = hop(crossing[h], 2)
    for h in (1, 0):
        sums, qg, sp = gradients((0, 1, h), qg, sp)
        siblings[0, h] = [hop(v, 1) for v in sums]
    for h in (1, 0):
        crossed[h], qg = tie((crossed[h], qg))
        chip_sums[0, h], qg, sp = gradients((0, 0, h), qg, sp, siblings[0, h])
        for j in range(n_z // 2):
            over = crossed[h][j * part : (j + 1) * part].astype(F32) * growths[0][:, :width_out]
            z_sums[h * n_z // 2 + j] = chip_sums[0, h][j] + over
    own_sum = z_sums[0]
    for j in range(n_z - 1, 0, -1):
        sent = hop((z_sums[j] * factors[1][:, :width_out]).astype(F16), j << 2)
        own_sum = own_sum + sent.astype(F32) * growths[1][:, :width_out]
    own_grad, others = tie((own_sum.astype(BF16), others))
    others = [(joined(got, hop(got, 1), core_first), b) for got, b in others]
    weights = [(packed, b_in[None, :])] + others
    if n_model > 2:
        turn = jnp.arange(n_model) ^ my_model
        stacks = [jnp.take(jnp.stack(group), turn, axis=0) for group in zip(*weights)]
        weights = [(stacks[0][k], stacks[1][k]) for k in range(n_model)]
    weights = [(w[:, :units], w[:, units:].reshape(units, width_out), b) for w, b in weights]
    masks = [dot(item_table, share_in) + b > 0.0 for share_in, _, b in weights]
    if n_model == 2:
        masks[0] = own_mask


    grads = [own_grad] + [hop(own_grad, k, "mp") for k in range(1, n_model)]
    grads, masks = tie((grads, masks))
    item_grad, pre_grad, local_b, value = run_backward(
        model_index, scales, grads, pre, hidden, item_table, w_out
    )

    width = value.shape[1]
    keep, give = (slice_at(value, (half_starts[k], 0), (half_rows, width)) for k in range(2))
    bias_steps = [1 << n for n in range(n_data.bit_length() - 1)]
    bias_steps = bias_steps[:1] + bias_steps[:0:-1]

    def step_bias(value, steps):
        for _ in range(min(steps, len(bias_steps))):
            bits = bias_steps.pop(0)
            value = value + hop(value, bits)
        return value

    value = (keep + hop(give.astype(F16), 1).astype(F32)).astype(F16)
    value, local_b = tie((value, step_bias(local_b, 1)))
    chips = n_data // 2
    groups = [[2 * chip + c for chip in range(chips)] for c in range(2)]

    def exchange(blocks):
        return lax.all_to_all(
            blocks, "dp", split_axis=0, concat_axis=0, axis_index_groups=groups, tiled=True
        )

    size = half_rows // chips
    grad_table = None
    for (share_in, share_out, _), mask in zip(weights, masks):
        back = jnp.where(mask, dot(item_grad, share_out, NT), 0.0).astype(BF16)
        term = dot(back, share_in, NT)
        grad_table = term if grad_table is None else grad_table + term

    pieces = exchange(value.reshape(chips, size, width))
    pieces, grad_table = tie((pieces, grad_table))
    total = jnp.sum(pieces.astype(F32), axis=0).astype(F16)
    total, local_b = tie((total, step_bias(local_b, 9)))
    own_half = exchange(jnp.broadcast_to(total[None], (chips, size, width)))
    own_half = own_half.reshape(half_rows, width)

    local_b, qg, sp = tie((local_b, qg, sp))

    item_max = n_model * units * hidden_max * W_OUT_MAX
    q_factor = LIMIT / (2.0 * item_max)
    sp1 = jnp.sum(sp, axis=0)[None, :]
    qg_parts = [
        slice_at(qg, (0, share_starts[k]), (width_out, query_part))
        for k in range(n_model)
    ]
    pos_score, query_sum = sp1, qg_parts[0]
    for k in range(1, n_model):
        sent = hop((qg_parts[k] * q_factor).astype(F16), k, "mp")
        query_sum = query_sum + sent.astype(F32) * (1.0 / q_factor)
        pos_score = pos_score + hop(sp1, k, "mp")
    loss = lse[0] * (1.0 / LOG2E) - (pos_score[0] * scale - pos_logc[0])
    query_grad = (query_sum * scale).T

    sides = [own_half, hop(own_half, 1)]
    sides_in = [v[:, :units].astype(F32) * growths[2][:, :units] for v in sides]
    tail_width = width - units
    sides_out = [v[:, units:].astype(F32) * growths[3][:, :tail_width] for v in sides]
    grad_w_in = joined(*sides_in, core_first)
    grad_w_out = joined(*sides_out, core_first).reshape(units, width_out)
    return (loss, query_grad, grad_w_in, local_b[0], grad_w_out, grad_table)


def solution(mesh):
    placed = (
        P("dp", None),
        P("dp", None),
        P("dp"),
        P("dp", None),
        P("dp"),
        P("dp"),
        P(None, "mp"),
        P("mp"),
        P("mp", None),
    )
    return jax.shard_map(
        per_device,
        mesh=mesh,
        in_specs=placed,
        out_specs=(
            P("dp"),
            P(("dp", "mp"), None),
            P(None, "mp"),
            P("mp"),
            P("mp", None),
            P("dp", None),
        ),
        check_vma=False,
    )
```

```python
import functools
import math

import jax
import jax.numpy as jnp
from jax import lax
from jax.experimental import pallas as pl
from jax.experimental.pallas import tpu as pltpu
from jax.sharding import PartitionSpec as P

F32 = jnp.float32
BF16 = jnp.bfloat16
F16 = jnp.float16
ABSENT = -1e30
COUNT_BASE = 128
WORD_BITS = 22
EXPONENT_BASE = 20
TABLE_MAX = 6.0
W_IN_MAX = 0.25
B_IN_MAX = 3.0
W_OUT_MAX = 0.1875
LIMIT = 32768.0
LOG2E = math.log2(math.e)
GROUP = 16
NT = (((1,), (1,)), ((), ()))
TN = (((0,), (0,)), ((), ()))


def hop(value, bits, axis="dp"):
    size = lax.axis_size(axis)
    return lax.ppermute(value, axis, [(i, i ^ bits) for i in range(size)])


def dot(a, b, dims=None, **kw):
    if dims is None:
        dims = (((1,), (0,)), ((), ()))
    return lax.dot_general(a, b, dims, preferred_element_type=F32, **kw)


def column_bias(bias_ref, first, count):
    lane = first // 128
    return bias_ref[pl.ds(first % 128, count), lane : lane + 1]


def stats_kernel(scale, base, count, last, *refs):
    items_refs, refs = refs[:count], refs[count:]
    qt_ref, bias_ref, m_in_ref, l_in_ref, m_ref, *score_refs = refs
    l_ref = None if last else score_refs.pop(0)
    block = score_refs[0].shape[0]
    old = m_in_ref[...]
    new = old
    for items_ref, score_ref in zip(items_refs, score_refs):
        score_ref[...] = dot(items_ref[0:block], qt_ref[...])
    for n, score_ref in enumerate(score_refs):
        for r in range(0, block, 8):
            bias = column_bias(bias_ref, base + n * block + r, 8)
            score = score_ref[r : r + 8] * scale + bias
            score_ref[r : r + 8] = score
            new = jnp.maximum(new, score)
    total = l_in_ref[...] * jnp.exp2(old - new)
    for score_ref in score_refs:
        for r in range(0, block, 8):
            total = total + jnp.exp2(score_ref[r : r + 8] - new)
    if last:
        top = jnp.max(new, axis=0, keepdims=True)
        m_ref[0:1] = top
        m_ref[1:2] = jnp.sum(total * jnp.exp2(new - top), axis=0, keepdims=True)
    else:
        m_ref[...] = new
        l_ref[...] = total


def in_vmem(count):
    return [pl.BlockSpec(memory_space=pltpu.VMEM)] * count


def run_stats(items, block, qt, bias, m, l, scale, base, last):
    count, nq = len(items), qt.shape[1]
    shapes = [(2, nq)] if last else [(8, nq)] * 2
    return pl.pallas_call(
        functools.partial(stats_kernel, scale, base, count, last),
        in_specs=in_vmem(count + 4),
        out_specs=in_vmem(len(shapes)),
        out_shape=[jax.ShapeDtypeStruct(shape, F32) for shape in shapes],
        scratch_shapes=[pltpu.VMEM((block, nq), F32)] * count,
        compiler_params=pltpu.CompilerParams(vmem_limit_bytes=6 << 20),
    )(*items, qt, bias, m, l)


def lse_kernel(count, index_ref, *refs):
    part_refs, (lse_ref, held_ref) = refs[:count], refs[count:]
    for k in range(count):
        held_ref[index_ref[0] ^ k] = part_refs[k][...]
    parts = [held_ref[k] for k in range(count)]
    top = functools.reduce(jnp.maximum, [p[0:1] for p in parts])
    total = functools.reduce(jnp.add, [p[1:2] * jnp.exp2(p[0:1] - top) for p in parts])
    lse_ref[...] = top + jnp.log2(total)


def run_lse(index, parts):
    nq = parts[0].shape[1]
    return pl.pallas_call(
        functools.partial(lse_kernel, len(parts)),
        in_specs=[pl.BlockSpec(memory_space=pltpu.SMEM)] + in_vmem(len(parts)),
        out_specs=in_vmem(1)[0],
        out_shape=jax.ShapeDtypeStruct((1, nq), F32),
        scratch_shapes=[pltpu.VMEM((len(parts), 2, nq), F32)],
        compiler_params=pltpu.CompilerParams(vmem_limit_bytes=2 << 20),
    )(index, *parts)


def grad_kernel(scale, base, count, add, *refs):
    items_refs, refs = refs[:count], refs[count:]
    more_refs, refs = refs[:add], refs[add:]
    qt_ref, q_ref, bias_ref, lse_ref, pos_ref, qg_in_ref, sp_in_ref, *refs = refs
    sums_refs, (qg_ref, sp_ref, *scratch) = refs[:count], refs[count:]
    score_refs, prob_refs = scratch[:count], scratch[count:]
    block, queries = score_refs[0].shape
    for items_ref, score_ref in zip(items_refs, score_refs):
        score_ref[...] = dot(items_ref[0:block], qt_ref[...])
    down = lax.broadcasted_iota(jnp.int32, (8, queries), 0)
    offset = jnp.broadcast_to(pos_ref[...], (8, queries)) - down
    lse = jnp.broadcast_to(lse_ref[...], (8, queries))
    found = sp_in_ref[...]
    for n in range(count):
        score_ref, prob_ref = score_refs[n], prob_refs[n]
        for r in range(0, block, GROUP):
            pieces = []
            for s in range(r, r + GROUP, 8):
                at = base + n * block + s
                score = score_ref[s : s + 8]
                here = offset == at
                found = found + jnp.where(here, score, 0.0)
                prob = jnp.exp2((score * (scale * LOG2E) + column_bias(bias_ref, at, 8)) - lse)
                pieces.append(jnp.where(here, prob - 1.0, prob))
            prob_ref[r : r + GROUP] = jnp.concatenate(pieces, axis=0).astype(BF16)
        sums = dot(prob_ref[...], q_ref[...]) * scale
        sums_refs[n][...] = sums + more_refs[n][...] if add else sums
        share = dot(items_refs[n][0:block], prob_ref[...], TN)
        qg_ref[...] = (qg_in_ref[...] if n == 0 else qg_ref[...]) + share
    sp_ref[...] = found


def run_grad(items, block, more, qt, q, bias, lse, pos, qg, sp, scale, base):
    count, (width, nq) = len(items), qt.shape
    before = count + len(more)
    *sums, qg, sp = pl.pallas_call(
        functools.partial(grad_kernel, scale, base, count, len(more)),
        in_specs=in_vmem(before + 7),
        out_specs=in_vmem(count + 2),
        out_shape=[jax.ShapeDtypeStruct((block, width), F32)] * count
        + [jax.ShapeDtypeStruct((width, nq), F32), jax.ShapeDtypeStruct((8, nq), F32)],
        scratch_shapes=[pltpu.VMEM((block, nq), F32)] * count
        + [pltpu.VMEM((block, nq), BF16)] * count,
        input_output_aliases={before + 5: count, before + 6: count + 1},
        compiler_params=pltpu.CompilerParams(vmem_limit_bytes=8 << 20),
    )(*items, *more, qt, q, bias, lse, pos, qg, sp)
    return sums, qg, sp


def backward_kernel(count, index_ref, scale_ref, *refs):
    grad_refs, (pre_ref, hidden_ref, emb_ref, w_out_ref) = refs[:count], refs[count : count + 4]
    grad_ref, pre_grad_ref, b_ref, *sums_refs = refs[count + 4 :]
    part = grad_refs[0].shape[0]
    for k in range(count):
        start = pl.multiple_of((index_ref[0] ^ k) * part, part)
        grad_ref[pl.ds(start, part)] = grad_refs[k][...]
    back = dot(grad_ref[...], w_out_ref[...], NT)
    pre_grad = jnp.where(pre_ref[...] > 0.0, back, 0.0).astype(BF16)
    pre_grad_ref[...] = pre_grad
    b_ref[...] = jnp.sum(pre_grad.astype(F32), axis=0, keepdims=True)
    sums_in = dot(emb_ref[...], pre_grad, TN) * scale_ref[2:3, : pre_grad.shape[1]]
    sums_out = dot(hidden_ref[...], grad_ref[...], TN) * scale_ref[3:4, : grad_ref.shape[1]]
    if len(sums_refs) == 1:
        units = sums_in.shape[1]
        sums_refs[0][:, :units] = sums_in
        sums_refs[0][:, units:] = sums_out
    else:
        sums_refs[0][...] = sums_in
        sums_refs[1][...] = sums_out


def run_backward(index, scales, grads, pre, hidden, emb, w_out):
    rows, units = pre.shape
    width_emb, width_out = emb.shape[1], w_out.shape[1]
    if units == width_emb:
        sums = [(width_emb, units + width_out)]
    else:
        sums = [(width_emb, units), (units, width_out)]
    grad, pre_grad, local_b, *sums = pl.pallas_call(
        functools.partial(backward_kernel, len(grads)),
        in_specs=[pl.BlockSpec(memory_space=pltpu.SMEM)] + in_vmem(len(grads) + 5),
        out_specs=in_vmem(3 + len(sums)),
        out_shape=[
            jax.ShapeDtypeStruct((rows, width_out), BF16),
            jax.ShapeDtypeStruct((rows, units), BF16),
            jax.ShapeDtypeStruct((1, units), F32),
        ]
        + [jax.ShapeDtypeStruct(shape, F32) for shape in sums],
        compiler_params=pltpu.CompilerParams(vmem_limit_bytes=12 << 20),
    )(index, scales, *grads, pre, hidden, emb, w_out)
    if len(sums) > 1:
        sums = [jnp.concatenate([sums[0], sums[1].reshape(width_emb, -1)], axis=1)]
    return grad, pre_grad, local_b, sums[0]


def prepare_kernel(part, rows, bounds, count, index_ref, *refs):
    block_refs, refs = refs[:count], refs[count:]
    spot_ref, bias_ref, pos_ref, logc_ref, scale_ref, tail_ref, words_ref, col_ref, share_ref = refs
    lines, width = words_ref.shape
    run = lines // count
    lanes = 128
    for z in range(count):
        tail_ref[...] = block_refs[z][part : part + tail_ref.shape[0]].astype(F32)
        for r in range(run):
            value = tail_ref[r : r + 1].astype(jnp.int32)
            for digit in range(1, 4):
                at = digit * run + r
                value += tail_ref[at : at + 1].astype(jnp.int32) << (8 * digit)
            words_ref[z * run + r : z * run + r + 1] = value
    words = words_ref[...]
    exponent = jnp.max(words >> WORD_BITS, axis=1, keepdims=True)
    exponent = jnp.max(exponent, axis=0, keepdims=True) - EXPONENT_BASE
    largest = jnp.exp2(jnp.broadcast_to(exponent.astype(F32), (1, scale_ref.shape[1])))
    for n, bound in enumerate(bounds):
        scale_ref[n : n + 1] = (LIMIT / bound) / largest
        scale_ref[n + len(bounds) : n + len(bounds) + 1] = largest * (bound / LIMIT)

    count_bits, row_bits, part_bits = (n.bit_length() - 1 for n in (COUNT_BASE, rows, part))

    def decoded(word):
        row = (word >> count_bits) & (rows - 1)
        rel = (word >> (count_bits + row_bits)) ^ index_ref[0]
        place = ((rel >> 1) & 1) * (2 * count) + (rel & 1) * count + (rel >> 2)
        column = place * part + (row & (part - 1))
        named = (word & (COUNT_BASE - 1)).astype(F32)
        return jnp.where((row >> part_bits) == index_ref[1], column, -1), named

    words = words & ((1 << WORD_BITS) - 1)
    column, named = decoded(words)
    col_ref[...] = column
    share_ref[...] = 1.0 / named
    blocks = bias_ref.shape[1]
    weight = jnp.zeros((lanes, blocks), F32)
    block_iota = lax.broadcasted_iota(jnp.int32, (blocks, width), 0)
    lane_iota = lax.broadcasted_iota(jnp.int32, (lanes, width), 0)
    for n in range(lines):
        column = col_ref[n : n + 1]
        high = jnp.where(block_iota == (column >> 7), 1.0, 0.0)
        low = jnp.where(lane_iota == (column & (lanes - 1)), share_ref[n : n + 1], 0.0)
        weight += dot(low, high, NT, precision=lax.Precision.HIGHEST)
    bias_ref[...] = jnp.where(weight > 0.0, jnp.log2(weight), ABSENT)

    spot = spot_ref[...]
    queries = spot.shape[1]
    line_iota = lax.broadcasted_iota(jnp.int32, (lines, queries), 0)
    picked = jnp.where(line_iota == spot // width, 1.0, 0.0).astype(BF16)
    found = jnp.zeros((width, queries), F32)
    for digit in range(3):
        part_of_word = ((words >> (8 * digit)) & 255).astype(F32).astype(BF16)
        found += dot(part_of_word, picked, TN) * float(256**digit)
    mine = lax.broadcasted_iota(jnp.int32, (width, queries), 0) == spot % width
    word = jnp.sum(jnp.where(mine, found, 0.0), axis=0, keepdims=True).astype(jnp.int32)
    pos, named = decoded(word)
    pos_ref[...] = pos
    logc_ref[...] = jnp.log(named)


def run_prepare(index, blocks, spot, part, rows, bounds, cand_local, n_cols, width):
    count, (height, across), nq = len(blocks), blocks[0].shape, spot.shape[1]
    lines = count * 4 * cand_local // across
    return pl.pallas_call(
        functools.partial(prepare_kernel, part, rows, bounds, count),
        in_specs=[pl.BlockSpec(memory_space=pltpu.SMEM)] + in_vmem(count + 1),
        out_specs=in_vmem(4),
        out_shape=[
            jax.ShapeDtypeStruct((128, n_cols // 128), F32),
            jax.ShapeDtypeStruct((1, nq), jnp.int32),
            jax.ShapeDtypeStruct((1, nq), F32),
            jax.ShapeDtypeStruct((2 * len(bounds), width), F32),
        ],
        scratch_shapes=[
            pltpu.VMEM((height - part, across), F32),
            pltpu.VMEM((lines, across), jnp.int32),
            pltpu.VMEM((lines, across), jnp.int32),
            pltpu.VMEM((lines, across), F32),
        ],
        compiler_params=pltpu.CompilerParams(vmem_limit_bytes=8 << 20),
    )(index, *blocks, spot)


def joined(mine, other, first):
    return jnp.where(
        first,
        jnp.concatenate([mine, other], axis=0),
        jnp.concatenate([other, mine], axis=0),
    )


def per_device(queries, item_table, cand_row, cand_owner, cand_count, positive, w_in, b_in, w_out):
    n_data = lax.axis_size("dp")
    n_model = lax.axis_size("mp")
    n_z = n_data // 4
    me = lax.axis_index("dp")
    my_model = lax.axis_index("mp")
    n_query, width_out = queries.shape
    rows, width_emb = item_table.shape
    units = w_in.shape[1]
    part = rows // n_model
    cand_local = cand_row.shape[0]
    n_cols = n_data * part
    chunk = n_z * part // 2
    scale = 1.0 / math.sqrt(width_out)
    tie = lax.optimization_barrier
    slice_at = functools.partial(lax.dynamic_slice, allow_negative_indices=False)
    core = me & 1
    half_rows = width_emb // 2
    query_part = n_query // n_model
    starts = [(my_model ^ k) * part for k in range(n_model)]
    share_starts = [(my_model ^ k) * query_part for k in range(n_model)]
    half_starts = [(core ^ k) * half_rows for k in range(2)]
    model_index = my_model.astype(jnp.int32).reshape(1)
    core_first = core == 0

    pre = dot(item_table, w_in) + b_in[None, :]
    hidden = jnp.maximum(pre, 0.0).astype(BF16)
    partial = dot(hidden, w_out)

    def part_of(value, k):
        return slice_at(value, (starts[k], 0), (part, value.shape[1]))

    outgoing = [part_of(partial, k) for k in range(1, n_model)]
    arrived = [hop(outgoing[k - 1], k, "mp") for k in range(1, n_model)]
    outgoing, queries, cand_row = tie((outgoing, queries, cand_row))
    qt = queries.T
    packed = jnp.concatenate([w_in, w_out.reshape(width_emb, -1)], axis=1)
    piece = slice_at(packed, (half_starts[0], 0), (half_rows, packed.shape[1]))

    largest = jnp.max(jnp.abs(queries)).astype(F32)
    exponent = jnp.floor(jnp.log2(jnp.maximum(largest, 1e-6))).astype(jnp.int32) + 1
    exponent = jnp.clip(exponent + EXPONENT_BASE, 0, 63)
    word = (cand_owner[:, 0] * rows + cand_row) * COUNT_BASE + cand_count
    word = (word + exponent * (1 << WORD_BITS))[None, :]
    words = jnp.concatenate([word, hop(word, 1)], axis=0)
    words = jnp.concatenate([words, hop(words, 2)], axis=0)

    spot = (((positive // cand_local) ^ me) * cand_local + positive % cand_local)[None, :]
    both_index = jnp.stack([me, my_model]).astype(jnp.int32)
    ready = (qt, piece, spot, both_index, share_starts, half_starts, model_index, core_first)
    total, arrived, ready = tie((part_of(partial, 0), arrived, ready))
    qt, piece, spot, both_index, share_starts, half_starts, model_index, core_first = ready
    for other in arrived:
        total = total + other
    size = 4 * cand_local
    digits = jnp.stack([(words.reshape(size) >> shift) & 255 for shift in (0, 8, 16, 24)])
    tail_rows = -(-4 * size // (16 * width_out)) * 16
    digits = jnp.pad(digits.reshape(-1), (0, tail_rows * width_out - 4 * size))
    tail = digits.reshape(tail_rows, width_out).astype(BF16)
    payload = jnp.concatenate([total.astype(BF16), tail], axis=0)

    along_z = {0: payload}
    for j in range(n_z - 1, 0, -1):
        along_z[j] = hop(payload, j << 2)
    along_x = {j: hop(along_z[j], 2) for j in range(2)}
    along_z, along_x = tie((along_z, along_x))

    hidden_max = width_emb * TABLE_MAX * W_IN_MAX + B_IN_MAX
    gradient_sum = n_data * n_query * 2.0 * scale
    bounds = [
        2 * n_query * 2.0 * scale,
        4 * n_query * 2.0 * scale,
        gradient_sum * width_out * W_OUT_MAX * TABLE_MAX,
        gradient_sum * hidden_max,
    ]
    bias, pos_col, pos_logc, scales = run_prepare(
        both_index, [along_z[j] for j in range(n_z)], spot, part, rows, bounds, cand_local,
        n_cols, max(units, width_out),
    )
    factors = [scales[n : n + 1] for n in range(4)]
    growths = [scales[n + 4 : n + 5] for n in range(4)]
    own_mask = dot(item_table, packed[:, :units]) + b_in[None, :] > 0.0
    bias, own_mask = tie((bias, own_mask))

    halves = [range(h * n_z // 2, (h + 1) * n_z // 2) for h in range(2)]
    start_of = {
        (x, c, h): ((x * 2 + c) * 2 + h) * chunk for x in range(2) for c in range(2) for h in range(2)
    }
    items = {}
    m8 = jnp.full((8, n_query), ABSENT, F32)
    l8 = jnp.zeros((8, n_query), F32)

    def gathered(x, h, blocks):
        items[x, 0, h] = [blocks[j] for j in halves[h]]
        items[x, 1, h] = [hop(v, 1) for v in items[x, 0, h]]

    def statistics(m, l, *chosen):
        for key in chosen:
            m, l = run_stats(items[key], part, qt, bias, m, l, scale * LOG2E, start_of[key], False)
        return m, l

    for j in range(2, n_z):
        along_x[j] = hop(along_z[j], 2)
    gathered(0, 0, along_z)
    m8, l8 = statistics(m8, l8, (0, 0, 0), (0, 1, 0))
    along_x, m8, l8 = tie((along_x, m8, l8))
    gathered(0, 1, along_z)
    m8, l8 = statistics(m8, l8, (0, 0, 1), (0, 1, 1))
    gathered(1, 0, along_x)
    m8, l8 = statistics(m8, l8, (1, 0, 0))
    gathered(1, 1, along_x)
    m8, l8 = statistics(m8, l8, (1, 1, 0), (1, 0, 1))
    (local,) = run_stats(
        items[1, 1, 1], part, qt, bias, m8, l8, scale * LOG2E, start_of[1, 1, 1], True
    )
    lse = run_lse(model_index, [local] + [hop(local, k, "mp") for k in range(1, n_model)])

    piece, b_late, lse = tie((piece, b_in[None, :], lse))
    others = [(hop(piece, k, "mp"), hop(b_late, k, "mp")) for k in range(1, n_model)]

    qg = jnp.zeros((width_out, n_query), F32)
    sp = jnp.zeros((8, n_query), F32)
    chip_sums, crossed = {}, {}

    def gradients(key, qg, sp, more=()):
        return run_grad(
            items[key], part, more, qt, queries, bias, lse, pos_col, qg, sp,
            scale, start_of[key],
        )

    siblings, crossing = {}, {}
    for h in (1, 0):
        sums, qg, sp = gradients((1, 1, h), qg, sp)
        siblings[1, h] = [hop(v, 1) for v in sums]
    for h in (1, 0):
        chip_sums[1, h], qg, sp = gradients((1, 0, h), qg, sp, siblings[1, h])
        crossing[h], qg = tie(
            ((jnp.concatenate(chip_sums[1, h], axis=0) * factors[0][:, :width_out]).astype(F16), qg)
        )
        crossed[h] = hop(crossing[h], 2)
    for h in (1, 0):
        sums, qg, sp = gradients((0, 1, h), qg, sp)
        siblings[0, h] = [hop(v, 1) for v in sums]
    leaving = {}
    for h in (1, 0):
        crossed[h], leaving, qg = tie((crossed[h], leaving, qg))
        chip_sums[0, h], qg, sp = gradients((0, 0, h), qg, sp, siblings[0, h])
        for j in range(n_z // 2):
            over = crossed[h][j * part : (j + 1) * part].astype(F32) * growths[0][:, :width_out]
            whole = chip_sums[0, h][j] + over
            place_z = h * n_z // 2 + j
            if place_z:
                leaving[place_z] = (whole * factors[1][:, :width_out]).astype(F16)
            else:
                own_sum = whole
    for j in range(n_z - 1, 0, -1):
        own_sum = own_sum + hop(leaving[j], j << 2).astype(F32) * growths[1][:, :width_out]
    own_grad, others = tie((own_sum.astype(BF16), others))
    others = [(joined(got, hop(got, 1), core_first), b) for got, b in others]
    weights = [(packed, b_in[None, :])] + others
    if n_model > 2:
        turn = jnp.arange(n_model) ^ my_model
        stacks = [jnp.take(jnp.stack(group), turn, axis=0) for group in zip(*weights)]
        weights = [(stacks[0][k], stacks[1][k]) for k in range(n_model)]
    weights = [(w[:, :units], w[:, units:].reshape(units, width_out), b) for w, b in weights]
    masks = [dot(item_table, share_in) + b > 0.0 for share_in, _, b in weights]
    if n_model == 2:
        masks[0] = own_mask


    grads = [own_grad] + [hop(own_grad, k, "mp") for k in range(1, n_model)]
    grads, masks = tie((grads, masks))
    item_grad, pre_grad, local_b, value = run_backward(
        model_index, scales, grads, pre, hidden, item_table, w_out
    )

    width = value.shape[1]
    keep, give = (slice_at(value, (half_starts[k], 0), (half_rows, width)) for k in range(2))
    bias_steps = [1 << n for n in range(n_data.bit_length() - 1)]

    def step_bias(value, steps):
        for _ in range(min(steps, len(bias_steps))):
            bits = bias_steps.pop(0)
            value = value + hop(value, bits)
        return value

    value = (keep + hop(give.astype(F16), 1).astype(F32)).astype(F16)
    value, local_b = tie((value, step_bias(local_b, 1)))
    chips = n_data // 2
    groups = [[2 * chip + c for chip in range(chips)] for c in range(2)]

    def exchange(blocks):
        return lax.all_to_all(
            blocks, "dp", split_axis=0, concat_axis=0, axis_index_groups=groups, tiled=True
        )

    size = half_rows // chips
    grad_table = None
    for (share_in, share_out, _), mask in zip(weights, masks):
        back = jnp.where(mask, dot(item_grad, share_out, NT), 0.0).astype(BF16)
        term = dot(back, share_in, NT)
        grad_table = term if grad_table is None else grad_table + term

    pieces = exchange(value.reshape(chips, size, width))
    pieces, grad_table = tie((pieces, grad_table))
    total = jnp.sum(pieces.astype(F32), axis=0).astype(F16)
    total, local_b = tie((total, step_bias(local_b, 9)))
    own_half = exchange(jnp.broadcast_to(total[None], (chips, size, width)))
    own_half = own_half.reshape(half_rows, width)

    local_b, qg, sp = tie((local_b, qg, sp))

    item_max = n_model * units * hidden_max * W_OUT_MAX
    q_factor = LIMIT / (2.0 * item_max)
    sp1 = jnp.sum(sp, axis=0)[None, :]
    qg_parts = [
        slice_at(qg, (0, share_starts[k]), (width_out, query_part))
        for k in range(n_model)
    ]
    pos_score, query_sum = sp1, qg_parts[0]
    for k in range(1, n_model):
        sent = hop((qg_parts[k] * q_factor).astype(F16), k, "mp")
        query_sum = query_sum + sent.astype(F32) * (1.0 / q_factor)
        pos_score = pos_score + hop(sp1, k, "mp")
    loss = lse[0] * (1.0 / LOG2E) - (pos_score[0] * scale - pos_logc[0])
    query_grad = (query_sum * scale).T

    sides = [own_half, hop(own_half, 1)]
    sides_in = [v[:, :units].astype(F32) * growths[2][:, :units] for v in sides]
    tail_width = width - units
    sides_out = [v[:, units:].astype(F32) * growths[3][:, :tail_width] for v in sides]
    grad_w_in = joined(*sides_in, core_first)
    grad_w_out = joined(*sides_out, core_first).reshape(units, width_out)
    return (loss, query_grad, grad_w_in, local_b[0], grad_w_out, grad_table)


def solution(mesh):
    placed = (
        P("dp", None),
        P("dp", None),
        P("dp"),
        P("dp", None),
        P("dp"),
        P("dp"),
        P(None, "mp"),
        P("mp"),
        P("mp", None),
    )
    return jax.shard_map(
        per_device,
        mesh=mesh,
        in_specs=placed,
        out_specs=(
            P("dp"),
            P(("dp", "mp"), None),
            P(None, "mp"),
            P("mp"),
            P("mp", None),
            P("dp", None),
        ),
        check_vma=False,
    )
```

```python
import functools
import math

import jax
import jax.numpy as jnp
from jax import lax
from jax.experimental import pallas as pl
from jax.experimental.pallas import tpu as pltpu
from jax.sharding import PartitionSpec as P

F32 = jnp.float32
BF16 = jnp.bfloat16
F16 = jnp.float16
ABSENT = -1e30
COUNT_BASE = 128
WORD_BITS = 22
EXPONENT_BASE = 20
TABLE_MAX = 6.0
W_IN_MAX = 0.25
B_IN_MAX = 3.0
W_OUT_MAX = 0.1875
LIMIT = 32768.0
LOG2E = math.log2(math.e)
GROUP = 16
NT = (((1,), (1,)), ((), ()))
TN = (((0,), (0,)), ((), ()))


def hop(value, bits, axis="dp"):
    size = lax.axis_size(axis)
    return lax.ppermute(value, axis, [(i, i ^ bits) for i in range(size)])


def dot(a, b, dims=None, **kw):
    if dims is None:
        dims = (((1,), (0,)), ((), ()))
    return lax.dot_general(a, b, dims, preferred_element_type=F32, **kw)


def column_bias(bias_ref, first, count):
    lane = first // 128
    return bias_ref[pl.ds(first % 128, count), lane : lane + 1]


def stats_kernel(scale, base, count, last, *refs):
    items_refs, refs = refs[:count], refs[count:]
    qt_ref, bias_ref, m_in_ref, l_in_ref, m_ref, *score_refs = refs
    l_ref = None if last else score_refs.pop(0)
    block = score_refs[0].shape[0]
    old = m_in_ref[...]
    new = old
    for items_ref, score_ref in zip(items_refs, score_refs):
        score_ref[...] = dot(items_ref[0:block], qt_ref[...])
    for n, score_ref in enumerate(score_refs):
        for r in range(0, block, 8):
            bias = column_bias(bias_ref, base + n * block + r, 8)
            score = score_ref[r : r + 8] * scale + bias
            score_ref[r : r + 8] = score
            new = jnp.maximum(new, score)
    total = l_in_ref[...] * jnp.exp2(old - new)
    for score_ref in score_refs:
        for r in range(0, block, 8):
            total = total + jnp.exp2(score_ref[r : r + 8] - new)
    if last:
        top = jnp.max(new, axis=0, keepdims=True)
        m_ref[0:1] = top
        m_ref[1:2] = jnp.sum(total * jnp.exp2(new - top), axis=0, keepdims=True)
    else:
        m_ref[...] = new
        l_ref[...] = total


def in_vmem(count):
    return [pl.BlockSpec(memory_space=pltpu.VMEM)] * count


def run_stats(items, block, qt, bias, m, l, scale, base, last):
    count, nq = len(items), qt.shape[1]
    shapes = [(2, nq)] if last else [(8, nq)] * 2
    return pl.pallas_call(
        functools.partial(stats_kernel, scale, base, count, last),
        in_specs=in_vmem(count + 4),
        out_specs=in_vmem(len(shapes)),
        out_shape=[jax.ShapeDtypeStruct(shape, F32) for shape in shapes],
        scratch_shapes=[pltpu.VMEM((block, nq), F32)] * count,
        compiler_params=pltpu.CompilerParams(vmem_limit_bytes=6 << 20),
    )(*items, qt, bias, m, l)


def lse_kernel(count, index_ref, *refs):
    part_refs, (lse_ref, held_ref) = refs[:count], refs[count:]
    for k in range(count):
        held_ref[index_ref[0] ^ k] = part_refs[k][...]
    parts = [held_ref[k] for k in range(count)]
    top = functools.reduce(jnp.maximum, [p[0:1] for p in parts])
    total = functools.reduce(jnp.add, [p[1:2] * jnp.exp2(p[0:1] - top) for p in parts])
    lse_ref[...] = top + jnp.log2(total)


def run_lse(index, parts):
    nq = parts[0].shape[1]
    return pl.pallas_call(
        functools.partial(lse_kernel, len(parts)),
        in_specs=[pl.BlockSpec(memory_space=pltpu.SMEM)] + in_vmem(len(parts)),
        out_specs=in_vmem(1)[0],
        out_shape=jax.ShapeDtypeStruct((1, nq), F32),
        scratch_shapes=[pltpu.VMEM((len(parts), 2, nq), F32)],
        compiler_params=pltpu.CompilerParams(vmem_limit_bytes=2 << 20),
    )(index, *parts)


def grad_kernel(scale, base, count, add, *refs):
    items_refs, refs = refs[:count], refs[count:]
    more_refs, refs = refs[:add], refs[add:]
    qt_ref, q_ref, bias_ref, lse_ref, pos_ref, qg_in_ref, sp_in_ref, *refs = refs
    sums_refs, (qg_ref, sp_ref, *scratch) = refs[:count], refs[count:]
    score_refs, prob_refs = scratch[:count], scratch[count:]
    block, queries = score_refs[0].shape
    for items_ref, score_ref in zip(items_refs, score_refs):
        score_ref[...] = dot(items_ref[0:block], qt_ref[...])
    down = lax.broadcasted_iota(jnp.int32, (8, queries), 0)
    offset = jnp.broadcast_to(pos_ref[...], (8, queries)) - down
    lse = jnp.broadcast_to(lse_ref[...], (8, queries))
    found = sp_in_ref[...]
    for n in range(count):
        score_ref, prob_ref = score_refs[n], prob_refs[n]
        for r in range(0, block, GROUP):
            pieces = []
            for s in range(r, r + GROUP, 8):
                at = base + n * block + s
                score = score_ref[s : s + 8]
                here = offset == at
                found = found + jnp.where(here, score, 0.0)
                prob = jnp.exp2((score * (scale * LOG2E) + column_bias(bias_ref, at, 8)) - lse)
                pieces.append(jnp.where(here, prob - 1.0, prob))
            prob_ref[r : r + GROUP] = jnp.concatenate(pieces, axis=0).astype(BF16)
        sums = dot(prob_ref[...], q_ref[...]) * scale
        sums_refs[n][...] = sums + more_refs[n][...] if add else sums
        share = dot(items_refs[n][0:block], prob_ref[...], TN)
        qg_ref[...] = (qg_in_ref[...] if n == 0 else qg_ref[...]) + share
    sp_ref[...] = found


def run_grad(items, block, more, qt, q, bias, lse, pos, qg, sp, scale, base):
    count, (width, nq) = len(items), qt.shape
    before = count + len(more)
    *sums, qg, sp = pl.pallas_call(
        functools.partial(grad_kernel, scale, base, count, len(more)),
        in_specs=in_vmem(before + 7),
        out_specs=in_vmem(count + 2),
        out_shape=[jax.ShapeDtypeStruct((block, width), F32)] * count
        + [jax.ShapeDtypeStruct((width, nq), F32), jax.ShapeDtypeStruct((8, nq), F32)],
        scratch_shapes=[pltpu.VMEM((block, nq), F32)] * count
        + [pltpu.VMEM((block, nq), BF16)] * count,
        input_output_aliases={before + 5: count, before + 6: count + 1},
        compiler_params=pltpu.CompilerParams(vmem_limit_bytes=8 << 20),
    )(*items, *more, qt, q, bias, lse, pos, qg, sp)
    return sums, qg, sp


def backward_kernel(count, index_ref, scale_ref, *refs):
    grad_refs, (pre_ref, hidden_ref, emb_ref, w_out_ref) = refs[:count], refs[count : count + 4]
    grad_ref, pre_grad_ref, b_ref, *sums_refs = refs[count + 4 :]
    part = grad_refs[0].shape[0]
    for k in range(count):
        start = pl.multiple_of((index_ref[0] ^ k) * part, part)
        grad_ref[pl.ds(start, part)] = grad_refs[k][...]
    back = dot(grad_ref[...], w_out_ref[...], NT)
    pre_grad = jnp.where(pre_ref[...] > 0.0, back, 0.0).astype(BF16)
    pre_grad_ref[...] = pre_grad
    b_ref[...] = jnp.sum(pre_grad.astype(F32), axis=0, keepdims=True)
    sums_in = dot(emb_ref[...], pre_grad, TN) * scale_ref[2:3, : pre_grad.shape[1]]
    sums_out = dot(hidden_ref[...], grad_ref[...], TN) * scale_ref[3:4, : grad_ref.shape[1]]
    if len(sums_refs) == 1:
        units = sums_in.shape[1]
        sums_refs[0][:, :units] = sums_in
        sums_refs[0][:, units:] = sums_out
    else:
        sums_refs[0][...] = sums_in
        sums_refs[1][...] = sums_out


def run_backward(index, scales, grads, pre, hidden, emb, w_out):
    rows, units = pre.shape
    width_emb, width_out = emb.shape[1], w_out.shape[1]
    if units == width_emb:
        sums = [(width_emb, units + width_out)]
    else:
        sums = [(width_emb, units), (units, width_out)]
    grad, pre_grad, local_b, *sums = pl.pallas_call(
        functools.partial(backward_kernel, len(grads)),
        in_specs=[pl.BlockSpec(memory_space=pltpu.SMEM)] + in_vmem(len(grads) + 5),
        out_specs=in_vmem(3 + len(sums)),
        out_shape=[
            jax.ShapeDtypeStruct((rows, width_out), BF16),
            jax.ShapeDtypeStruct((rows, units), BF16),
            jax.ShapeDtypeStruct((1, units), F32),
        ]
        + [jax.ShapeDtypeStruct(shape, F32) for shape in sums],
        compiler_params=pltpu.CompilerParams(vmem_limit_bytes=12 << 20),
    )(index, scales, *grads, pre, hidden, emb, w_out)
    if len(sums) > 1:
        sums = [jnp.concatenate([sums[0], sums[1].reshape(width_emb, -1)], axis=1)]
    return grad, pre_grad, local_b, sums[0]


def prepare_kernel(part, rows, bounds, count, index_ref, *refs):
    block_refs, refs = refs[:count], refs[count:]
    spot_ref, bias_ref, pos_ref, logc_ref, scale_ref, tail_ref, words_ref, col_ref, share_ref = refs
    lines, width = words_ref.shape
    run = lines // count
    lanes = 128
    for z in range(count):
        tail_ref[...] = block_refs[z][part : part + tail_ref.shape[0]].astype(F32)
        for r in range(run):
            value = tail_ref[r : r + 1].astype(jnp.int32)
            for digit in range(1, 4):
                at = digit * run + r
                value += tail_ref[at : at + 1].astype(jnp.int32) << (8 * digit)
            words_ref[z * run + r : z * run + r + 1] = value
    words = words_ref[...]
    exponent = jnp.max(words >> WORD_BITS, axis=1, keepdims=True)
    exponent = jnp.max(exponent, axis=0, keepdims=True) - EXPONENT_BASE
    largest = jnp.exp2(jnp.broadcast_to(exponent.astype(F32), (1, scale_ref.shape[1])))
    for n, bound in enumerate(bounds):
        scale_ref[n : n + 1] = (LIMIT / bound) / largest
        scale_ref[n + len(bounds) : n + len(bounds) + 1] = largest * (bound / LIMIT)

    count_bits, row_bits, part_bits = (n.bit_length() - 1 for n in (COUNT_BASE, rows, part))

    def decoded(word):
        row = (word >> count_bits) & (rows - 1)
        rel = (word >> (count_bits + row_bits)) ^ index_ref[0]
        place = ((rel >> 1) & 1) * (2 * count) + (rel & 1) * count + (rel >> 2)
        column = place * part + (row & (part - 1))
        named = (word & (COUNT_BASE - 1)).astype(F32)
        return jnp.where((row >> part_bits) == index_ref[1], column, -1), named

    words = words & ((1 << WORD_BITS) - 1)
    column, named = decoded(words)
    col_ref[...] = column
    share_ref[...] = 1.0 / named
    blocks = bias_ref.shape[1]
    weight = jnp.zeros((lanes, blocks), F32)
    block_iota = lax.broadcasted_iota(jnp.int32, (blocks, width), 0)
    lane_iota = lax.broadcasted_iota(jnp.int32, (lanes, width), 0)
    for n in range(lines):
        column = col_ref[n : n + 1]
        high = jnp.where(block_iota == (column >> 7), 1.0, 0.0)
        low = jnp.where(lane_iota == (column & (lanes - 1)), share_ref[n : n + 1], 0.0)
        weight += dot(low, high, NT, precision=lax.Precision.HIGHEST)
    bias_ref[...] = jnp.where(weight > 0.0, jnp.log2(weight), ABSENT)

    spot = spot_ref[...]
    queries = spot.shape[1]
    line_iota = lax.broadcasted_iota(jnp.int32, (lines, queries), 0)
    picked = jnp.where(line_iota == spot // width, 1.0, 0.0).astype(BF16)
    found = jnp.zeros((width, queries), F32)
    for digit in range(3):
        part_of_word = ((words >> (8 * digit)) & 255).astype(F32).astype(BF16)
        found += dot(part_of_word, picked, TN) * float(256**digit)
    mine = lax.broadcasted_iota(jnp.int32, (width, queries), 0) == spot % width
    word = jnp.sum(jnp.where(mine, found, 0.0), axis=0, keepdims=True).astype(jnp.int32)
    pos, named = decoded(word)
    pos_ref[...] = pos
    logc_ref[...] = jnp.log(named)


def run_prepare(index, blocks, spot, part, rows, bounds, cand_local, n_cols, width):
    count, (height, across), nq = len(blocks), blocks[0].shape, spot.shape[1]
    lines = count * 4 * cand_local // across
    return pl.pallas_call(
        functools.partial(prepare_kernel, part, rows, bounds, count),
        in_specs=[pl.BlockSpec(memory_space=pltpu.SMEM)] + in_vmem(count + 1),
        out_specs=in_vmem(4),
        out_shape=[
            jax.ShapeDtypeStruct((128, n_cols // 128), F32),
            jax.ShapeDtypeStruct((1, nq), jnp.int32),
            jax.ShapeDtypeStruct((1, nq), F32),
            jax.ShapeDtypeStruct((2 * len(bounds), width), F32),
        ],
        scratch_shapes=[
            pltpu.VMEM((height - part, across), F32),
            pltpu.VMEM((lines, across), jnp.int32),
            pltpu.VMEM((lines, across), jnp.int32),
            pltpu.VMEM((lines, across), F32),
        ],
        compiler_params=pltpu.CompilerParams(vmem_limit_bytes=8 << 20),
    )(index, *blocks, spot)


def joined(mine, other, first):
    return jnp.where(
        first,
        jnp.concatenate([mine, other], axis=0),
        jnp.concatenate([other, mine], axis=0),
    )


def per_device(queries, item_table, cand_row, cand_owner, cand_count, positive, w_in, b_in, w_out):
    n_data = lax.axis_size("dp")
    n_model = lax.axis_size("mp")
    n_z = n_data // 4
    me = lax.axis_index("dp")
    my_model = lax.axis_index("mp")
    n_query, width_out = queries.shape
    rows, width_emb = item_table.shape
    units = w_in.shape[1]
    part = rows // n_model
    cand_local = cand_row.shape[0]
    n_cols = n_data * part
    chunk = n_z * part // 2
    scale = 1.0 / math.sqrt(width_out)
    tie = lax.optimization_barrier
    slice_at = functools.partial(lax.dynamic_slice, allow_negative_indices=False)
    core = me & 1
    half_rows = width_emb // 2
    query_part = n_query // n_model
    starts = [(my_model ^ k) * part for k in range(n_model)]
    share_starts = [(my_model ^ k) * query_part for k in range(n_model)]
    half_starts = [(core ^ k) * half_rows for k in range(2)]
    model_index = my_model.astype(jnp.int32).reshape(1)
    core_first = core == 0

    pre = dot(item_table, w_in) + b_in[None, :]
    hidden = jnp.maximum(pre, 0.0).astype(BF16)
    partial = dot(hidden, w_out)

    def part_of(value, k):
        return slice_at(value, (starts[k], 0), (part, value.shape[1]))

    outgoing = [part_of(partial, k) for k in range(1, n_model)]
    arrived = [hop(outgoing[k - 1], k, "mp") for k in range(1, n_model)]
    outgoing, queries, cand_row = tie((outgoing, queries, cand_row))
    qt = queries.T
    packed = jnp.concatenate([w_in, w_out.reshape(width_emb, -1)], axis=1)
    piece = slice_at(packed, (half_starts[0], 0), (half_rows, packed.shape[1]))

    largest = jnp.max(jnp.abs(queries)).astype(F32)
    exponent = jnp.floor(jnp.log2(jnp.maximum(largest, 1e-6))).astype(jnp.int32) + 1
    exponent = jnp.clip(exponent + EXPONENT_BASE, 0, 63)
    word = (cand_owner[:, 0] * rows + cand_row) * COUNT_BASE + cand_count
    word = (word + exponent * (1 << WORD_BITS))[None, :]
    words = jnp.concatenate([word, hop(word, 1)], axis=0)
    words = jnp.concatenate([words, hop(words, 2)], axis=0)

    spot = (((positive // cand_local) ^ me) * cand_local + positive % cand_local)[None, :]
    both_index = jnp.stack([me, my_model]).astype(jnp.int32)
    ready = (qt, piece, spot, both_index, share_starts, half_starts, model_index, core_first)
    total, arrived, ready = tie((part_of(partial, 0), arrived, ready))
    qt, piece, spot, both_index, share_starts, half_starts, model_index, core_first = ready
    for other in arrived:
        total = total + other
    size = 4 * cand_local
    digits = jnp.stack([(words.reshape(size) >> shift) & 255 for shift in (0, 8, 16, 24)])
    tail_rows = -(-4 * size // (16 * width_out)) * 16
    digits = jnp.pad(digits.reshape(-1), (0, tail_rows * width_out - 4 * size))
    tail = digits.reshape(tail_rows, width_out).astype(BF16)
    payload = jnp.concatenate([total.astype(BF16), tail], axis=0)

    along_z = {0: payload}
    for j in range(n_z - 1, 0, -1):
        along_z[j] = hop(payload, j << 2)
    along_x = {j: hop(along_z[j], 2) for j in range(2)}
    along_z, along_x = tie((along_z, along_x))

    hidden_max = width_emb * TABLE_MAX * W_IN_MAX + B_IN_MAX
    gradient_sum = n_data * n_query * 2.0 * scale
    bounds = [
        2 * n_query * 2.0 * scale,
        4 * n_query * 2.0 * scale,
        gradient_sum * width_out * W_OUT_MAX * TABLE_MAX,
        gradient_sum * hidden_max,
    ]
    bias, pos_col, pos_logc, scales = run_prepare(
        both_index, [along_z[j] for j in range(n_z)], spot, part, rows, bounds, cand_local,
        n_cols, max(units, width_out),
    )
    factors = [scales[n : n + 1] for n in range(4)]
    growths = [scales[n + 4 : n + 5] for n in range(4)]
    own_mask = dot(item_table, packed[:, :units]) + b_in[None, :] > 0.0
    bias, own_mask = tie((bias, own_mask))

    halves = [range(h * n_z // 2, (h + 1) * n_z // 2) for h in range(2)]
    start_of = {
        (x, c, h): ((x * 2 + c) * 2 + h) * chunk for x in range(2) for c in range(2) for h in range(2)
    }
    items = {}
    m8 = jnp.full((8, n_query), ABSENT, F32)
    l8 = jnp.zeros((8, n_query), F32)

    def gathered(x, h, blocks):
        items[x, 0, h] = [blocks[j] for j in halves[h]]
        items[x, 1, h] = [hop(v, 1) for v in items[x, 0, h]]

    def statistics(m, l, *chosen):
        for key in chosen:
            m, l = run_stats(items[key], part, qt, bias, m, l, scale * LOG2E, start_of[key], False)
        return m, l

    for j in range(2, n_z):
        along_x[j] = hop(along_z[j], 2)
    gathered(0, 0, along_z)
    m8, l8 = statistics(m8, l8, (0, 0, 0), (0, 1, 0))
    along_x, m8, l8 = tie((along_x, m8, l8))
    gathered(0, 1, along_z)
    m8, l8 = statistics(m8, l8, (0, 0, 1), (0, 1, 1))
    gathered(1, 0, along_x)
    m8, l8 = statistics(m8, l8, (1, 0, 0))
    gathered(1, 1, along_x)
    m8, l8 = statistics(m8, l8, (1, 1, 0), (1, 0, 1))
    (local,) = run_stats(
        items[1, 1, 1], part, qt, bias, m8, l8, scale * LOG2E, start_of[1, 1, 1], True
    )
    lse = run_lse(model_index, [local] + [hop(local, k, "mp") for k in range(1, n_model)])

    piece, b_late, lse = tie((piece, b_in[None, :], lse))
    others = [(hop(piece, k, "mp"), hop(b_late, k, "mp")) for k in range(1, n_model)]

    qg = jnp.zeros((width_out, n_query), F32)
    sp = jnp.zeros((8, n_query), F32)
    chip_sums, crossed = {}, {}

    def gradients(key, qg, sp, more=()):
        return run_grad(
            items[key], part, more, qt, queries, bias, lse, pos_col, qg, sp,
            scale, start_of[key],
        )

    siblings, crossing = {}, {}
    for h in (1, 0):
        sums, qg, sp = gradients((1, 1, h), qg, sp)
        siblings[1, h] = [hop(v, 1) for v in sums]
    for h in (1, 0):
        chip_sums[1, h], qg, sp = gradients((1, 0, h), qg, sp, siblings[1, h])
        crossing[h], qg = tie(
            ((jnp.concatenate(chip_sums[1, h], axis=0) * factors[0][:, :width_out]).astype(F16), qg)
        )
        crossed[h] = hop(crossing[h], 2)
    for h in (1, 0):
        sums, qg, sp = gradients((0, 1, h), qg, sp)
        siblings[0, h] = [hop(v, 1) for v in sums]
    leaving = {}
    for h in (1, 0):
        crossed[h], leaving, qg = tie((crossed[h], leaving, qg))
        chip_sums[0, h], qg, sp = gradients((0, 0, h), qg, sp, siblings[0, h])
        for j in range(n_z // 2):
            over = crossed[h][j * part : (j + 1) * part].astype(F32) * growths[0][:, :width_out]
            whole = chip_sums[0, h][j] + over
            place_z = h * n_z // 2 + j
            if place_z:
                leaving[place_z] = (whole * factors[1][:, :width_out]).astype(F16)
            else:
                own_sum = whole
    sent = {j: hop(leaving[j], j << 2) for j in range(n_z - 1, 0, -1)}
    far_sum = sent[n_z - 1].astype(F32)
    for j in range(n_z - 2, 1, -1):
        far_sum = far_sum + sent[j].astype(F32)
    far_sum, sent[1] = tie((far_sum, sent[1]))
    own_sum = own_sum + (far_sum + sent[1].astype(F32)) * growths[1][:, :width_out]
    own_grad, others = tie((own_sum.astype(BF16), others))
    others = [(joined(got, hop(got, 1), core_first), b) for got, b in others]
    weights = [(packed, b_in[None, :])] + others
    if n_model > 2:
        turn = jnp.arange(n_model) ^ my_model
        stacks = [jnp.take(jnp.stack(group), turn, axis=0) for group in zip(*weights)]
        weights = [(stacks[0][k], stacks[1][k]) for k in range(n_model)]
    weights = [(w[:, :units], w[:, units:].reshape(units, width_out), b) for w, b in weights]
    masks = [dot(item_table, share_in) + b > 0.0 for share_in, _, b in weights]
    if n_model == 2:
        masks[0] = own_mask


    grads = [own_grad] + [hop(own_grad, k, "mp") for k in range(1, n_model)]
    grads, masks = tie((grads, masks))
    item_grad, pre_grad, local_b, value = run_backward(
        model_index, scales, grads, pre, hidden, item_table, w_out
    )

    width = value.shape[1]
    keep, give = (slice_at(value, (half_starts[k], 0), (half_rows, width)) for k in range(2))
    bias_steps = [1 << n for n in range(n_data.bit_length() - 1)]

    def step_bias(value, steps):
        for _ in range(min(steps, len(bias_steps))):
            bits = bias_steps.pop(0)
            value = value + hop(value, bits)
        return value

    value = (keep + hop(give.astype(F16), 1).astype(F32)).astype(F16)
    value, local_b = tie((value, step_bias(local_b, 1)))
    chips = n_data // 2
    groups = [[2 * chip + c for chip in range(chips)] for c in range(2)]

    def exchange(blocks):
        return lax.all_to_all(
            blocks, "dp", split_axis=0, concat_axis=0, axis_index_groups=groups, tiled=True
        )

    size = half_rows // chips
    pieces = exchange(value.reshape(chips, size, width))
    total = jnp.sum(pieces.astype(F32), axis=0).astype(F16)
    total, local_b, item_grad = tie((total, step_bias(local_b, 9), item_grad))
    own_half = exchange(jnp.broadcast_to(total[None], (chips, size, width)))
    own_half = own_half.reshape(half_rows, width)

    grad_table = None
    for (share_in, share_out, _), mask in zip(weights, masks):
        back = jnp.where(mask, dot(item_grad, share_out, NT), 0.0).astype(BF16)
        term = dot(back, share_in, NT)
        grad_table = term if grad_table is None else grad_table + term
    own_half, grad_table = tie((own_half, grad_table))


    local_b, qg, sp = tie((local_b, qg, sp))

    item_max = n_model * units * hidden_max * W_OUT_MAX
    q_factor = LIMIT / (2.0 * item_max)
    sp1 = jnp.sum(sp, axis=0)[None, :]
    qg_parts = [
        slice_at(qg, (0, share_starts[k]), (width_out, query_part))
        for k in range(n_model)
    ]
    pos_score, query_sum = sp1, qg_parts[0]
    for k in range(1, n_model):
        sent = hop((qg_parts[k] * q_factor).astype(F16), k, "mp")
        query_sum = query_sum + sent.astype(F32) * (1.0 / q_factor)
        pos_score = pos_score + hop(sp1, k, "mp")
    loss = lse[0] * (1.0 / LOG2E) - (pos_score[0] * scale - pos_logc[0])
    query_grad = (query_sum * scale).T

    sides = [own_half, hop(own_half, 1)]
    sides_in = [v[:, :units].astype(F32) * growths[2][:, :units] for v in sides]
    tail_width = width - units
    sides_out = [v[:, units:].astype(F32) * growths[3][:, :tail_width] for v in sides]
    grad_w_in = joined(*sides_in, core_first)
    grad_w_out = joined(*sides_out, core_first).reshape(units, width_out)
    return (loss, query_grad, grad_w_in, local_b[0], grad_w_out, grad_table)


def solution(mesh):
    placed = (
        P("dp", None),
        P("dp", None),
        P("dp"),
        P("dp", None),
        P("dp"),
        P("dp"),
        P(None, "mp"),
        P("mp"),
        P("mp", None),
    )
    return jax.shard_map(
        per_device,
        mesh=mesh,
        in_specs=placed,
        out_specs=(
            P("dp"),
            P(("dp", "mp"), None),
            P(None, "mp"),
            P("mp"),
            P("mp", None),
            P("dp", None),
        ),
        check_vma=False,
    )
```

```python
import functools
import math

import jax
import jax.numpy as jnp
from jax import lax
from jax.experimental import pallas as pl
from jax.experimental.pallas import tpu as pltpu
from jax.sharding import PartitionSpec as P

F32 = jnp.float32
BF16 = jnp.bfloat16
F16 = jnp.float16
ABSENT = -1e30
COUNT_BASE = 128
WORD_BITS = 22
EXPONENT_BASE = 20
TABLE_MAX = 6.0
W_IN_MAX = 0.25
B_IN_MAX = 3.0
W_OUT_MAX = 0.1875
LIMIT = 32768.0
LOG2E = math.log2(math.e)
GROUP = 16
NT = (((1,), (1,)), ((), ()))
TN = (((0,), (0,)), ((), ()))


def hop(value, bits, axis="dp"):
    size = lax.axis_size(axis)
    return lax.ppermute(value, axis, [(i, i ^ bits) for i in range(size)])


def dot(a, b, dims=None, **kw):
    if dims is None:
        dims = (((1,), (0,)), ((), ()))
    return lax.dot_general(a, b, dims, preferred_element_type=F32, **kw)


def column_bias(bias_ref, first, count):
    lane = first // 128
    return bias_ref[pl.ds(first % 128, count), lane : lane + 1]


def stats_kernel(scale, base, count, last, *refs):
    items_refs, refs = refs[:count], refs[count:]
    qt_ref, bias_ref, m_in_ref, l_in_ref, m_ref, *score_refs = refs
    l_ref = None if last else score_refs.pop(0)
    block = score_refs[0].shape[0]
    old = m_in_ref[...]
    new = old
    for items_ref, score_ref in zip(items_refs, score_refs):
        score_ref[...] = dot(items_ref[0:block], qt_ref[...])
    for n, score_ref in enumerate(score_refs):
        for r in range(0, block, 8):
            bias = column_bias(bias_ref, base + n * block + r, 8)
            score = score_ref[r : r + 8] * scale + bias
            score_ref[r : r + 8] = score
            new = jnp.maximum(new, score)
    total = l_in_ref[...] * jnp.exp2(old - new)
    for score_ref in score_refs:
        for r in range(0, block, 8):
            total = total + jnp.exp2(score_ref[r : r + 8] - new)
    if last:
        top = jnp.max(new, axis=0, keepdims=True)
        m_ref[0:1] = top
        m_ref[1:2] = jnp.sum(total * jnp.exp2(new - top), axis=0, keepdims=True)
    else:
        m_ref[...] = new
        l_ref[...] = total


def in_vmem(count):
    return [pl.BlockSpec(memory_space=pltpu.VMEM)] * count


def run_stats(items, block, qt, bias, m, l, scale, base, last):
    count, nq = len(items), qt.shape[1]
    shapes = [(2, nq)] if last else [(8, nq)] * 2
    return pl.pallas_call(
        functools.partial(stats_kernel, scale, base, count, last),
        in_specs=in_vmem(count + 4),
        out_specs=in_vmem(len(shapes)),
        out_shape=[jax.ShapeDtypeStruct(shape, F32) for shape in shapes],
        scratch_shapes=[pltpu.VMEM((block, nq), F32)] * count,
        compiler_params=pltpu.CompilerParams(vmem_limit_bytes=6 << 20),
    )(*items, qt, bias, m, l)


def lse_kernel(count, index_ref, *refs):
    part_refs, (lse_ref, held_ref) = refs[:count], refs[count:]
    for k in range(count):
        held_ref[index_ref[0] ^ k] = part_refs[k][...]
    parts = [held_ref[k] for k in range(count)]
    top = functools.reduce(jnp.maximum, [p[0:1] for p in parts])
    total = functools.reduce(jnp.add, [p[1:2] * jnp.exp2(p[0:1] - top) for p in parts])
    lse_ref[...] = top + jnp.log2(total)


def run_lse(index, parts):
    nq = parts[0].shape[1]
    return pl.pallas_call(
        functools.partial(lse_kernel, len(parts)),
        in_specs=[pl.BlockSpec(memory_space=pltpu.SMEM)] + in_vmem(len(parts)),
        out_specs=in_vmem(1)[0],
        out_shape=jax.ShapeDtypeStruct((1, nq), F32),
        scratch_shapes=[pltpu.VMEM((len(parts), 2, nq), F32)],
        compiler_params=pltpu.CompilerParams(vmem_limit_bytes=2 << 20),
    )(index, *parts)


def grad_kernel(scale, base, count, add, *refs):
    items_refs, refs = refs[:count], refs[count:]
    more_refs, refs = refs[:add], refs[add:]
    qt_ref, q_ref, bias_ref, lse_ref, pos_ref, qg_in_ref, sp_in_ref, *refs = refs
    sums_refs, (qg_ref, sp_ref, *scratch) = refs[:count], refs[count:]
    score_refs, prob_refs = scratch[:count], scratch[count:]
    block, queries = score_refs[0].shape
    for items_ref, score_ref in zip(items_refs, score_refs):
        score_ref[...] = dot(items_ref[0:block], qt_ref[...])
    down = lax.broadcasted_iota(jnp.int32, (8, queries), 0)
    offset = jnp.broadcast_to(pos_ref[...], (8, queries)) - down
    lse = jnp.broadcast_to(lse_ref[...], (8, queries))
    found = sp_in_ref[...]
    for n in range(count):
        score_ref, prob_ref = score_refs[n], prob_refs[n]
        for r in range(0, block, GROUP):
            pieces = []
            for s in range(r, r + GROUP, 8):
                at = base + n * block + s
                score = score_ref[s : s + 8]
                here = offset == at
                found = found + jnp.where(here, score, 0.0)
                prob = jnp.exp2((score * (scale * LOG2E) + column_bias(bias_ref, at, 8)) - lse)
                pieces.append(jnp.where(here, prob - 1.0, prob))
            prob_ref[r : r + GROUP] = jnp.concatenate(pieces, axis=0).astype(BF16)
        sums = dot(prob_ref[...], q_ref[...]) * scale
        sums_refs[n][...] = sums + more_refs[n][...] if add else sums
        share = dot(items_refs[n][0:block], prob_ref[...], TN)
        qg_ref[...] = (qg_in_ref[...] if n == 0 else qg_ref[...]) + share
    sp_ref[...] = found


def run_grad(items, block, more, qt, q, bias, lse, pos, qg, sp, scale, base):
    count, (width, nq) = len(items), qt.shape
    before = count + len(more)
    *sums, qg, sp = pl.pallas_call(
        functools.partial(grad_kernel, scale, base, count, len(more)),
        in_specs=in_vmem(before + 7),
        out_specs=in_vmem(count + 2),
        out_shape=[jax.ShapeDtypeStruct((block, width), F32)] * count
        + [jax.ShapeDtypeStruct((width, nq), F32), jax.ShapeDtypeStruct((8, nq), F32)],
        scratch_shapes=[pltpu.VMEM((block, nq), F32)] * count
        + [pltpu.VMEM((block, nq), BF16)] * count,
        input_output_aliases={before + 5: count, before + 6: count + 1},
        compiler_params=pltpu.CompilerParams(vmem_limit_bytes=8 << 20),
    )(*items, *more, qt, q, bias, lse, pos, qg, sp)
    return sums, qg, sp


def backward_kernel(count, index_ref, scale_ref, *refs):
    grad_refs, (pre_ref, hidden_ref, emb_ref, w_out_ref) = refs[:count], refs[count : count + 4]
    grad_ref, pre_grad_ref, b_ref, *sums_refs = refs[count + 4 :]
    part = grad_refs[0].shape[0]
    for k in range(count):
        start = pl.multiple_of((index_ref[0] ^ k) * part, part)
        grad_ref[pl.ds(start, part)] = grad_refs[k][...]
    back = dot(grad_ref[...], w_out_ref[...], NT)
    pre_grad = jnp.where(pre_ref[...] > 0.0, back, 0.0).astype(BF16)
    pre_grad_ref[...] = pre_grad
    b_ref[...] = jnp.sum(pre_grad.astype(F32), axis=0, keepdims=True)
    sums_in = dot(emb_ref[...], pre_grad, TN) * scale_ref[2:3, : pre_grad.shape[1]]
    sums_out = dot(hidden_ref[...], grad_ref[...], TN) * scale_ref[3:4, : grad_ref.shape[1]]
    if len(sums_refs) == 1:
        units = sums_in.shape[1]
        sums_refs[0][:, :units] = sums_in
        sums_refs[0][:, units:] = sums_out
    else:
        sums_refs[0][...] = sums_in
        sums_refs[1][...] = sums_out


def run_backward(index, scales, grads, pre, hidden, emb, w_out):
    rows, units = pre.shape
    width_emb, width_out = emb.shape[1], w_out.shape[1]
    if units == width_emb:
        sums = [(width_emb, units + width_out)]
    else:
        sums = [(width_emb, units), (units, width_out)]
    grad, pre_grad, local_b, *sums = pl.pallas_call(
        functools.partial(backward_kernel, len(grads)),
        in_specs=[pl.BlockSpec(memory_space=pltpu.SMEM)] + in_vmem(len(grads) + 5),
        out_specs=in_vmem(3 + len(sums)),
        out_shape=[
            jax.ShapeDtypeStruct((rows, width_out), BF16),
            jax.ShapeDtypeStruct((rows, units), BF16),
            jax.ShapeDtypeStruct((1, units), F32),
        ]
        + [jax.ShapeDtypeStruct(shape, F32) for shape in sums],
        compiler_params=pltpu.CompilerParams(vmem_limit_bytes=12 << 20),
    )(index, scales, *grads, pre, hidden, emb, w_out)
    if len(sums) > 1:
        sums = [jnp.concatenate([sums[0], sums[1].reshape(width_emb, -1)], axis=1)]
    return grad, pre_grad, local_b, sums[0]


def prepare_kernel(part, rows, bounds, count, index_ref, *refs):
    block_refs, refs = refs[:count], refs[count:]
    spot_ref, bias_ref, pos_ref, logc_ref, scale_ref, tail_ref, words_ref, col_ref, share_ref = refs
    lines, width = words_ref.shape
    run = lines // count
    lanes = 128
    for z in range(count):
        tail_ref[...] = block_refs[z][part : part + tail_ref.shape[0]].astype(F32)
        for r in range(run):
            value = tail_ref[r : r + 1].astype(jnp.int32)
            for digit in range(1, 4):
                at = digit * run + r
                value += tail_ref[at : at + 1].astype(jnp.int32) << (8 * digit)
            words_ref[z * run + r : z * run + r + 1] = value
    words = words_ref[...]
    exponent = jnp.max(words >> WORD_BITS, axis=1, keepdims=True)
    exponent = jnp.max(exponent, axis=0, keepdims=True) - EXPONENT_BASE
    largest = jnp.exp2(jnp.broadcast_to(exponent.astype(F32), (1, scale_ref.shape[1])))
    for n, bound in enumerate(bounds):
        scale_ref[n : n + 1] = (LIMIT / bound) / largest
        scale_ref[n + len(bounds) : n + len(bounds) + 1] = largest * (bound / LIMIT)

    count_bits, row_bits, part_bits = (n.bit_length() - 1 for n in (COUNT_BASE, rows, part))

    def decoded(word):
        row = (word >> count_bits) & (rows - 1)
        rel = (word >> (count_bits + row_bits)) ^ index_ref[0]
        place = ((rel >> 1) & 1) * (2 * count) + (rel & 1) * count + (rel >> 2)
        column = place * part + (row & (part - 1))
        named = (word & (COUNT_BASE - 1)).astype(F32)
        return jnp.where((row >> part_bits) == index_ref[1], column, -1), named

    words = words & ((1 << WORD_BITS) - 1)
    column, named = decoded(words)
    col_ref[...] = column
    share_ref[...] = 1.0 / named
    blocks = bias_ref.shape[1]
    weight = jnp.zeros((lanes, blocks), F32)
    block_iota = lax.broadcasted_iota(jnp.int32, (blocks, width), 0)
    lane_iota = lax.broadcasted_iota(jnp.int32, (lanes, width), 0)
    for n in range(lines):
        column = col_ref[n : n + 1]
        high = jnp.where(block_iota == (column >> 7), 1.0, 0.0)
        low = jnp.where(lane_iota == (column & (lanes - 1)), share_ref[n : n + 1], 0.0)
        weight += dot(low, high, NT, precision=lax.Precision.HIGHEST)
    bias_ref[...] = jnp.where(weight > 0.0, jnp.log2(weight), ABSENT)

    spot = spot_ref[...]
    queries = spot.shape[1]
    line_iota = lax.broadcasted_iota(jnp.int32, (lines, queries), 0)
    picked = jnp.where(line_iota == spot // width, 1.0, 0.0).astype(BF16)
    found = jnp.zeros((width, queries), F32)
    for digit in range(3):
        part_of_word = ((words >> (8 * digit)) & 255).astype(F32).astype(BF16)
        found += dot(part_of_word, picked, TN) * float(256**digit)
    mine = lax.broadcasted_iota(jnp.int32, (width, queries), 0) == spot % width
    word = jnp.sum(jnp.where(mine, found, 0.0), axis=0, keepdims=True).astype(jnp.int32)
    pos, named = decoded(word)
    pos_ref[...] = pos
    logc_ref[...] = jnp.log(named)


def run_prepare(index, blocks, spot, part, rows, bounds, cand_local, n_cols, width):
    count, (height, across), nq = len(blocks), blocks[0].shape, spot.shape[1]
    lines = count * 4 * cand_local // across
    return pl.pallas_call(
        functools.partial(prepare_kernel, part, rows, bounds, count),
        in_specs=[pl.BlockSpec(memory_space=pltpu.SMEM)] + in_vmem(count + 1),
        out_specs=in_vmem(4),
        out_shape=[
            jax.ShapeDtypeStruct((128, n_cols // 128), F32),
            jax.ShapeDtypeStruct((1, nq), jnp.int32),
            jax.ShapeDtypeStruct((1, nq), F32),
            jax.ShapeDtypeStruct((2 * len(bounds), width), F32),
        ],
        scratch_shapes=[
            pltpu.VMEM((height - part, across), F32),
            pltpu.VMEM((lines, across), jnp.int32),
            pltpu.VMEM((lines, across), jnp.int32),
            pltpu.VMEM((lines, across), F32),
        ],
        compiler_params=pltpu.CompilerParams(vmem_limit_bytes=8 << 20),
    )(index, *blocks, spot)


def joined(mine, other, first):
    return jnp.where(
        first,
        jnp.concatenate([mine, other], axis=0),
        jnp.concatenate([other, mine], axis=0),
    )


def per_device(queries, item_table, cand_row, cand_owner, cand_count, positive, w_in, b_in, w_out):
    n_data = lax.axis_size("dp")
    n_model = lax.axis_size("mp")
    n_z = n_data // 4
    me = lax.axis_index("dp")
    my_model = lax.axis_index("mp")
    n_query, width_out = queries.shape
    rows, width_emb = item_table.shape
    units = w_in.shape[1]
    part = rows // n_model
    cand_local = cand_row.shape[0]
    n_cols = n_data * part
    chunk = n_z * part // 2
    scale = 1.0 / math.sqrt(width_out)
    tie = lax.optimization_barrier
    slice_at = functools.partial(lax.dynamic_slice, allow_negative_indices=False)
    core = me & 1
    half_rows = width_emb // 2
    query_part = n_query // n_model
    starts = [(my_model ^ k) * part for k in range(n_model)]
    share_starts = [(my_model ^ k) * query_part for k in range(n_model)]
    half_starts = [(core ^ k) * half_rows for k in range(2)]
    model_index = my_model.astype(jnp.int32).reshape(1)
    core_first = core == 0

    pre = dot(item_table, w_in) + b_in[None, :]
    hidden = jnp.maximum(pre, 0.0).astype(BF16)
    partial = dot(hidden, w_out)

    def part_of(value, k):
        return slice_at(value, (starts[k], 0), (part, value.shape[1]))

    outgoing = [part_of(partial, k) for k in range(1, n_model)]
    arrived = [hop(outgoing[k - 1], k, "mp") for k in range(1, n_model)]
    outgoing, queries, cand_row = tie((outgoing, queries, cand_row))
    qt = queries.T
    packed = jnp.concatenate([w_in, w_out.reshape(width_emb, -1)], axis=1)
    piece = slice_at(packed, (half_starts[0], 0), (half_rows, packed.shape[1]))

    largest = jnp.max(jnp.abs(queries)).astype(F32)
    exponent = jnp.floor(jnp.log2(jnp.maximum(largest, 1e-6))).astype(jnp.int32) + 1
    exponent = jnp.clip(exponent + EXPONENT_BASE, 0, 63)
    word = (cand_owner[:, 0] * rows + cand_row) * COUNT_BASE + cand_count
    word = (word + exponent * (1 << WORD_BITS))[None, :]
    words = jnp.concatenate([word, hop(word, 1)], axis=0)
    words = jnp.concatenate([words, hop(words, 2)], axis=0)

    spot = (((positive // cand_local) ^ me) * cand_local + positive % cand_local)[None, :]
    both_index = jnp.stack([me, my_model]).astype(jnp.int32)
    ready = (qt, piece, spot, both_index, share_starts, half_starts, model_index, core_first)
    total, arrived, ready = tie((part_of(partial, 0), arrived, ready))
    qt, piece, spot, both_index, share_starts, half_starts, model_index, core_first = ready
    for other in arrived:
        total = total + other
    size = 4 * cand_local
    digits = jnp.stack([(words.reshape(size) >> shift) & 255 for shift in (0, 8, 16, 24)])
    tail_rows = -(-4 * size // (16 * width_out)) * 16
    digits = jnp.pad(digits.reshape(-1), (0, tail_rows * width_out - 4 * size))
    tail = digits.reshape(tail_rows, width_out).astype(BF16)
    payload = jnp.concatenate([total.astype(BF16), tail], axis=0)

    along_z = {0: payload}
    for j in range(n_z - 1, 0, -1):
        along_z[j] = hop(payload, j << 2)
    along_x = {j: hop(along_z[j], 2) for j in range(2)}
    along_z, along_x = tie((along_z, along_x))

    hidden_max = width_emb * TABLE_MAX * W_IN_MAX + B_IN_MAX
    gradient_sum = n_data * n_query * 2.0 * scale
    bounds = [
        2 * n_query * 2.0 * scale,
        4 * n_query * 2.0 * scale,
        gradient_sum * width_out * W_OUT_MAX * TABLE_MAX,
        gradient_sum * hidden_max,
    ]
    bias, pos_col, pos_logc, scales = run_prepare(
        both_index, [along_z[j] for j in range(n_z)], spot, part, rows, bounds, cand_local,
        n_cols, max(units, width_out),
    )
    factors = [scales[n : n + 1] for n in range(4)]
    growths = [scales[n + 4 : n + 5] for n in range(4)]
    own_mask = dot(item_table, packed[:, :units]) + b_in[None, :] > 0.0
    bias, own_mask = tie((bias, own_mask))

    halves = [range(h * n_z // 2, (h + 1) * n_z // 2) for h in range(2)]
    start_of = {
        (x, c, h): ((x * 2 + c) * 2 + h) * chunk for x in range(2) for c in range(2) for h in range(2)
    }
    items = {}
    m8 = jnp.full((8, n_query), ABSENT, F32)
    l8 = jnp.zeros((8, n_query), F32)

    def gathered(x, h, blocks):
        items[x, 0, h] = [blocks[j] for j in halves[h]]
        items[x, 1, h] = [hop(v, 1) for v in items[x, 0, h]]

    def statistics(m, l, *chosen):
        for key in chosen:
            m, l = run_stats(items[key], part, qt, bias, m, l, scale * LOG2E, start_of[key], False)
        return m, l

    for j in range(2, n_z):
        along_x[j] = hop(along_z[j], 2)
    gathered(0, 0, along_z)
    m8, l8 = statistics(m8, l8, (0, 0, 0), (0, 1, 0))
    along_x, m8, l8 = tie((along_x, m8, l8))
    gathered(0, 1, along_z)
    m8, l8 = statistics(m8, l8, (0, 0, 1), (0, 1, 1))
    gathered(1, 0, along_x)
    m8, l8 = statistics(m8, l8, (1, 0, 0))
    gathered(1, 1, along_x)
    m8, l8 = statistics(m8, l8, (1, 1, 0), (1, 0, 1))
    (local,) = run_stats(
        items[1, 1, 1], part, qt, bias, m8, l8, scale * LOG2E, start_of[1, 1, 1], True
    )
    lse = run_lse(model_index, [local] + [hop(local, k, "mp") for k in range(1, n_model)])

    piece, b_late, lse = tie((piece, b_in[None, :], lse))
    others = [(hop(piece, k, "mp"), hop(b_late, k, "mp")) for k in range(1, n_model)]

    qg = jnp.zeros((width_out, n_query), F32)
    sp = jnp.zeros((8, n_query), F32)
    chip_sums, crossed = {}, {}

    def gradients(key, qg, sp, more=()):
        return run_grad(
            items[key], part, more, qt, queries, bias, lse, pos_col, qg, sp,
            scale, start_of[key],
        )

    siblings, crossing = {}, {}
    for h in (1, 0):
        sums, qg, sp = gradients((1, 1, h), qg, sp)
        siblings[1, h] = [hop(v, 1) for v in sums]
    for h in (1, 0):
        chip_sums[1, h], qg, sp = gradients((1, 0, h), qg, sp, siblings[1, h])
        crossing[h], qg = tie(
            ((jnp.concatenate(chip_sums[1, h], axis=0) * factors[0][:, :width_out]).astype(F16), qg)
        )
        crossed[h] = hop(crossing[h], 2)
    for h in (1, 0):
        sums, qg, sp = gradients((0, 1, h), qg, sp)
        siblings[0, h] = [hop(v, 1) for v in sums]
    leaving = {}
    for h in (1, 0):
        crossed[h], leaving, qg = tie((crossed[h], leaving, qg))
        chip_sums[0, h], qg, sp = gradients((0, 0, h), qg, sp, siblings[0, h])
        for j in range(n_z // 2):
            over = crossed[h][j * part : (j + 1) * part].astype(F32) * growths[0][:, :width_out]
            whole = chip_sums[0, h][j] + over
            place_z = h * n_z // 2 + j
            if place_z:
                leaving[place_z] = (whole * factors[1][:, :width_out]).astype(F16)
            else:
                own_sum = whole
    sent = {j: hop(leaving[j], j << 2) for j in range(n_z - 1, 0, -1)}
    far_sum = sent[n_z - 1].astype(F32)
    for j in range(n_z - 2, 1, -1):
        far_sum = far_sum + sent[j].astype(F32)
    far_sum, sent[1] = tie((far_sum, sent[1]))
    own_sum = own_sum + (far_sum + sent[1].astype(F32)) * growths[1][:, :width_out]
    own_grad, others = tie((own_sum.astype(BF16), others))
    others = [(joined(got, hop(got, 1), core_first), b) for got, b in others]
    weights = [(packed, b_in[None, :])] + others
    if n_model > 2:
        turn = jnp.arange(n_model) ^ my_model
        stacks = [jnp.take(jnp.stack(group), turn, axis=0) for group in zip(*weights)]
        weights = [(stacks[0][k], stacks[1][k]) for k in range(n_model)]
    weights = [(w[:, :units], w[:, units:].reshape(units, width_out), b) for w, b in weights]
    masks = [dot(item_table, share_in) + b > 0.0 for share_in, _, b in weights]
    if n_model == 2:
        masks[0] = own_mask


    grads = [own_grad] + [hop(own_grad, k, "mp") for k in range(1, n_model)]
    grads, masks = tie((grads, masks))
    item_grad, pre_grad, local_b, value = run_backward(
        model_index, scales, grads, pre, hidden, item_table, w_out
    )

    width = value.shape[1]
    keep, give = (slice_at(value, (half_starts[k], 0), (half_rows, width)) for k in range(2))
    bias_steps = [1 << n for n in range(n_data.bit_length() - 1)]

    def step_bias(value, steps):
        for _ in range(min(steps, len(bias_steps))):
            bits = bias_steps.pop(0)
            value = value + hop(value, bits)
        return value

    value = (keep + hop(give.astype(F16), 1).astype(F32)).astype(F16)
    value, local_b = tie((value, step_bias(local_b, 1)))
    chips = n_data // 2
    groups = [[2 * chip + c for chip in range(chips)] for c in range(2)]

    def exchange(blocks):
        return lax.all_to_all(
            blocks, "dp", split_axis=0, concat_axis=0, axis_index_groups=groups, tiled=True
        )

    size = half_rows // chips
    pieces = exchange(value.reshape(chips, size, width))
    total = jnp.sum(pieces.astype(F32), axis=0).astype(F16)
    total, local_b, item_grad = tie((total, step_bias(local_b, 9), item_grad))
    own_half = exchange(jnp.broadcast_to(total[None], (chips, size, width)))
    own_half = own_half.reshape(half_rows, width)

    grad_table = None
    for (share_in, share_out, _), mask in zip(weights, masks):
        back = jnp.where(mask, dot(item_grad, share_out, NT), 0.0).astype(BF16)
        term = dot(back, share_in, NT)
        grad_table = term if grad_table is None else grad_table + term


    local_b, qg, sp = tie((local_b, qg, sp))

    item_max = n_model * units * hidden_max * W_OUT_MAX
    q_factor = LIMIT / (2.0 * item_max)
    sp1 = jnp.sum(sp, axis=0)[None, :]
    qg_parts = [
        slice_at(qg, (0, share_starts[k]), (width_out, query_part))
        for k in range(n_model)
    ]
    pos_score, query_sum = sp1, qg_parts[0]
    for k in range(1, n_model):
        sent = hop((qg_parts[k] * q_factor).astype(F16), k, "mp")
        query_sum = query_sum + sent.astype(F32) * (1.0 / q_factor)
        pos_score = pos_score + hop(sp1, k, "mp")
    loss = lse[0] * (1.0 / LOG2E) - (pos_score[0] * scale - pos_logc[0])
    query_grad = (query_sum * scale).T
    own_half, grad_table, query_grad, loss = tie((own_half, grad_table, query_grad, loss))

    sides = [own_half, hop(own_half, 1)]
    sides_in = [v[:, :units].astype(F32) * growths[2][:, :units] for v in sides]
    tail_width = width - units
    sides_out = [v[:, units:].astype(F32) * growths[3][:, :tail_width] for v in sides]
    grad_w_in = joined(*sides_in, core_first)
    grad_w_out = joined(*sides_out, core_first).reshape(units, width_out)
    return (loss, query_grad, grad_w_in, local_b[0], grad_w_out, grad_table)


def solution(mesh):
    placed = (
        P("dp", None),
        P("dp", None),
        P("dp"),
        P("dp", None),
        P("dp"),
        P("dp"),
        P(None, "mp"),
        P("mp"),
        P("mp", None),
    )
    return jax.shard_map(
        per_device,
        mesh=mesh,
        in_specs=placed,
        out_specs=(
            P("dp"),
            P(("dp", "mp"), None),
            P(None, "mp"),
            P("mp"),
            P("mp", None),
            P("dp", None),
        ),
        check_vma=False,
    )
```
